32 devices in a mesh: dp: 16 (over z, x, core), tensor: 2 (over y).
Axes of the slice: x: 2, y: 2, z: 4, core: 2. Of those that a mesh axis runs over, the one named last changes fastest.
Arguments:
- tokens: bfloat16 [8192, 768], P('dp'), may hold values from -6 to 6
- w_qkv: bfloat16 [2, 768, 3, 768], P(None, None, None, 'tensor'), may hold values from -0.21875 to 0.21875
- w_out: bfloat16 [2, 768, 768], P(None, 'tensor'), may hold values from -0.875 to 0.875
- w_up: bfloat16 [2, 768, 3072], P(None, None, 'tensor'), may hold values from -0.21875 to 0.21875
- w_down: bfloat16 [2, 3072, 768], P(None, 'tensor'), may hold values from -0.109375 to 0.109375
- norm_gain: float32 [2, 2, 768], replicated, may hold values from 0.5 to 1.5
- norm_shift: float32 [2, 2, 768], replicated, may hold values from -1.5 to 1.5
- d_out: bfloat16 [8192, 768], P('dp'), may hold values from -6 to 6
Outputs:
- out_one: bfloat16 [8192, 768], P('dp')
- out_two: bfloat16 [8192, 768], P('dp')
- input_grad: float32 [8192, 768], P('dp')
- grad_qkv: float32 [2, 768, 3, 768], P(None, None, None, 'tensor')
- grad_out: float32 [2, 768, 768], P(None, 'tensor')
- grad_up: float32 [2, 768, 3072], P(None, None, 'tensor')
- grad_down: float32 [2, 3072, 768], P(None, 'tensor')
- grad_gain: float32 [2, 2, 768], replicated
- grad_shift: float32 [2, 2, 768], replicated
The draws below stay inside these ranges and needn't reach their ends.
All inputs are finite; a program needn't handle non-finite values.
Results may differ from the reference program's by a relative error of at most 0.028.
Values may be sent and summed in bfloat16 or wider, within the bound.
No kernel may reach another device: no remote copies, remote signals or barrier semaphores. Data moves between devices by JAX's collectives and lax.ppermute only.
A program may use at most 192 MiB of HBM per device.

```python
import math
import jax
import jax.numpy as jnp
from jax import lax

D = 768
FF = 3072
HEAD_DIM = 64
LAYERS = 2
L = 512
TOKENS = 8192
N_DP = 16
N_TENSOR = 2


def block_scale(stream_key, dims, pieces, least, high):
    def one(position, parts):
        heights = jax.random.uniform(jax.random.fold_in(jax.random.fold_in(stream_key, 6), position), (parts,), jnp.float32, least / len(pieces), high / len(pieces))
        return jnp.repeat(jnp.exp(heights), dims[position] // parts).reshape((-1,) + (1,) * (len(dims) - position - 1))

    level = one(*pieces[0])
    for cut in pieces[1:]:
        level = level * one(*cut)
    return level


def bell_draw(key, dims, deviation, reach, pieces=(), kind=jnp.bfloat16):
    result = deviation * jax.random.normal(key, dims, jnp.float32)
    if pieces:
        result = result * block_scale(key, dims, pieces, -0.22, 0.18)
    return jnp.clip(result, -reach, reach).astype(kind)


def setup_inputs(seed: int = 0) -> dict:
    arg_keys = jax.random.split(jax.random.key(seed), 9)
    tokens = bell_draw(arg_keys[0], (TOKENS, D), 1.0, 6.0, ((0, 16),))
    w_qkv = bell_draw(arg_keys[1], (LAYERS, D, 3, D), D ** -0.5, 0.21875, ((3, 2),))
    w_out = bell_draw(arg_keys[2], (LAYERS, D, D), (D // 16) ** -0.5, 0.875, ((1, 2),))
    w_up = bell_draw(arg_keys[3], (LAYERS, D, FF), D ** -0.5, 0.21875, ((2, 2),))
    w_down = bell_draw(arg_keys[4], (LAYERS, FF, D), FF ** -0.5, 0.109375, ((1, 2),))
    norm_gain = jnp.clip(1.0 + 0.1 * jax.random.normal(arg_keys[5], (LAYERS, 2, D), jnp.float32), 0.5, 1.5)
    norm_shift = bell_draw(arg_keys[6], (LAYERS, 2, D), 0.3, 1.5, (), jnp.float32)
    d_out = bell_draw(arg_keys[7], (TOKENS, D), 1.0, 6.0, ((0, 16),))
    return dict(tokens=tokens, w_qkv=w_qkv, w_out=w_out, w_up=w_up, w_down=w_down, norm_gain=norm_gain, norm_shift=norm_shift, d_out=d_out)


@jax.custom_vjp
def low(v):
    return lax.optimization_barrier(v.astype(jnp.bfloat16)).astype(jnp.float32)

@jax.custom_vjp
def low_back(v):
    return v

def low_keep(v):
    return (low(v), None)

def low_pass(kept, grad):
    return (grad,)

def back_keep(v):
    return (v, None)

def back_low(kept, grad):
    return (low(grad),)
low.defvjp(low_keep, low_pass)
low_back.defvjp(back_keep, back_low)
SOFTNESS = 0.25
EPSILON = 1e-05
PRECISE = lax.Precision.HIGHEST

def round_both(values_in):
    return low(low_back(values_in))

def norm_rows(rows_in, gain, shift):
    row_mean = lax.optimization_barrier(jnp.mean(rows_in, axis=-1, keepdims=True))
    centered = rows_in - row_mean
    spread = lax.optimization_barrier(jnp.mean(centered * centered, axis=-1, keepdims=True))
    return centered * lax.rsqrt(spread + EPSILON) * gain + shift

def attend(queries, keys_all, values_in, signed):
    seq_count, length, head_count, head_size = queries.shape
    block_len = min(512, length)
    num_blocks = length // block_len
    query_blocks = jnp.moveaxis(queries.reshape(seq_count, num_blocks, block_len, head_count, head_size), 1, 0)
    block_starts = jnp.arange(num_blocks, dtype=jnp.int32) * block_len

    def one_block(element):
        query_block, block_start = element
        raw = jnp.einsum('bqhd,bkhd->bhqk', query_block, keys_all, precision=PRECISE)
        scores = low_back(raw * head_size ** (-0.5))
        row_ids = block_start + jnp.arange(block_len, dtype=jnp.int32)
        col_ids = jnp.arange(length, dtype=jnp.int32)
        allowed = col_ids[None, :] <= row_ids[:, None]
        if signed:
            magnitude = jnp.sqrt(scores * scores + SOFTNESS * SOFTNESS)
        else:
            magnitude = scores
        masked = jnp.where(allowed, magnitude, -1e+30)
        peak = lax.optimization_barrier(jnp.max(masked, axis=-1, keepdims=True))
        exponent = jnp.where(allowed, jnp.exp(masked - peak), 0.0)
        softmax_part = exponent / lax.optimization_barrier(jnp.sum(exponent, axis=-1, keepdims=True))
        if signed:
            weights = softmax_part * (scores / magnitude)
        else:
            weights = softmax_part
        return jnp.einsum('bhqk,bkhd->bqhd', low(weights), values_in, precision=PRECISE)
    attended = lax.map(jax.checkpoint(one_block), (query_blocks, block_starts))
    return jnp.moveaxis(attended, 0, 1).reshape(queries.shape)

def layer(rows_in, w_qkv, w_out, w_up, w_down, gain, shift, signed):
    seq_count, length, model_width = rows_in.shape
    width_part = model_width // N_TENSOR
    ff_part = w_up.shape[1] // N_TENSOR
    head_part = width_part // HEAD_DIM
    normed_one = low(norm_rows(rows_in, gain[0], shift[0]))
    branch = jnp.zeros_like(rows_in)
    for tensor_part in range(N_TENSOR):
        offset = tensor_part * width_part
        projected = jnp.einsum('bld,dcf->blcf', low_back(normed_one), w_qkv[:, :, offset:offset + width_part], precision=PRECISE)
        projected = round_both(projected)
        head_shape = (seq_count, length, head_part, HEAD_DIM)
        attended = attend(projected[:, :, 0].reshape(head_shape), projected[:, :, 1].reshape(head_shape), projected[:, :, 2].reshape(head_shape), signed)
        attended = round_both(attended.reshape(seq_count, length, width_part))
        branch = branch + jnp.einsum('blf,fd->bld', attended, w_out[offset:offset + width_part], precision=PRECISE)
    middle = rows_in + low_back(branch)
    normed_two = low(norm_rows(middle, gain[1], shift[1]))
    mixed = jnp.zeros_like(rows_in)
    for tensor_part in range(N_TENSOR):
        offset = tensor_part * ff_part
        pre_act = low_back(jnp.einsum('bld,df->blf', low_back(normed_two), w_up[:, offset:offset + ff_part], precision=PRECISE))
        hidden = low(jax.nn.gelu(pre_act, approximate=True))
        mixed = mixed + jnp.einsum('blf,fd->bld', hidden, w_down[offset:offset + ff_part], precision=PRECISE)
    return middle + low_back(mixed)

def forward(params, rows_in):
    w_qkv, w_out, w_up, w_down, gains, shifts = params
    first_out = layer(rows_in, w_qkv[0], w_out[0], w_up[0], w_down[0], gains[0], shifts[0], True)
    second_out = layer(first_out, w_qkv[1], w_out[1], w_up[1], w_down[1], gains[1], shifts[1], False)
    return (first_out, second_out)

def reference(tokens, w_qkv, w_out, w_up, w_down, norm_gain, norm_shift, d_out):
    params = tuple((member.astype(jnp.float32) for member in (w_qkv, w_out, w_up, w_down, norm_gain, norm_shift)))
    group_size = math.gcd(N_DP, max(1, 4096 // L))
    model_width = tokens.shape[1]
    inputs = tokens.astype(jnp.float32).reshape(N_DP // group_size, group_size, L, model_width)
    cotangent = d_out.astype(jnp.float32).reshape(N_DP // group_size, group_size, L, model_width)

    def scan_step(totals, element):
        rows_in, cot_rows = element
        outputs, puller = jax.vjp(forward, params, rows_in)
        grad_params, grad_rows = puller((jnp.zeros_like(outputs[0]), cot_rows))
        return (jax.tree.map(jnp.add, totals, grad_params), (outputs[0], outputs[1], grad_rows))
    zeros = jax.tree.map(jnp.zeros_like, params)
    totals, (first_all, second_all, grad_all) = lax.scan(scan_step, zeros, (inputs, cotangent))
    return (first_all.reshape(TOKENS, model_width).astype(jnp.bfloat16), second_all.reshape(TOKENS, model_width).astype(jnp.bfloat16), grad_all.reshape(TOKENS, model_width), totals[0], totals[1], totals[2], totals[3], totals[4], totals[5])
```

```python
import jax
import jax.numpy as jnp
from jax import lax
from jax.sharding import PartitionSpec as P

HEAD_DIM = 64
SOFTNESS = 0.25
EPSILON = 1e-05
F32 = jnp.float32
BF16 = jnp.bfloat16


def mm(a, b, dims):
    return lax.dot_general(a, b, (dims, ((), ())), preferred_element_type=F32)


def nn(a, b):
    return mm(a, b, ((1,), (0,)))


def nt(a, b):
    return mm(a, b, ((1,), (1,)))


def tn(a, b):
    return mm(a, b, ((0,), (0,)))


def normalise(rows_in):
    row_mean = jnp.mean(rows_in, axis=-1, keepdims=True)
    centered = rows_in - row_mean
    spread = jnp.mean(centered * centered, axis=-1, keepdims=True)
    inverse = lax.rsqrt(spread + EPSILON)
    return centered * inverse, inverse


def norm_back(d_normed, unit, inverse, gain):
    scaled = d_normed * gain
    mean_one = jnp.mean(scaled, axis=-1, keepdims=True)
    mean_two = jnp.mean(scaled * unit, axis=-1, keepdims=True)
    return inverse * (scaled - mean_one - unit * mean_two)


def gelu_both(u):
    rate = 0.7978845608028654
    squared = u * u
    bend = jnp.tanh(rate * u * (1.0 + 0.044715 * squared))
    half = 0.5 * (1.0 + bend)
    slope = half + 0.5 * u * (1.0 - bend * bend) * rate * (1.0 + 3 * 0.044715 * squared)
    return u * half, slope


def scores_of(q, k, start, signed):
    scores = nt(q, k) * HEAD_DIM**-0.5
    rows = start + lax.broadcasted_iota(jnp.int32, scores.shape, 0)
    cols = lax.broadcasted_iota(jnp.int32, scores.shape, 1)
    allowed = cols <= rows
    if signed:
        inv_mag = lax.rsqrt(scores * scores + SOFTNESS * SOFTNESS)
        magnitude = (scores * scores + SOFTNESS * SOFTNESS) * inv_mag
    else:
        inv_mag, magnitude = None, scores
    masked = jnp.where(allowed, magnitude, -1e30)
    peak = jnp.max(masked, axis=-1, keepdims=True)
    exponent = jnp.exp(masked - peak)
    softmax_part = exponent / jnp.sum(exponent, axis=-1, keepdims=True)
    return scores, inv_mag, softmax_part


def head_forward(q, k, v, start, signed):
    scores, inv_mag, weights = scores_of(q, k, start, signed)
    if signed:
        weights = weights * (scores * inv_mag)
    return nn(weights.astype(BF16), v).astype(BF16)


def head_backward(q, k, v, d_att, start, signed):
    scores, inv_mag, part = scores_of(q, k, start, signed)
    d_probs = nt(d_att, v)
    if signed:
        sign = scores * inv_mag
        weights = part * sign
        bend = sign * sign + (SOFTNESS * SOFTNESS) * (inv_mag * inv_mag * inv_mag)
        delta = jnp.sum(weights * d_probs, axis=-1, keepdims=True)
        d_scores = part * (d_probs * bend - sign * delta)
    else:
        weights = part
        delta = jnp.sum(weights * d_probs, axis=-1, keepdims=True)
        d_scores = weights * (d_probs - delta)
    low = d_scores.astype(BF16)
    scale = HEAD_DIM**-0.5
    return nn(low, k) * scale, tn(low, q) * scale, tn(weights.astype(BF16), d_att)


def swap_tensor(v):
    return lax.ppermute(v, "tensor", [(0, 1), (1, 0)])


def half_of(v, which, axis):
    size = v.shape[axis] // 2
    return lax.dynamic_slice_in_dim(v, which * size, size, axis)


def joined(own, other, which, axis=0):
    first = which == 0
    return jnp.concatenate(
        [jnp.where(first, own, other), jnp.where(first, other, own)], axis=axis
    )


def pairs(count, step):
    return [(i, i ^ step) for i in range(count)]


def reduce_block(keep, send, place):
    core, x, z = place
    n_dp = 16
    total = keep + lax.ppermute(send, "dp", pairs(n_dp, 1)).astype(F32)
    low = total.astype(BF16)
    total = half_of(total, x, 0) + lax.ppermute(half_of(low, 1 - x, 0), "dp", pairs(n_dp, 2)).astype(F32)
    far = half_of(total, 1 - z // 2, 0)
    near = half_of(total, z // 2, 0)
    line = lambda moves: [(a * 4 + r, b * 4 + r) for a, b in moves for r in range(4)]
    out_to_in = lax.ppermute(far.astype(BF16), "dp", line([(0, 1), (3, 2)])).astype(F32)
    across = lax.ppermute((far + out_to_in).astype(BF16), "dp", line([(1, 2), (2, 1)])).astype(F32)
    near = near + across
    own = half_of(near, z % 2, 0)
    sibling = half_of(near, 1 - z % 2, 0).astype(BF16)
    own = own + lax.ppermute(sibling, "dp", pairs(n_dp, 4)).astype(F32)
    own = own.astype(BF16)
    near = joined(own, lax.ppermute(own, "dp", pairs(n_dp, 4)), z % 2)
    across = lax.ppermute(near, "dp", line([(1, 2), (2, 1)]))
    out = lax.ppermute(across, "dp", line([(1, 0), (2, 3)]))
    far = jnp.where((z == 1) | (z == 2), across, out)
    low = joined(near, far, z // 2)
    low = joined(low, lax.ppermute(low, "dp", pairs(n_dp, 2)), x)
    return low, lax.ppermute(low, "dp", pairs(n_dp, 1))


def reduce_any(keep, send, place, n_dp):
    if n_dp == 16:
        return reduce_block(keep, send, place)
    whole = lax.psum(joined(keep.astype(BF16), send, place[0]), "dp")
    return half_of(whole, place[0], 0), half_of(whole, 1 - place[0], 0)


def sum_small(v, n_dp):
    if n_dp == 16:
        for step in (1, 2, 4, 8):
            v = v + lax.ppermute(v, "dp", pairs(n_dp, step))
        return v + swap_tensor(v)
    return lax.psum(v, ("dp", "tensor"))


def attention_part(stream, gain, shift, w_qkv, earlier, signed):
    unit, inverse = normalise(stream)
    normed = (unit * gain + shift).astype(BF16)
    qkv = [nn(normed, w_qkv[c]).astype(BF16) for c in range(3)]
    keys = jnp.concatenate([b[1] for b in earlier] + [qkv[1]])
    values = jnp.concatenate([b[2] for b in earlier] + [qkv[2]])
    start = keys.shape[0] - stream.shape[0]
    heads = []
    for h in range(keys.shape[1] // HEAD_DIM):
        cut = slice(h * HEAD_DIM, (h + 1) * HEAD_DIM)
        heads.append(head_forward(qkv[0][:, cut], keys[:, cut], values[:, cut], start, signed))
    return normed, qkv, jnp.concatenate(heads, axis=1)


def mlp_part(middle, gain, shift, w_up, w_down):
    unit, inverse = normalise(middle)
    normed = (unit * gain + shift).astype(BF16)
    value, slope = gelu_both(nn(normed, w_up))
    hidden = value.astype(BF16)
    return normed, hidden, slope.astype(BF16), nn(hidden, w_down).astype(BF16)


def attention_back(d_att, blocks, row, signed):
    start = row * d_att.shape[0]
    keys = jnp.concatenate([b[1] for b in blocks[: row + 1]])
    values = jnp.concatenate([b[2] for b in blocks[: row + 1]])
    outs = []
    for h in range(keys.shape[1] // HEAD_DIM):
        cut = slice(h * HEAD_DIM, (h + 1) * HEAD_DIM)
        outs.append(
            head_backward(
                blocks[row][0][:, cut], keys[:, cut], values[:, cut], d_att[:, cut], start, signed
            )
        )
    return [jnp.concatenate(part, axis=1) for part in zip(*outs)]


def on_device(parts, n_dp, tokens, w_qkv, w_out, w_up, w_down, norm_gain, norm_shift, d_out):
    layers = w_qkv.shape[0]
    length = tokens.shape[0]
    size = length // parts
    cuts = [slice(r * size, (r + 1) * size) for r in range(parts)]
    w_qkv = jnp.transpose(w_qkv, (0, 2, 1, 3))
    index = lax.axis_index("dp")
    place = (index % 2, index // 2 % 2, index // 4)
    core = place[0]
    streams = [tokens[c].astype(F32) for c in cuts]
    saved = []
    outputs = []
    for l in range(layers):
        signed = l == 0
        blocks, normed_one, attended, middles, own_parts = [], [], [], [], []
        for r in range(parts):
            normed, qkv, att = attention_part(
                streams[r], norm_gain[l, 0], norm_shift[l, 0], w_qkv[l], blocks, signed
            )
            blocks.append(qkv)
            normed_one.append(normed)
            attended.append(att)
        for r in range(parts):
            partial = nn(attended[r], w_out[l]).astype(BF16)
            middles.append(streams[r] + (partial.astype(F32) + swap_tensor(partial).astype(F32)))
        mlp = []
        nexts = []
        for r in range(parts):
            mlp.append(mlp_part(middles[r], norm_gain[l, 1], norm_shift[l, 1], w_up[l], w_down[l]))
            partial = mlp[r][3]
            nexts.append(middles[r] + (partial.astype(F32) + swap_tensor(partial).astype(F32)))
        saved.append((streams, blocks, normed_one, attended, middles, mlp))
        streams = nexts
        outputs.append(jnp.concatenate([s.astype(BF16) for s in streams]))
    d_next = [d_out[c].astype(F32) for c in cuts]
    small = [[None] * 4 for _ in range(layers)]
    big = [None] * layers

    def row_sums(partials, units):
        own = [p.astype(F32) for p in partials]
        return (
            sum(jnp.sum(o * u, axis=0) for o, u in zip(own, units)),
            sum(jnp.sum(o, axis=0) for o in own),
        )

    for l in reversed(range(layers)):
        signed = l == 0
        streams, blocks, normed_one, attended, middles, mlp = saved[l]
        rows = range(parts)
        d_low = [d.astype(BF16) for d in d_next]
        d_pre = [
            (nt(d_low[r], w_down[l]) * mlp[r][2].astype(F32)).astype(BF16) for r in rows
        ]
        two_own = [nt(d, w_up[l]).astype(BF16) for d in d_pre]
        two_other = [swap_tensor(p) for p in two_own]
        hidden = jnp.concatenate([m[1] for m in mlp])
        normed_two = jnp.concatenate([m[0] for m in mlp])
        low_all, pre_all = jnp.concatenate(d_low), jnp.concatenate(d_pre)

        def mlp_grads(which):
            return jnp.concatenate(
                [tn(half_of(hidden, which, 1), low_all), tn(normed_two, half_of(pre_all, which, 1))],
                axis=1,
            )

        mlp_sum = reduce_any(mlp_grads(core), mlp_grads(1 - core).astype(BF16), place, n_dp)
        d_mid, mid_low, units = [], [], []
        for r in rows:
            unit, inverse = normalise(middles[r])
            units.append(unit)
            total = two_own[r].astype(F32) + two_other[r].astype(F32)
            d_mid.append(d_next[r] + norm_back(total, unit, inverse, norm_gain[l, 1]))
            mid_low.append(d_mid[r].astype(BF16))
        small[l][2:] = row_sums(two_own, units)
        d_qkv = [None] * parts
        carried = None
        for r in reversed(rows):
            d_att = nt(mid_low[r], w_out[l]).astype(BF16)
            d_q, d_k, d_v = attention_back(d_att, blocks, r, signed)
            if carried is not None:
                d_k, d_v = d_k + carried[0], d_v + carried[1]
            carried = (d_k[: r * size], d_v[: r * size])
            d_qkv[r] = [d_q.astype(BF16), d_k[r * size :].astype(BF16), d_v[r * size :].astype(BF16)]
        one_own = [
            sum(nt(d_qkv[r][c], w_qkv[l, c]) for c in range(3)).astype(BF16) for r in rows
        ]
        one_other = [swap_tensor(p) for p in one_own]
        att_all, mid_all = jnp.concatenate(attended), jnp.concatenate(mid_low)
        normed_all = jnp.concatenate(normed_one)
        qkv_all = [jnp.concatenate([d[c] for d in d_qkv]) for c in range(3)]

        def att_grads(which):
            lhs = half_of(normed_all, which, 1)
            return jnp.concatenate(
                [tn(lhs, d) for d in qkv_all] + [tn(att_all, half_of(mid_all, which, 1))], axis=1
            )

        att_sum = reduce_any(att_grads(core), att_grads(1 - core).astype(BF16), place, n_dp)
        big[l] = (mlp_sum, att_sum)
        units = []
        for r in rows:
            unit, inverse = normalise(streams[r])
            units.append(unit)
            total = one_own[r].astype(F32) + one_other[r].astype(F32)
            d_mid[r] = d_mid[r] + norm_back(total, unit, inverse, norm_gain[l, 0])
        small[l][:2] = row_sums(one_own, units)
        d_next = d_mid
    small_sum = sum_small(jnp.stack([s for row in small for s in row]), n_dp)
    small_sum = small_sum.reshape(layers, 2, 2, small_sum.shape[-1])
    width = tokens.shape[1]
    part = w_qkv.shape[3]
    g_qkv, g_out, g_up, g_down = [], [], [], []
    for l in range(layers):
        (own, other), (own_a, other_a) = big[l]
        both = lambda a, b, axis=0: joined(a.astype(F32), b.astype(F32), core, axis)
        g_down.append(both(own[:, :width], other[:, :width]))
        g_up.append(both(own[:, width:], other[:, width:], 1))
        g_qkv.append(
            jnp.stack(
                [
                    both(own_a[:, c * part : (c + 1) * part], other_a[:, c * part : (c + 1) * part])
                    for c in range(3)
                ]
            )
        )
        g_out.append(both(own_a[:, 3 * part :], other_a[:, 3 * part :], 1))
    return (
        outputs[0],
        outputs[1],
        jnp.concatenate(d_next),
        jnp.transpose(jnp.stack(g_qkv), (0, 2, 1, 3)),
        jnp.stack(g_out),
        jnp.stack(g_up),
        jnp.stack(g_down),
        small_sum[:, :, 0],
        small_sum[:, :, 1],
    )


def solution(mesh):
    n_dp = mesh.shape["dp"]
    in_specs = (
        P("dp", None),
        P(None, None, None, "tensor"),
        P(None, "tensor", None),
        P(None, None, "tensor"),
        P(None, "tensor", None),
        P(),
        P(),
        P("dp", None),
    )
    out_specs = (
        P("dp", None),
        P("dp", None),
        P("dp", None),
        P(None, None, None, "tensor"),
        P(None, "tensor", None),
        P(None, None, "tensor"),
        P(None, "tensor", None),
        P(),
        P(),
    )

    def body(*args):
        return on_device(1, n_dp, *args)

    return jax.shard_map(body, mesh=mesh, in_specs=in_specs, out_specs=out_specs, check_vma=False)
```

```python
import functools

import jax
import jax.numpy as jnp
from jax import lax
from jax.experimental import pallas as pl
from jax.experimental.pallas import tpu as pltpu
from jax.sharding import PartitionSpec as P

HEAD_DIM = 64
SOFTNESS = 0.25
EPSILON = 1e-05
F32 = jnp.float32
BF16 = jnp.bfloat16
SCALE = HEAD_DIM**-0.5


def mm(a, b, dims):
    return lax.dot_general(a, b, (dims, ((), ())), preferred_element_type=F32)


def nn(a, b):
    return mm(a, b, ((1,), (0,)))


def nt(a, b):
    return mm(a, b, ((1,), (1,)))


def tn(a, b):
    return mm(a, b, ((0,), (0,)))


def normalise(rows_in):
    row_mean = jnp.mean(rows_in, axis=-1, keepdims=True)
    centered = rows_in - row_mean
    spread = jnp.mean(centered * centered, axis=-1, keepdims=True)
    inverse = lax.rsqrt(spread + EPSILON)
    return centered * inverse, inverse


def norm_back(d_normed, unit, inverse, gain):
    scaled = d_normed * gain
    mean_one = jnp.mean(scaled, axis=-1, keepdims=True)
    mean_two = jnp.mean(scaled * unit, axis=-1, keepdims=True)
    return inverse * (scaled - mean_one - unit * mean_two)


def gelu_both(u):
    rate = 0.7978845608028654
    squared = u * u
    bend = jnp.tanh(rate * u * (1.0 + 0.044715 * squared))
    half = 0.5 * (1.0 + bend)
    slope = half + 0.5 * u * (1.0 - bend * bend) * (rate + (rate * 3 * 0.044715) * squared)
    return u * half, slope


def exponents(q, k, signed):
    scores = nt(q, k) * SCALE
    start = k.shape[0] - q.shape[0]
    rows = start + lax.broadcasted_iota(jnp.int32, scores.shape, 0)
    cols = lax.broadcasted_iota(jnp.int32, scores.shape, 1)
    if signed:
        soft = scores * scores + SOFTNESS * SOFTNESS
        inv_mag = lax.rsqrt(soft)
        magnitude = soft * inv_mag
    else:
        inv_mag, magnitude = None, scores
    masked = jnp.where(cols <= rows, magnitude, -1e30)
    exponent = jnp.exp(masked - jnp.max(masked, axis=-1, keepdims=True))
    return scores, inv_mag, exponent, 1.0 / jnp.sum(exponent, axis=-1, keepdims=True)


def head_forward(q, k, v, signed):
    scores, inv_mag, exponent, inv_sum = exponents(q, k, signed)
    if signed:
        exponent = exponent * (scores * inv_mag)
    return (nn(exponent.astype(BF16), v) * inv_sum).astype(BF16)


def head_backward(q, k, v, d_att, signed):
    scores, inv_mag, exponent, inv_sum = exponents(q, k, signed)
    part = exponent * inv_sum
    d_probs = nt(d_att, v)
    if signed:
        sign = scores * inv_mag
        weights = part * sign
        delta = jnp.sum(weights * d_probs, axis=-1, keepdims=True)
        bend = sign * sign + (SOFTNESS * SOFTNESS) * (inv_mag * inv_mag * inv_mag)
        d_scores = part * (d_probs * bend - sign * delta)
    else:
        weights = part
        delta = jnp.sum(weights * d_probs, axis=-1, keepdims=True)
        d_scores = weights * (d_probs - delta)
    low = d_scores.astype(BF16)
    return nn(low, k) * SCALE, tn(low, q) * SCALE, tn(weights.astype(BF16), d_att)


def head_cuts(width):
    return [slice(h * HEAD_DIM, (h + 1) * HEAD_DIM) for h in range(width // HEAD_DIM)]


def kernel_call(body, outs, *args, smem=0):
    whole = pl.BlockSpec(memory_space=pltpu.VMEM)
    return pl.pallas_call(
        body,
        out_shape=[jax.ShapeDtypeStruct(s, d) for s, d in outs],
        in_specs=[pl.BlockSpec(memory_space=pltpu.SMEM)] * smem + [whole] * (len(args) - smem),
        out_specs=[whole] * len(outs),
        compiler_params=pltpu.CompilerParams(vmem_limit_bytes=28 * 2**20),
    )(*args)


def attention_part(stream, sums, norms, w_qkv, earlier, signed, name):
    rows, width = stream.shape
    part = w_qkv.shape[2]
    count = len(earlier)

    def body(*refs):
        refs = list(refs)
        x_ref = refs.pop(0)
        x = x_ref[...].astype(F32)
        if sums:
            x = x + (refs.pop(0)[...].astype(F32) + refs.pop(0)[...].astype(F32))
        g_ref, s_ref, w_ref = refs.pop(0), refs.pop(0), refs.pop(0)
        olds = [refs.pop(0) for _ in range(2 * count)]
        if sums:
            refs.pop(0)[...] = x
            refs.pop(0)[...] = x.astype(BF16)
        n_ref, q_ref, k_ref, v_ref, a_ref = refs
        unit, _ = normalise(x)
        normed = (unit * g_ref[0:1, :] + s_ref[0:1, :]).astype(BF16)
        n_ref[...] = normed
        for c, ref in enumerate((q_ref, k_ref, v_ref)):
            ref[...] = nn(normed, w_ref[c]).astype(BF16)
        heads = []
        for cut in head_cuts(part):
            k = jnp.concatenate([o[:, cut] for o in olds[:count]] + [k_ref[:, cut]], axis=0)
            v = jnp.concatenate([o[:, cut] for o in olds[count:]] + [v_ref[:, cut]], axis=0)
            heads.append(head_forward(q_ref[:, cut], k, v, signed))
        a_ref[...] = jnp.concatenate(heads, axis=1)

    outs = [((rows, width), BF16)] + [((rows, part), BF16)] * 4
    if sums:
        outs = [((rows, width), F32), ((rows, width), BF16)] + outs
    olds = [b[1] for b in earlier] + [b[2] for b in earlier]
    with jax.named_scope(name):
        res = kernel_call(body, outs, stream, *sums, *norms, w_qkv, *olds)
    if sums:
        stream, low = res[0], res[1]
        res = res[2:]
    else:
        low = None
    return stream, low, res[0], tuple(res[1:4]), res[4]


def mlp_part(side, stream, att_own, att_other, w_out, norms, w_up, w_down, name):
    rows, width = stream.shape
    hid = w_up.shape[1]

    def body(t_ref, x_ref, own_ref, oth_ref, wo_ref, g_ref, s_ref, u_ref, d_ref, m_ref, n_ref, h_ref, b_ref, p_ref):
        first = t_ref[0] == 0
        own, other = own_ref[...], oth_ref[...]
        att = jnp.concatenate([jnp.where(first, own, other), jnp.where(first, other, own)], axis=1)
        middle = x_ref[...].astype(F32) + nn(att, wo_ref[...])
        m_ref[...] = middle
        unit, _ = normalise(middle)
        normed = (unit * g_ref[1:2, :] + s_ref[1:2, :]).astype(BF16)
        n_ref[...] = normed
        value, slope = gelu_both(nn(normed, u_ref[...]))
        hidden = value.astype(BF16)
        h_ref[...] = hidden
        b_ref[...] = slope.astype(BF16)
        p_ref[...] = nn(hidden, d_ref[...]).astype(BF16)

    outs = [
        ((rows, width), F32),
        ((rows, width), BF16),
        ((rows, hid), BF16),
        ((rows, hid), BF16),
        ((rows, width), BF16),
    ]
    with jax.named_scope(name):
        return kernel_call(
            body, outs, side, stream, att_own, att_other, w_out, *norms, w_up, w_down, smem=1
        )


def mlp_back(d_in, upper, slope, w_up, w_down, name):
    rows, width = d_in.shape
    hid = w_up.shape[1]

    def body(*refs):
        refs = list(refs)
        d_ref = refs.pop(0)
        if upper:
            own_ref, oth_ref, x_ref, g_ref = refs[:4]
            refs = refs[4:]
            slope_ref, u_ref, w_ref, next_ref, low_ref, pre_ref, p_ref = refs
            unit, inverse = normalise(x_ref[...])
            total = own_ref[...].astype(F32) + oth_ref[...].astype(F32)
            d_next = d_ref[...] + norm_back(total, unit, inverse, g_ref[0:1, :])
            next_ref[...] = d_next
            low = d_next.astype(BF16)
            low_ref[...] = low
        else:
            slope_ref, u_ref, w_ref, pre_ref, p_ref = refs
            low = d_ref[...]
        d_pre = (nt(low, w_ref[...]) * slope_ref[...].astype(F32)).astype(BF16)
        pre_ref[...] = d_pre
        p_ref[...] = nt(d_pre, u_ref[...]).astype(BF16)

    outs = [((rows, hid), BF16), ((rows, width), BF16)]
    if upper:
        outs = [((rows, width), F32), ((rows, width), BF16)] + outs
    with jax.named_scope(name):
        res = kernel_call(body, outs, d_in, *upper, slope, w_up, w_down)
    if upper:
        return res
    return [d_in, d_in, *res]


def attention_back(d_next, two, middle, stream, gain, w_out, w_qkv, blocks, carried, signed, name):
    rows, width = middle.shape
    part = w_qkv.shape[2]
    count = len(blocks)
    before = (count - 1) * rows
    has = len(carried)

    def body(*refs):
        refs = list(refs)
        dn_ref, own_ref, oth_ref, m_ref, x_ref, g_ref, wo_ref, w_ref = refs[:8]
        refs = refs[8:]
        q_ref = refs.pop(0)
        k_refs = [refs.pop(0) for _ in range(count)]
        v_refs = [refs.pop(0) for _ in range(count)]
        c_refs = [refs.pop(0) for _ in range(has)]
        mid_ref, low_ref, dq_ref, dk_ref, dv_ref, p_ref, small_ref = refs[:7]
        out_carried = refs[7:]
        unit, inverse = normalise(m_ref[...])
        own = own_ref[...].astype(F32)
        small_ref[2:3, :] = jnp.sum(own * unit, axis=0, keepdims=True)
        small_ref[3:4, :] = jnp.sum(own, axis=0, keepdims=True)
        total = own + oth_ref[...].astype(F32)
        d_mid = dn_ref[...].astype(F32) + norm_back(total, unit, inverse, g_ref[1:2, :])
        mid_ref[...] = d_mid
        low = d_mid.astype(BF16)
        low_ref[...] = low
        d_att = nt(low, wo_ref[...]).astype(BF16)
        grads = []
        for cut in head_cuts(part):
            k = jnp.concatenate([r[:, cut] for r in k_refs], axis=0)
            v = jnp.concatenate([r[:, cut] for r in v_refs], axis=0)
            grads.append(head_backward(q_ref[:, cut], k, v, d_att[:, cut], signed))
        d_q, d_k, d_v = [jnp.concatenate(g, axis=1) for g in zip(*grads)]
        if has:
            d_k, d_v = d_k + c_refs[0][...], d_v + c_refs[1][...]
        if before:
            out_carried[0][...] = d_k[:before]
            out_carried[1][...] = d_v[:before]
        d_q, d_k, d_v = d_q.astype(BF16), d_k[before:].astype(BF16), d_v[before:].astype(BF16)
        dq_ref[...] = d_q
        dk_ref[...] = d_k
        dv_ref[...] = d_v
        partial = (nt(d_q, w_ref[0]) + nt(d_k, w_ref[1]) + nt(d_v, w_ref[2])).astype(BF16)
        p_ref[...] = partial
        unit, _ = normalise(x_ref[...].astype(F32))
        own = partial.astype(F32)
        small_ref[0:1, :] = jnp.sum(own * unit, axis=0, keepdims=True)
        small_ref[1:2, :] = jnp.sum(own, axis=0, keepdims=True)

    outs = [((rows, width), F32), ((rows, width), BF16)] + [((rows, part), BF16)] * 3
    outs += [((rows, width), BF16), ((4, width), F32)]
    if before:
        outs += [((before, part), F32)] * 2
    with jax.named_scope(name):
        res = kernel_call(
            body,
            outs,
            d_next,
            *two,
            middle,
            stream,
            gain,
            w_out,
            w_qkv,
            blocks[-1][0],
            *[b[1] for b in blocks],
            *[b[2] for b in blocks],
            *carried,
        )
    return res[0], res[1], tuple(res[2:5]), res[5], res[6], tuple(res[7:])


def rows_joined(refs):
    return jnp.concatenate([r[...] for r in refs], axis=0)


def pair_grads(core, lhs_half, rhs_whole, lhs_whole, rhs_half, name):
    n = len(lhs_half)
    half_l = lhs_half[0].shape[1] // 2
    half_r = rhs_half[0].shape[1] // 2
    wide = [b.shape[1] for b in rhs_whole[0]]
    out_cols = sum(wide) + half_r
    flat = list(lhs_half) + list(lhs_whole)
    for group in rhs_whole:
        flat += list(group)
    flat += list(rhs_half)

    def body(c_ref, *refs):
        refs = list(refs)
        send_ref, keep_ref = refs[-2:]
        lh = refs[:n]
        lw = refs[n : 2 * n]
        rw = [refs[2 * n + i * len(wide) : 2 * n + (i + 1) * len(wide)] for i in range(n)]
        rh = refs[2 * n + n * len(wide) : -2]
        c = c_ref[0]
        for which, out_ref in ((1 - c, send_ref), (c, keep_ref)):
            at_l = pl.ds(pl.multiple_of(which * half_l, 128), half_l)
            at_r = pl.ds(pl.multiple_of(which * half_r, 128), half_r)
            left = jnp.concatenate([r[:, at_l] for r in lh], axis=0)
            col = 0
            for j, w in enumerate(wide):
                right = jnp.concatenate([rw[i][j][...] for i in range(n)], axis=0)
                out_ref[:, col : col + w] = tn(left, right).astype(BF16)
                col += w
            left = rows_joined(lw)
            right = jnp.concatenate([r[:, at_r] for r in rh], axis=0)
            out_ref[:, col:] = tn(left, right).astype(BF16)

    outs = [((half_l, out_cols), BF16)] * 2
    with jax.named_scope(name):
        return kernel_call(body, outs, core, *flat, smem=1)


def swap_tensor(v):
    return lax.ppermute(v, "tensor", [(0, 1), (1, 0)])


def half_of(v, which, axis):
    size = v.shape[axis] // 2
    return lax.dynamic_slice_in_dim(v, which * size, size, axis)


def joined(own, other, which, axis=0):
    first = which == 0
    return jnp.concatenate(
        [jnp.where(first, own, other), jnp.where(first, other, own)], axis=axis
    )


def pairs(count, step):
    return [(i, i ^ step) for i in range(count)]


def line(moves):
    return [(a * 4 + r, b * 4 + r) for a, b in moves for r in range(4)]


def plus(a, b):
    return (a.astype(F32) + b.astype(F32)).astype(BF16)


def reduce_block(keep, send, place):
    core, x, z = place
    n_dp = 16
    came = lax.ppermute(send, "dp", pairs(n_dp, 1))
    away = plus(half_of(keep, 1 - x, 0), half_of(came, 1 - x, 0))
    total = plus(half_of(keep, x, 0), half_of(came, x, 0))
    came = lax.ppermute(away, "dp", pairs(n_dp, 2))
    far = plus(half_of(total, 1 - z // 2, 0), half_of(came, 1 - z // 2, 0))
    near = plus(half_of(total, z // 2, 0), half_of(came, z // 2, 0))
    inward = lax.ppermute(far, "dp", line([(0, 1), (3, 2)]))
    across = lax.ppermute(plus(far, inward), "dp", line([(1, 2), (2, 1)]))
    sibling = plus(half_of(near, 1 - z % 2, 0), half_of(across, 1 - z % 2, 0))
    own = plus(half_of(near, z % 2, 0), half_of(across, z % 2, 0))
    own = plus(own, lax.ppermute(sibling, "dp", pairs(n_dp, 4)))
    near = joined(own, lax.ppermute(own, "dp", pairs(n_dp, 4)), z % 2)
    across = lax.ppermute(near, "dp", line([(1, 2), (2, 1)]))
    out = lax.ppermute(across, "dp", line([(1, 0), (2, 3)]))
    far = jnp.where((z == 1) | (z == 2), across, out)
    low = joined(near, far, z // 2)
    low = joined(low, lax.ppermute(low, "dp", pairs(n_dp, 2)), x)
    return low, lax.ppermute(low, "dp", pairs(n_dp, 1))


def reduce_any(keep, send, place, n_dp):
    if n_dp == 16:
        return reduce_block(keep, send, place)
    whole = lax.psum(joined(keep, send, place[0]), "dp")
    return half_of(whole, place[0], 0), half_of(whole, 1 - place[0], 0)


def sum_small(v, n_dp):
    if n_dp == 16:
        for step in (1, 2, 4, 8):
            v = v + lax.ppermute(v, "dp", pairs(n_dp, step))
        return v + swap_tensor(v)
    return lax.psum(v, ("dp", "tensor"))


def full_w_out(w_out, core, side, n_dp):
    part = swap_tensor(half_of(w_out, core, 0))
    other = joined(part, lax.ppermute(part, "dp", pairs(n_dp, 1)), core)
    return joined(w_out, other, side)


def on_device(parts, n_dp, tokens, w_qkv, w_out, w_up, w_down, norm_gain, norm_shift, d_out):
    layers = w_qkv.shape[0]
    length, width = tokens.shape
    size = length // parts
    rows = range(parts)
    cuts = [slice(r * size, (r + 1) * size) for r in rows]
    w_qkv = jnp.transpose(w_qkv, (0, 2, 1, 3))
    index = lax.axis_index("dp")
    side = lax.axis_index("tensor")
    place = (index % 2, index // 2 % 2, index // 4)
    core = place[0]
    core_arg = core.reshape(1).astype(jnp.int32)
    side_arg = side.reshape(1).astype(jnp.int32)
    streams = [tokens[c] for c in cuts]
    sums = [()] * parts
    saved = []
    outputs = []
    for l in range(layers):
        signed = l == 0
        norms = (norm_gain[l], norm_shift[l])
        whole_out = full_w_out(w_out[l], core, side, n_dp)
        blocks, normed_one, attended, mlp, inputs, lows = [], [], [], [], [], []
        for r in rows:
            stream, low, normed, qkv, att = attention_part(
                streams[r], sums[r], norms, w_qkv[l], blocks, signed, f"attention_{l}_{r}"
            )
            inputs.append(stream)
            lows.append(low)
            blocks.append(qkv)
            normed_one.append(normed)
            attended.append(att)
        if l:
            outputs.append(jnp.concatenate(lows))
        for r in rows:
            mlp.append(
                mlp_part(
                    side_arg, inputs[r], attended[r], swap_tensor(attended[r]), whole_out, norms,
                    w_up[l], w_down[l], f"mlp_{l}_{r}",
                )
            )
        saved.append((inputs, blocks, normed_one, attended, mlp))
        streams = [m[0] for m in mlp]
        sums = [(m[4], swap_tensor(m[4])) for m in mlp]
    outputs.append(
        jnp.concatenate(
            [
                (s + (a.astype(F32) + b.astype(F32))).astype(BF16)
                for s, (a, b) in zip(streams, sums)
            ]
        )
    )
    d_in = [d_out[c] for c in cuts]
    upper = [()] * parts
    small = [None] * layers
    big = [None] * layers
    for l in reversed(range(layers)):
        signed = l == 0
        inputs, blocks, normed_one, attended, mlp = saved[l]
        order = list(reversed(rows))
        back = [None] * parts
        two = [None] * parts
        for r in order:
            back[r] = mlp_back(d_in[r], upper[r], mlp[r][3], w_up[l], w_down[l], f"mlp_back_{l}_{r}")
            two[r] = (back[r][3], swap_tensor(back[r][3]))
        send, keep = pair_grads(
            core_arg,
            [m[2] for m in mlp],
            [[b[1]] for b in back],
            [m[1] for m in mlp],
            [b[2] for b in back],
            f"mlp_grads_{l}",
        )
        mlp_sum = reduce_any(keep, send, place, n_dp)
        d_mid, mid_low, d_qkv, one, sums_small = ([None] * parts for _ in range(5))
        carried = ()
        for r in order:
            d_mid[r], mid_low[r], d_qkv[r], own, sums_small[r], carried = attention_back(
                back[r][0], two[r], mlp[r][0], inputs[r], norm_gain[l], w_out[l], w_qkv[l],
                blocks[: r + 1], carried, signed, f"attention_back_{l}_{r}",
            )
            one[r] = (own, swap_tensor(own))
        send, keep = pair_grads(
            core_arg, normed_one, d_qkv, attended, mid_low, f"attention_grads_{l}"
        )
        att_sum = reduce_any(keep, send, place, n_dp)
        big[l] = (mlp_sum, att_sum)
        small[l] = sum(sums_small)
        d_in = d_mid
        upper = [(*one[r], inputs[r], norm_gain[l]) for r in rows]
    grads = []
    for r in rows:
        own, other, stream, gain = upper[r]
        unit, inverse = normalise(stream.astype(F32))
        total = own.astype(F32) + other.astype(F32)
        grads.append(d_in[r] + norm_back(total, unit, inverse, gain[0:1]))
    small_sum = sum_small(jnp.concatenate(small), n_dp).reshape(layers, 2, 2, width)
    part = w_qkv.shape[3]
    g_qkv, g_out, g_up, g_down = [], [], [], []
    for l in range(layers):
        (own, other), (own_a, other_a) = big[l]
        both = lambda a, b, axis=0: joined(a.astype(F32), b.astype(F32), core, axis)
        g_down.append(both(own[:, :width], other[:, :width]))
        g_up.append(both(own[:, width:], other[:, width:], 1))
        g_qkv.append(
            jnp.stack(
                [
                    both(own_a[:, c * part : (c + 1) * part], other_a[:, c * part : (c + 1) * part])
                    for c in range(3)
                ]
            )
        )
        g_out.append(both(own_a[:, 3 * part :], other_a[:, 3 * part :], 1))
    return (
        outputs[0],
        outputs[1],
        jnp.concatenate(grads),
        jnp.transpose(jnp.stack(g_qkv), (0, 2, 1, 3)),
        jnp.stack(g_out),
        jnp.stack(g_up),
        jnp.stack(g_down),
        small_sum[:, :, 0],
        small_sum[:, :, 1],
    )


def solution(mesh):
    n_dp = mesh.shape["dp"]
    in_specs = (
        P("dp", None),
        P(None, None, None, "tensor"),
        P(None, "tensor", None),
        P(None, None, "tensor"),
        P(None, "tensor", None),
        P(),
        P(),
        P("dp", None),
    )
    out_specs = (
        P("dp", None),
        P("dp", None),
        P("dp", None),
        P(None, None, None, "tensor"),
        P(None, "tensor", None),
        P(None, None, "tensor"),
        P(None, "tensor", None),
        P(),
        P(),
    )

    def body(*args):
        return on_device(2, n_dp, *args)

    return jax.shard_map(body, mesh=mesh, in_specs=in_specs, out_specs=out_specs, check_vma=False)
```

```python
import functools

import jax
import jax.numpy as jnp
from jax import lax
from jax.experimental import pallas as pl
from jax.experimental.pallas import tpu as pltpu
from jax.sharding import PartitionSpec as P

HEAD_DIM = 64
SOFTNESS = 0.25
EPSILON = 1e-05
F32 = jnp.float32
BF16 = jnp.bfloat16
SCALE = HEAD_DIM**-0.5


def mm(a, b, dims):
    return lax.dot_general(a, b, (dims, ((), ())), preferred_element_type=F32)


def nn(a, b):
    return mm(a, b, ((1,), (0,)))


def nt(a, b):
    return mm(a, b, ((1,), (1,)))


def tn(a, b):
    return mm(a, b, ((0,), (0,)))


def normalise(rows_in):
    row_mean = jnp.mean(rows_in, axis=-1, keepdims=True)
    centered = rows_in - row_mean
    spread = jnp.mean(centered * centered, axis=-1, keepdims=True)
    inverse = lax.rsqrt(spread + EPSILON)
    return centered * inverse, inverse


def norm_back(d_normed, unit, inverse, gain):
    scaled = d_normed * gain
    mean_one = jnp.mean(scaled, axis=-1, keepdims=True)
    mean_two = jnp.mean(scaled * unit, axis=-1, keepdims=True)
    return inverse * (scaled - mean_one - unit * mean_two)


def gelu_both(u):
    rate = 0.7978845608028654
    squared = u * u
    bend = jnp.tanh(rate * u * (1.0 + 0.044715 * squared))
    half = 0.5 * (1.0 + bend)
    slope = half + 0.5 * u * (1.0 - bend * bend) * (rate + (rate * 3 * 0.044715) * squared)
    return u * half, slope


def exponents(q, k, signed):
    scores = nt(q, k) * SCALE
    start = k.shape[0] - q.shape[0]
    rows = start + lax.broadcasted_iota(jnp.int32, scores.shape, 0)
    cols = lax.broadcasted_iota(jnp.int32, scores.shape, 1)
    if signed:
        soft = scores * scores + SOFTNESS * SOFTNESS
        inv_mag = lax.rsqrt(soft)
        magnitude = soft * inv_mag
    else:
        inv_mag, magnitude = None, scores
    masked = jnp.where(cols <= rows, magnitude, -1e30)
    exponent = jnp.exp(masked - jnp.max(masked, axis=-1, keepdims=True))
    return scores, inv_mag, exponent, 1.0 / jnp.sum(exponent, axis=-1, keepdims=True)


def head_forward(q, k, v, signed):
    scores, inv_mag, exponent, inv_sum = exponents(q, k, signed)
    if signed:
        exponent = exponent * (scores * inv_mag)
    return (nn(exponent.astype(BF16), v) * inv_sum).astype(BF16)


def head_backward(q, k, v, d_att, signed):
    scores, inv_mag, exponent, inv_sum = exponents(q, k, signed)
    part = exponent * inv_sum
    d_probs = nt(d_att, v)
    if signed:
        sign = scores * inv_mag
        weights = part * sign
        delta = jnp.sum(weights * d_probs, axis=-1, keepdims=True)
        bend = sign * sign + (SOFTNESS * SOFTNESS) * (inv_mag * inv_mag * inv_mag)
        d_scores = part * (d_probs * bend - sign * delta)
    else:
        weights = part
        delta = jnp.sum(weights * d_probs, axis=-1, keepdims=True)
        d_scores = weights * (d_probs - delta)
    low = d_scores.astype(BF16)
    return nn(low, k) * SCALE, tn(low, q) * SCALE, tn(weights.astype(BF16), d_att)


def head_cuts(width):
    return [slice(h * HEAD_DIM, (h + 1) * HEAD_DIM) for h in range(width // HEAD_DIM)]


class Kept:
    def __init__(self, ref, target, sem):
        self.ref = ref
        self.copy = pltpu.make_async_copy(ref, target, sem)


def store(out, value):
    if isinstance(out, Kept):
        out.ref[...] = value
        out.copy.start()
        return out.ref
    out[...] = value
    return out


def near(array, at=None):
    return (None, at, array)


def load_rows(array, start, rows):
    return near(array, pl.ds(start, rows))


def unit_of(normed, norms, layer, which):
    gain, shift = [ref[layer, which : which + 1, :] for ref in norms]
    return (normed.astype(F32) - shift) * (1.0 / gain)


def takes(microseconds):
    return pl.CostEstimate(flops=int(microseconds * 30e9), bytes_accessed=2**16, transcendentals=0)


class Order:
    def __init__(self):
        self.token = jnp.zeros((8, 128), F32)

    @staticmethod
    def with_layers(body, loads, args, smem):
        count, placed = len(args), [v for v in loads if v[0] is None]
        copied = len(loads) - len(placed)

        def full(*refs):
            getters = iter(refs[:copied])
            ins = refs[copied : copied + count]
            extra = iter(refs[copied + count : copied + count + len(placed)])
            given = []
            for v in loads:
                if v[0] is None:
                    given.append(lambda ref=next(extra), at=v[1]: ref if at is None else ref.at[at])
                else:
                    given.append(next(getters))
            body(*given, *ins, *refs[copied + count + len(placed) :])

        return full

    def call(self, name, body, outs, *args, smem=0, loads=(), cost=1):
        whole = pl.BlockSpec(memory_space=pltpu.VMEM)
        far = pl.BlockSpec(memory_space=pltpu.HBM)
        placed = [v for v in loads if v[0] is None]
        body, args = self.with_layers(body, loads, args, smem), [*args, *[v[2] for v in placed]]
        loads = [v for v in loads if v[0] is not None]
        sources = [piece[0] for _, _, pieces in loads for piece in pieces]
        kept = [len(out) > 2 for out in outs]
        count, extra = len(args), len(sources)

        def inner(*refs):
            ins, given = refs[:count], refs[count : count + extra]
            at = count + extra + 1
            results = list(refs[at : at + len(outs)])
            at += len(outs) + 1
            buffers = refs[at : at + len(loads)]
            at += len(loads)
            getters, used = [], 0
            for buffer, (_, _, pieces) in zip(buffers, loads):
                copies = []
                for _, place, rows, first in pieces:
                    source = given[used] if place is None else given[used].at[place]
                    target = buffer
                    if rows is not None:
                        start = pl.multiple_of(first(*ins[:smem]), 16)
                        target = buffer.at[pl.ds(start, rows), :]
                    copies.append(pltpu.make_async_copy(source, target, refs[-1].at[used]))
                    copies[-1].start()
                    used += 1

                def get(buffer=buffer, copies=copies):
                    for copy in copies:
                        copy.wait()
                    return buffer

                getters.append(get)
            out_copies = []
            for k, out in enumerate(outs):
                if kept[k]:
                    results[k] = Kept(refs[at], results[k], refs[-1].at[used])
                    out_copies.append(results[k].copy)
                    at += 1
                    used += 1
            body(*getters, *ins, *results)
            for copy in out_copies:
                copy.wait()

        scratch = [pltpu.VMEM(shape, dtype) for shape, dtype, _ in loads]
        scratch += [pltpu.VMEM(out[0], out[1]) for out in outs if len(out) > 2]
        if scratch:
            scratch.append(pltpu.SemaphoreType.DMA((extra + sum(kept),)))
        with jax.named_scope(name):
            *res, self.token = pl.pallas_call(
                inner,
                out_shape=[
                    pltpu.HBM(out[0], out[1]) if keep else jax.ShapeDtypeStruct(out[0], out[1])
                    for out, keep in zip(outs, kept)
                ]
                + [pltpu.HBM(self.token.shape, F32)],
                in_specs=[pl.BlockSpec(memory_space=pltpu.SMEM)] * smem
                + [whole] * (count - smem)
                + [far] * (extra + 1),
                out_specs=[far if keep else whole for keep in kept] + [far],
                scratch_shapes=scratch,
                compiler_params=pltpu.CompilerParams(vmem_limit_bytes=24 * 2**20),
                cost_estimate=takes(cost),
            )(*args, *[pltpu.with_memory_space_constraint(v, pltpu.HBM) for v in (*sources, self.token)])
        return res

    def gate(self, value):
        value, self.token = lax.optimization_barrier((value, self.token))
        return value


def attention_part(run, layer, rows, spot, stream, sums, norms, w_qkv, earlier, signed, name):
    width, part = w_qkv.shape[2], w_qkv.shape[3]
    count = len(earlier)

    def body(*refs):
        refs = list(refs)
        x_get, w_get = refs[:2]
        olds = refs[2 : 2 + 2 * count]
        refs = refs[3 + 2 * count :]
        x = x_get()[...].astype(F32)
        if sums:
            x = x + (refs.pop(0)[...].astype(F32) + refs.pop(0)[...].astype(F32))
        g_ref, s_ref = refs.pop(0), refs.pop(0)
        if sums:
            store(refs.pop(0), x)
            store(refs.pop(0), x.astype(BF16))
        n_out, q_out, k_out, v_out, a_ref, i_ref = refs
        unit, inverse = normalise(x)
        store(i_ref, inverse)
        normed = (unit * g_ref[layer, 0:1, :] + s_ref[layer, 0:1, :]).astype(BF16)
        store(n_out, normed)
        w_ref = w_get()
        q_ref, k_ref, v_ref = [
            store(out, nn(normed, w_ref[c]).astype(BF16)) for c, out in enumerate((q_out, k_out, v_out))
        ]
        olds = [get() for get in olds]
        heads = []
        for cut in head_cuts(part):
            k = jnp.concatenate([o[:, cut] for o in olds[:count]] + [k_ref[:, cut]], axis=0)
            v = jnp.concatenate([o[:, cut] for o in olds[count:]] + [v_ref[:, cut]], axis=0)
            heads.append(head_forward(q_ref[:, cut], k, v, signed))
        store(a_ref, jnp.concatenate(heads, axis=1))

    outs = [((rows, width), BF16)] + [((rows, part), BF16)] * 4 + [((rows, 1), F32)]
    if sums:
        outs = [((rows, width), F32), ((rows, width), BF16, True)] + outs
    olds = [near(b[1]) for b in earlier] + [near(b[2]) for b in earlier]
    res = run.call(
        name, body, outs, spot, *sums, *norms, smem=1, loads=[stream, near(w_qkv, layer)] + olds, cost=4
    )
    low = None
    if sums:
        stream, low = near(res[0]), res[1]
        res = res[2:]
    return stream, low, res[0], tuple(res[1:4]), res[4], res[5]


def mlp_part(run, layer, rows, spot, stream, att_own, att_other, w_out, lacking, norms, w_up, w_down, name):
    width, hid = w_up.shape[1], w_up.shape[2]
    half = w_out.shape[1]
    quarter = half // 2
    w_pieces = [
        (w_out, layer, half, lambda t: t[3] * half),
        (lacking[0], None, quarter, lambda t: (1 - t[3]) * half + t[0] * quarter),
        (lacking[1], None, quarter, lambda t: (1 - t[3]) * half + (1 - t[0]) * quarter),
    ]

    def body(wo_get, x_get, u_get, d_get, t_ref, own_ref, oth_ref, g_ref, s_ref, m_out, n_out, h_out, b_out, p_ref, i_ref):
        first = t_ref[3] == 0
        own, other = own_ref[...], oth_ref[...]
        att = jnp.concatenate([jnp.where(first, own, other), jnp.where(first, other, own)], axis=1)
        wo_ref = wo_get()
        middle = x_get()[...].astype(F32) + nn(att, wo_ref[...])
        store(m_out, middle)
        unit, inverse = normalise(middle)
        store(i_ref, inverse)
        normed = (unit * g_ref[layer, 1:2, :] + s_ref[layer, 1:2, :]).astype(BF16)
        store(n_out, normed)
        value, slope = gelu_both(nn(normed, u_get()[...]))
        hidden = value.astype(BF16)
        store(h_out, hidden)
        store(b_out, slope.astype(BF16))
        store(p_ref, nn(hidden, d_get()[...]).astype(BF16))

    outs = [
        ((rows, width), F32),
        ((rows, width), BF16),
        ((rows, hid), BF16),
        ((rows, hid), BF16),
        ((rows, width), BF16),
        ((rows, 1), F32),
    ]
    return run.call(
        name, body, outs, spot, att_own, att_other, *norms, smem=1,
        loads=[((2 * half, width), BF16, w_pieces), stream, near(w_up, layer), near(w_down, layer)],
        cost=4,
    )


def mlp_back(run, layer, rows, d_in, upper, slope, w_up, w_down, name):
    width, hid = w_up.shape[1], w_up.shape[2]

    def body(*refs):
        refs = list(refs)
        w_get, slope_get, u_get, x_get = refs[:4]
        if upper:
            d_ref, own_ref, oth_ref, i_ref, g_ref, s_ref, next_ref, low_ref, pre_ref, p_ref = refs[4:]
            unit = unit_of(x_get()[...], (g_ref, s_ref), layer + 1, 0)
            inverse = i_ref[...]
            total = own_ref[...].astype(F32) + oth_ref[...].astype(F32)
            d_next = d_ref[...] + norm_back(total, unit, inverse, g_ref[layer + 1, 0:1, :])
            store(next_ref, d_next)
            low = d_next.astype(BF16)
            store(low_ref, low)
        else:
            pre_ref, p_ref = refs[4:]
            low = x_get()[...]
        d_pre = (nt(low, w_get()[...]) * slope_get()[...].astype(F32)).astype(BF16)
        store(pre_ref, d_pre)
        store(p_ref, nt(d_pre, u_get()[...]).astype(BF16))

    outs = [((rows, hid), BF16), ((rows, width), BF16)]
    loads = [near(w_down, layer), near(slope), near(w_up, layer)]
    if upper:
        outs = [((rows, width), F32), ((rows, width), BF16)] + outs
        return run.call(name, body, outs, d_in, *upper[1:], loads=loads + [upper[0]], cost=3)
    res = run.call(name, body, outs, loads=loads + [d_in], cost=3)
    return [None, None, *res]


def attention_back(
    run, layer, d_next, two, normed_two, inverse_two, normed_one, norms, w_out, w_qkv, blocks, carried, signed, name
):
    rows, width = normed_two.shape
    part = w_qkv.shape[3]
    count = len(blocks)
    before = (count - 1) * rows
    has = len(carried)
    late = isinstance(d_next, tuple)

    def body(*refs):
        m_get, wo_get, q_get = refs[:3]
        kv_gets = refs[3 : 3 + 2 * count]
        w_get, x_get = refs[3 + 2 * count : 5 + 2 * count]
        refs = list(refs[5 + 2 * count :])
        dn_get = refs.pop(0) if late else None
        dn_ref = None if late else refs.pop(0)
        own_ref, oth_ref, i_ref, g_ref, s_ref = refs[:5]
        refs = refs[5:]
        c_refs = refs[:has]
        mid_ref, low_ref, dq_ref, dk_ref, dv_ref, p_ref, small_ref = refs[has : 7 + has]
        out_carried = refs[7 + has :]
        unit = unit_of(m_get()[...], (g_ref, s_ref), layer, 1)
        inverse = i_ref[...]
        own = own_ref[...].astype(F32)
        small_ref[2:3, :] = jnp.sum(own * unit, axis=0, keepdims=True)
        small_ref[3:4, :] = jnp.sum(own, axis=0, keepdims=True)
        total = own + oth_ref[...].astype(F32)
        if late:
            dn_ref = dn_get()
        d_mid = dn_ref[...].astype(F32) + norm_back(total, unit, inverse, g_ref[layer, 1:2, :])
        store(mid_ref, d_mid)
        low = d_mid.astype(BF16)
        store(low_ref, low)
        d_att = nt(low, wo_get()[...]).astype(BF16)
        q_ref = q_get()
        kv_refs = [get() for get in kv_gets]
        grads = []
        for cut in head_cuts(part):
            k = jnp.concatenate([r[:, cut] for r in kv_refs[:count]], axis=0)
            v = jnp.concatenate([r[:, cut] for r in kv_refs[count:]], axis=0)
            grads.append(head_backward(q_ref[:, cut], k, v, d_att[:, cut], signed))
        d_q, d_k, d_v = [jnp.concatenate(g, axis=1) for g in zip(*grads)]
        if has:
            d_k, d_v = d_k + c_refs[0][...], d_v + c_refs[1][...]
        if before:
            out_carried[0][...] = d_k[:before]
            out_carried[1][...] = d_v[:before]
        d_q, d_k, d_v = d_q.astype(BF16), d_k[before:].astype(BF16), d_v[before:].astype(BF16)
        dq_ref[...] = d_q
        dk_ref[...] = d_k
        dv_ref[...] = d_v
        w_ref = w_get()
        partial = (nt(d_q, w_ref[0]) + nt(d_k, w_ref[1]) + nt(d_v, w_ref[2])).astype(BF16)
        p_ref[...] = partial
        unit = unit_of(x_get()[...], (g_ref, s_ref), layer, 0)
        own = partial.astype(F32)
        small_ref[0:1, :] = jnp.sum(own * unit, axis=0, keepdims=True)
        small_ref[1:2, :] = jnp.sum(own, axis=0, keepdims=True)

    outs = [((rows, width), F32), ((rows, width), BF16)] + [((rows, part), BF16)] * 3
    outs += [((rows, width), BF16), ((4, width), F32)]
    if before:
        outs += [((before, part), F32)] * 2
    loads = [near(normed_two), near(w_out, layer), near(blocks[-1][0])]
    loads += [near(b[1]) for b in blocks] + [near(b[2]) for b in blocks]
    loads += [near(w_qkv, layer), near(normed_one)]
    args = [*two, inverse_two, *norms, *carried]
    if late:
        loads.append(d_next)
    else:
        args = [d_next] + args
    res = run.call(name, body, outs, *args, loads=loads, cost=8)
    return res[0], res[1], tuple(res[2:5]), res[5], res[6], tuple(res[7:])


def weight_grads(run, spot, job, name, small=()):
    flat, steps, height, width = [], [], None, 0
    for left, right, halved in job:
        cols = [b[0].shape[1] for b in (left, right)]
        cols[halved] //= 2
        steps.append((len(flat), len(left), cols, halved, width))
        flat += list(left) + list(right)
        height = cols[0]
        width += cols[1]
    count = len(flat)
    extra = 16 if small else 0
    half = height // 2

    def body(c_ref, *refs):
        core_here = c_ref[0]
        for which, out_ref in zip((1 - core_here, core_here), refs[count + 4 * bool(small) :]):
            for at, blocks, cols, halved, col in steps:
                sides = []
                for side in range(2):
                    group = refs[at + side * blocks : at + (side + 1) * blocks]
                    if side == halved:
                        start = pl.multiple_of(which * cols[side], 128)
                        group = [r[:, pl.ds(start, cols[side])] for r in group]
                    else:
                        group = [r[...] for r in group]
                    sides.append(jnp.concatenate(group, axis=0))
                value = tn(*sides).astype(BF16)
                out_ref[:half, col : col + cols[1]] = value[:half]
                out_ref[half + extra : 2 * half + extra, col : col + cols[1]] = value[half:]
            if extra:
                sums = [r[...] for r in refs[count : count + 4]]
                sums = jnp.concatenate([sums[0] + sums[1], sums[2] + sums[3]], axis=0)
                wide = sums.shape[1]
                rest = jnp.zeros((8, wide), F32)
                sums = jnp.concatenate([sums, rest], axis=0).astype(BF16)
                for h in range(2):
                    at = (h + 1) * half + h * extra
                    out_ref[at : at + extra, :wide] = sums
                    out_ref[at : at + extra, wide:] = jnp.zeros((extra, width - wide), BF16)

    outs = [((height + 2 * extra, width), BF16)] * 2
    return run.call(name, body, outs, spot, *flat, *small, smem=1, cost=3)


def place_pieces(run, pieces, slots, total, shape, block, index, layer, steps, name, cols=None, at=0, used=None):
    rows = pieces[0].shape[0] // steps
    used = used or rows
    cols = cols or pieces[0].shape[1]
    count = len(pieces)

    def body(s_ref, *refs):
        out_ref = refs[-2]
        turn = pl.program_id(0)
        for k in range(count):

            @pl.when(turn == k)
            def _(k=k):
                if len(block) == 4:
                    for c in range(block[1]):
                        out_ref[0, c] = refs[k][:used, c * block[3] : (c + 1) * block[3]].astype(F32)
                else:
                    out_ref[0] = refs[k][:used, :].astype(F32)

    def source(k):
        def at_step(turn, i, s_ref):
            return (jnp.where(turn == k, i, jnp.where(turn < k, 0, steps - 1)), at)

        return pl.BlockSpec((rows, cols), at_step)

    def target(turn, i, s_ref):
        return index(layer, s_ref[turn], i, steps)

    free = pl.BlockSpec(memory_space=pltpu.HBM)
    more = [] if total is None else [total]
    with jax.named_scope(name):
        total, run.token = pl.pallas_call(
            body,
            out_shape=[
                jax.ShapeDtypeStruct(shape, F32),
                pltpu.HBM(run.token.shape, F32),
            ],
            grid_spec=pltpu.PrefetchScalarGridSpec(
                num_scalar_prefetch=1,
                grid=(count, steps),
                in_specs=[source(k) for k in range(count)] + [free] * (1 + len(more)),
                out_specs=[pl.BlockSpec(block, target), free],
            ),
            input_output_aliases={2 + count: 0} if more else {},
            cost_estimate=takes(3),
            compiler_params=pltpu.CompilerParams(vmem_limit_bytes=20 * 2**20),
        )(slots, *pieces, pltpu.with_memory_space_constraint(run.token, pltpu.HBM), *more)
    return total


def plus(a, b):
    return (a.astype(F32) + b.astype(F32)).astype(BF16)


def split_sum(run, spot, keep, came, widths, name):
    half = keep.shape[0] // 2

    def body(p_ref, k_ref, c_ref, *out_refs):
        x = p_ref[1]
        col = 0
        for j, w in enumerate(widths):
            for which, ref in ((1 - x, out_refs[2 * j]), (x, out_refs[2 * j + 1])):
                at = pl.ds(pl.multiple_of(which * half, 16), half)
                ref[...] = plus(k_ref[at, col : col + w], c_ref[at, col : col + w])
            col += w

    outs = [((half, w), BF16) for w in widths for _ in range(2)]
    return run.call(name, body, outs, spot, keep, came, smem=1)


def add_up(run, a, b, name):
    def body(a_ref, b_ref, o_ref):
        o_ref[...] = plus(a_ref[...], b_ref[...])

    return run.call(name, body, [(a.shape, a.dtype)], a, b)[0]


def pick_inner(run, spot, inner, outer, name):
    def body(p_ref, a_ref, b_ref, o_ref):
        z = p_ref[2]
        o_ref[...] = jnp.where((z == 1) | (z == 2), a_ref[...], b_ref[...])

    return run.call(name, body, [(inner.shape, inner.dtype)], spot, inner, outer, smem=1)[0]


def join_halves(run, spot, near, far, name):
    rows, cols = near.shape

    def body(p_ref, near_ref, far_ref, o_ref):
        x = p_ref[1]
        o_ref[pl.ds(pl.multiple_of(x * rows, 16), rows), :] = near_ref[...]
        o_ref[pl.ds(pl.multiple_of((1 - x) * rows, 16), rows), :] = far_ref[...]

    return run.call(name, body, [((2 * rows, cols), BF16)], spot, near, far, smem=1)[0]


def cut_rows(run, value, start, rows, name):
    def body(v_ref, o_ref):
        o_ref[...] = v_ref[start : start + rows, :]

    return run.call(name, body, [((rows, value.shape[1]), value.dtype)], value)[0]


def finish_small(run, own, other, width):
    def body(a_ref, b_ref, gain_ref, shift_ref):
        total = a_ref[...].astype(F32) + b_ref[...].astype(F32)
        for l in range(2):
            for n in range(2):
                row = 4 * l + 2 * n
                gain_ref[l, n : n + 1, :] = total[row : row + 1, :width]
                shift_ref[l, n : n + 1, :] = total[row + 1 : row + 2, :width]

    return run.call("finish_small", body, [((2, 2, width), F32)] * 2, own, other)


def swap_tensor(v):
    return lax.ppermute(v, "tensor", [(0, 1), (1, 0)])


def half_of(v, which, axis):
    size = v.shape[axis] // 2
    return lax.dynamic_slice_in_dim(v, which * size, size, axis)


def joined(own, other, which, axis=0):
    first = which == 0
    return jnp.concatenate(
        [jnp.where(first, own, other), jnp.where(first, other, own)], axis=axis
    )


def pairs(count, step):
    return [(i, i ^ step) for i in range(count)]


def line(moves):
    return [(a * 4 + r, b * 4 + r) for a, b in moves for r in range(4)]


CORE, SIDE = pairs(16, 1), pairs(16, 2)
INWARD, ACROSS, OUTWARD = line([(0, 1), (3, 2)]), line([(1, 2), (2, 1)]), line([(1, 0), (2, 3)])


class Chain:
    def __init__(self, run, spot, away, near, name):
        self.pieces = None
        self.todo = self.steps(run, spot, away, near, name)

    def step(self):
        next(self.todo, None)

    def steps(self, run, spot, away, near, name):
        if near is None:
            self.pieces = away
            return
        came = lax.ppermute(run.gate(away), "dp", SIDE)
        yield
        for move in (INWARD, ACROSS, OUTWARD):
            near = add_up(run, near, came, f"{name}_add")
            came = lax.ppermute(near, "dp", move)
            yield
        near = pick_inner(run, spot, near, came, f"{name}_pick")
        came = lax.ppermute(near, "dp", SIDE)
        yield
        low = join_halves(run, spot, near, came, f"{name}_join")
        self.pieces = [low, lax.ppermute(low, "dp", CORE)]
        yield


class Block:
    def __init__(self, run, spot, n_dp, send, keep, widths, name):
        self.args = (run, spot, keep, widths, name)
        self.whole = None
        if n_dp == 16:
            self.came = lax.ppermute(send, "dp", CORE)
        else:
            whole = lax.psum(joined(keep, send, spot[0]), "dp")
            self.whole = [half_of(whole, spot[0], 0), half_of(whole, 1 - spot[0], 0)]

    def split(self):
        run, spot, keep, widths, name = self.args
        names = [f"{name}_{j}" for j in range(len(widths))]
        if self.whole:
            edges = [sum(widths[:j]) for j in range(len(widths) + 1)]
            parts = [[v[:, a:b] for v in self.whole] for a, b in zip(edges, edges[1:])]
            return [Chain(run, spot, p, None, n) for p, n in zip(parts, names)]
        parts = split_sum(run, spot, keep, self.came, widths, f"{name}_split")
        return [Chain(run, spot, parts[2 * j], parts[2 * j + 1], n) for j, n in enumerate(names)]


def finish_outputs(run, lows, streams, sums):
    count = len(lows)
    rows, width = lows[0].shape

    def body(*refs):
        low, stream, own, other = [refs[i * count : (i + 1) * count] for i in range(4)]
        first_ref, second_ref = refs[4 * count :]
        for r in range(count):
            at = slice(r * rows, (r + 1) * rows)
            first_ref[at, :] = low[r]()[...]
            total = own[r][...].astype(F32) + other[r][...].astype(F32)
            second_ref[at, :] = (stream[r]()[...] + total).astype(BF16)

    return run.call(
        "finish_outputs", body, [((count * rows, width), BF16)] * 2, *[s[0] for s in sums],
        *[s[1] for s in sums], loads=[near(v) for v in (*lows, *streams)], cost=3,
    )


def finish_grad(run, d_mids, ones, normed, spreads, norms):
    count = len(d_mids)
    rows, width = d_mids[0].shape

    def body(*refs):
        x, d_mid, own, other, inverse = [refs[i * count : (i + 1) * count] for i in range(5)]
        g_ref, s_ref, grad_ref = refs[5 * count :]
        for r in range(count):
            unit = unit_of(x[r]()[...], (g_ref, s_ref), 0, 0)
            total = own[r][...].astype(F32) + other[r][...].astype(F32)
            grad = norm_back(total, unit, inverse[r][...], g_ref[0, 0:1, :])
            grad_ref[r * rows : (r + 1) * rows, :] = d_mid[r][...] + grad

    return run.call(
        "finish_grad", body, [((count * rows, width), F32)], *d_mids, *[o[0] for o in ones],
        *[o[1] for o in ones], *spreads, *norms, loads=[near(v) for v in normed], cost=3,
    )[0]


def on_device(parts, n_dp, tokens, w_qkv, w_out, w_up, w_down, norm_gain, norm_shift, d_out):
    length, width = tokens.shape
    size = length // parts
    rows = range(parts)
    cuts = [slice(r * size, (r + 1) * size) for r in rows]
    w_qkv = jnp.transpose(w_qkv, (0, 2, 1, 3))
    part = w_qkv.shape[3]
    hid = w_up.shape[2]
    index = lax.axis_index("dp")
    side = lax.axis_index("tensor")
    spot = jnp.stack([index % 2, index // 2 % 2, index // 4, side]).astype(jnp.int32)
    spot = jnp.concatenate([spot, 1 - spot[:1]])
    slots = jnp.stack([spot[0], spot[4]])
    run = Order()
    norms = (norm_gain, norm_shift)
    quarters = [half_of(w, spot[0], 0) for w in w_out]
    lacking = [(swap_tensor(quarters[0]),), None]

    inputs, lows, blocks, normed_one, attended, exchanged, mlp, sums, spreads = ([{}, {}] for _ in range(9))

    def attention(l, r):
        stream = load_rows(tokens, r * size, size) if l == 0 else near(mlp[l - 1][r][0])
        inputs[l][r], lows[l][r], normed_one[l][r], blocks[l][r], attended[l][r], spreads[l][r] = attention_part(
            run, l, size, spot, stream, sums[l - 1][r] if l else (), norms, w_qkv,
            [blocks[l][q] for q in range(r)], l == 0, f"attention_{l}_{r}",
        )
        exchanged[l][r] = swap_tensor(attended[l][r])

    def fetch_w_out(l):
        lacking[l] = (swap_tensor(run.gate(quarters[l])),)

    def share_w_out(l):
        quarter = run.gate(lacking[l][0])
        lacking[l] = (quarter, lax.ppermute(quarter, "dp", pairs(n_dp, 1)))

    def feed_forward(l, r):
        mlp[l][r] = mlp_part(
            run, l, size, spot, inputs[l][r], attended[l][r], exchanged[l][r], w_out, lacking[l], norms,
            w_up, w_down, f"mlp_{l}_{r}",
        )
        sums[l][r] = (mlp[l][r][4], swap_tensor(mlp[l][r][4])) if l == 0 else None

    def last_sums():
        for r in rows:
            own = run.gate(mlp[1][r][4])
            sums[1][r] = (own, swap_tensor(own))

    back, two, d_mid, mid_low, d_qkv, one, small, carried = ([{}, {}] for _ in range(8))

    def feed_back(l, r):
        upper = (near(normed_one[l + 1][r]), *one[l + 1][r], spreads[l + 1][r], *norms) if l == 0 else ()
        d_in = d_mid[l + 1][r] if l == 0 else load_rows(d_out, r * size, size)
        back[l][r] = mlp_back(run, l, size, d_in, upper, mlp[l][r][3], w_up, w_down, f"mlp_back_{l}_{r}")
        two[l][r] = (back[l][r][3], swap_tensor(back[l][r][3]))
        if l:
            back[l][r][0] = d_in
            back[l][r][1] = d_out[cuts[r]]

    def attend_back(l, r):
        d_mid[l][r], mid_low[l][r], d_qkv[l][r], own, small[l][r], carried[l][r] = attention_back(
            run, l, back[l][r][0], two[l][r], mlp[l][r][1], mlp[l][r][5], normed_one[l][r], norms, w_out, w_qkv,
            [blocks[l][q] for q in range(r + 1)], carried[l].get(r + 1, ()), l == 0,
            f"attention_back_{l}_{r}",
        )
        one[l][r] = (own, swap_tensor(own)) if l else own

    def last_ones():
        for r in rows:
            own = run.gate(one[0][r])
            one[0][r] = (own, swap_tensor(own))

    def every(table):
        return [table[r] for r in rows]

    def mlp_grads(l):
        down = ([m[2] for m in every(mlp[l])], [b[1] for b in every(back[l])], 0)
        up = ([m[1] for m in every(mlp[l])], [b[2] for b in every(back[l])], 1)
        halves = weight_grads(run, spot, [down, up], f"mlp_grads_{l}")
        return Block(run, spot, n_dp, *halves, [width, width], f"mlp_{l}")

    def attention_grads(l):
        job = [(every(normed_one[l]), [d[c] for d in every(d_qkv[l])], 0) for c in range(3)]
        job.append((every(attended[l]), every(mid_low[l]), 1))
        sums_small = every(small[0]) + every(small[1]) if l == 0 else ()
        halves = weight_grads(run, spot, job, f"attention_grads_{l}", sums_small)
        return Block(run, spot, n_dp, *halves, [2 * width], f"att_{l}")

    half = width // 2
    quarter = width // 4

    def place_down(chain, l, total):
        return place_pieces(
            run, chain.pieces, slots, total, (2, hid, width), (1, half, width),
            lambda l, s, i, n: (l, s * n + i, 0), l, 2, f"place_down_{l}",
        )

    def place_up(chain, l, total):
        return place_pieces(
            run, chain.pieces, slots, total, (2, width, hid), (1, half, width),
            lambda l, s, i, n: (l, i, s), l, 2, f"place_up_{l}",
        )

    def place_qkv(chain, l, total):
        return place_pieces(
            run, chain.pieces, slots, total, (2, 3, width, part), (1, 3, quarter, part),
            lambda l, s, i, n: (l, 0, s * n + i, 0), l, 2, f"place_qkv_{l}", 3 * part, 0, quarter,
        )

    def place_out(chain, l, total):
        return place_pieces(
            run, chain.pieces, slots, total, (2, part, width), (1, quarter, half),
            lambda l, s, i, n: (l, i, s), l, 2, f"place_out_{l}", half, 3, quarter,
        )

    order = list(reversed(rows))
    for r in rows:
        attention(0, r)
    share_w_out(0)
    fetch_w_out(1)
    feed_forward(0, 0)
    share_w_out(1)
    for r in rows[1:]:
        feed_forward(0, r)
    for r in rows:
        attention(1, r)
    for r in rows:
        feed_forward(1, r)
    for r in order:
        feed_back(1, r)
    m1 = mlp_grads(1)
    attend_back(1, 1)
    d1, u1 = m1.split()
    d1.step()
    attend_back(1, 0)
    u1.step()
    a1 = attention_grads(1)
    feed_back(0, 1)
    d1.step()
    (a1,) = a1.split()
    feed_back(0, 0)
    m0 = mlp_grads(0)
    attend_back(0, 1)
    u1.step()
    a1.step()
    d1.step()
    d0, u0 = m0.split()
    d0.step()
    attend_back(0, 0)
    a0 = attention_grads(0)
    d1.step()
    a1.step()
    (a0,) = a0.split()
    u1.step()
    last_ones()
    d0.step()
    d1.step()
    a1.step()
    u1.step()
    input_grad = finish_grad(
        run, every(d_mid[0]), every(one[0]), every(normed_one[0]), every(spreads[0]), norms
    )
    u0.step()
    d0.step()
    d1.step()
    u1.step()
    a1.step()
    u0.step()
    g_down = place_down(d1, 1, None)
    a0.step()
    d0.step()
    u1.step()
    a1.step()
    u0.step()
    a0.step()
    g_up = place_up(u1, 1, None)
    last_sums()
    d0.step()
    a1.step()
    u0.step()
    a0.step()
    g_qkv = place_qkv(a1, 1, None)
    g_out = place_out(a1, 1, None)
    first, second = finish_outputs(run, every(lows[1]), [m[0] for m in every(mlp[1])], every(sums[1]))
    d0.step()
    u0.step()
    a0.step()
    g_down = place_down(d0, 0, g_down)
    u0.step()
    a0.step()
    g_up = place_up(u0, 0, g_up)
    a0.step()
    tiny = cut_rows(run, a0.pieces[0], quarter, 16, "small_rows")
    tiny = (tiny, swap_tensor(tiny))
    g_qkv = place_qkv(a0, 0, g_qkv)
    g_out = place_out(a0, 0, g_out)
    g_gain, g_shift = finish_small(run, *tiny, width)
    return (
        first,
        second,
        input_grad,
        jnp.transpose(g_qkv, (0, 2, 1, 3)),
        g_out,
        g_up,
        g_down,
        g_gain,
        g_shift,
    )


def solution(mesh):
    n_dp = mesh.shape["dp"]
    in_specs = (
        P("dp", None),
        P(None, None, None, "tensor"),
        P(None, "tensor", None),
        P(None, None, "tensor"),
        P(None, "tensor", None),
        P(),
        P(),
        P("dp", None),
    )
    out_specs = (
        P("dp", None),
        P("dp", None),
        P("dp", None),
        P(None, None, None, "tensor"),
        P(None, "tensor", None),
        P(None, None, "tensor"),
        P(None, "tensor", None),
        P(),
        P(),
    )

    def body(*args):
        return on_device(2, n_dp, *args)

    return jax.shard_map(body, mesh=mesh, in_specs=in_specs, out_specs=out_specs, check_vma=False)
```

```python
import functools

import jax
import jax.numpy as jnp
from jax import lax
from jax.experimental import pallas as pl
from jax.experimental.pallas import tpu as pltpu
from jax.sharding import PartitionSpec as P

HEAD_DIM = 64
SOFTNESS = 0.25
EPSILON = 1e-05
F32 = jnp.float32
BF16 = jnp.bfloat16
SCALE = HEAD_DIM**-0.5


def mm(a, b, dims):
    return lax.dot_general(a, b, (dims, ((), ())), preferred_element_type=F32)


def nn(a, b):
    return mm(a, b, ((1,), (0,)))


def nt(a, b):
    return mm(a, b, ((1,), (1,)))


def tn(a, b):
    return mm(a, b, ((0,), (0,)))


def normalise(rows_in):
    row_mean = jnp.mean(rows_in, axis=-1, keepdims=True)
    centered = rows_in - row_mean
    spread = jnp.mean(centered * centered, axis=-1, keepdims=True)
    inverse = lax.rsqrt(spread + EPSILON)
    return centered * inverse, inverse


def norm_back(d_normed, unit, inverse, gain):
    scaled = d_normed * gain
    mean_one = jnp.mean(scaled, axis=-1, keepdims=True)
    mean_two = jnp.mean(scaled * unit, axis=-1, keepdims=True)
    return inverse * (scaled - mean_one - unit * mean_two)


def gelu_both(u):
    rate = 0.7978845608028654
    squared = u * u
    bend = jnp.tanh(rate * u * (1.0 + 0.044715 * squared))
    half = 0.5 * (1.0 + bend)
    slope = half + 0.5 * u * (1.0 - bend * bend) * (rate + (rate * 3 * 0.044715) * squared)
    return u * half, slope


def exponents(q, k, signed):
    scores = nt(q, k) * SCALE
    start = k.shape[0] - q.shape[0]
    rows = start + lax.broadcasted_iota(jnp.int32, scores.shape, 0)
    cols = lax.broadcasted_iota(jnp.int32, scores.shape, 1)
    if signed:
        soft = scores * scores + SOFTNESS * SOFTNESS
        inv_mag = lax.rsqrt(soft)
        magnitude = soft * inv_mag
    else:
        inv_mag, magnitude = None, scores
    masked = jnp.where(cols <= rows, magnitude, -1e30)
    exponent = jnp.exp(masked - jnp.max(masked, axis=-1, keepdims=True))
    return scores, inv_mag, exponent, 1.0 / jnp.sum(exponent, axis=-1, keepdims=True)


def head_forward(q, k, v, signed):
    scores, inv_mag, exponent, inv_sum = exponents(q, k, signed)
    if signed:
        exponent = exponent * (scores * inv_mag)
    return (nn(exponent.astype(BF16), v) * inv_sum).astype(BF16)


def head_backward(q, k, v, d_att, signed):
    scores, inv_mag, exponent, inv_sum = exponents(q, k, signed)
    part = exponent * inv_sum
    d_probs = nt(d_att, v)
    if signed:
        sign = scores * inv_mag
        weights = part * sign
        delta = jnp.sum(weights * d_probs, axis=-1, keepdims=True)
        bend = sign * sign + (SOFTNESS * SOFTNESS) * (inv_mag * inv_mag * inv_mag)
        d_scores = part * (d_probs * bend - sign * delta)
    else:
        weights = part
        delta = jnp.sum(weights * d_probs, axis=-1, keepdims=True)
        d_scores = weights * (d_probs - delta)
    low = d_scores.astype(BF16)
    return nn(low, k) * SCALE, tn(low, q) * SCALE, tn(weights.astype(BF16), d_att)


def head_cuts(width):
    return [slice(h * HEAD_DIM, (h + 1) * HEAD_DIM) for h in range(width // HEAD_DIM)]


class Kept:
    def __init__(self, ref, target, sem):
        self.ref = ref
        self.copy = pltpu.make_async_copy(ref, target, sem)


def store(out, value):
    if isinstance(out, Kept):
        out.ref[...] = value
        out.copy.start()
        return out.ref
    out[...] = value
    return out


def near(array, at=None):
    return (None, at, array)


def load_rows(array, start, rows):
    return near(array, pl.ds(start, rows))


def unit_of(normed, norms, layer, which):
    gain, shift = [ref[layer, which : which + 1, :] for ref in norms]
    return (normed.astype(F32) - shift) * (1.0 / gain)


def takes(microseconds):
    return pl.CostEstimate(flops=int(microseconds * 0e9) + 1, bytes_accessed=2**16, transcendentals=0)


class Order:
    def __init__(self):
        self.token = jnp.zeros((8, 128), F32)

    @staticmethod
    def with_layers(body, loads, args, smem):
        count, placed = len(args), [v for v in loads if v[0] is None]
        copied = len(loads) - len(placed)

        def full(*refs):
            getters = iter(refs[:copied])
            ins = refs[copied : copied + count]
            extra = iter(refs[copied + count : copied + count + len(placed)])
            given = []
            for v in loads:
                if v[0] is None:
                    given.append(lambda ref=next(extra), at=v[1]: ref if at is None else ref.at[at])
                else:
                    given.append(next(getters))
            body(*given, *ins, *refs[copied + count + len(placed) :])

        return full

    def call(self, name, body, outs, *args, smem=0, loads=(), cost=1):
        whole = pl.BlockSpec(memory_space=pltpu.VMEM)
        far = pl.BlockSpec(memory_space=pltpu.HBM)
        placed = [v for v in loads if v[0] is None]
        body, args = self.with_layers(body, loads, args, smem), [*args, *[v[2] for v in placed]]
        loads = [v for v in loads if v[0] is not None]
        sources = [piece[0] for _, _, pieces in loads for piece in pieces]
        kept = [len(out) > 2 for out in outs]
        count, extra = len(args), len(sources)

        def inner(*refs):
            ins, given = refs[:count], refs[count : count + extra]
            at = count + extra + 1
            results = list(refs[at : at + len(outs)])
            at += len(outs) + 1
            buffers = refs[at : at + len(loads)]
            at += len(loads)
            getters, used = [], 0
            for buffer, (_, _, pieces) in zip(buffers, loads):
                copies = []
                for _, place, rows, first in pieces:
                    source = given[used] if place is None else given[used].at[place]
                    target = buffer
                    if rows is not None:
                        start = pl.multiple_of(first(*ins[:smem]), 16)
                        target = buffer.at[pl.ds(start, rows), :]
                    copies.append(pltpu.make_async_copy(source, target, refs[-1].at[used]))
                    copies[-1].start()
                    used += 1

                def get(buffer=buffer, copies=copies):
                    for copy in copies:
                        copy.wait()
                    return buffer

                getters.append(get)
            out_copies = []
            for k, out in enumerate(outs):
                if kept[k]:
                    results[k] = Kept(refs[at], results[k], refs[-1].at[used])
                    out_copies.append(results[k].copy)
                    at += 1
                    used += 1
            body(*getters, *ins, *results)
            for copy in out_copies:
                copy.wait()

        scratch = [pltpu.VMEM(shape, dtype) for shape, dtype, _ in loads]
        scratch += [pltpu.VMEM(out[0], out[1]) for out in outs if len(out) > 2]
        if scratch:
            scratch.append(pltpu.SemaphoreType.DMA((extra + sum(kept),)))
        with jax.named_scope(name):
            *res, self.token = pl.pallas_call(
                inner,
                out_shape=[
                    pltpu.HBM(out[0], out[1]) if keep else jax.ShapeDtypeStruct(out[0], out[1])
                    for out, keep in zip(outs, kept)
                ]
                + [pltpu.HBM(self.token.shape, F32)],
                in_specs=[pl.BlockSpec(memory_space=pltpu.SMEM)] * smem
                + [whole] * (count - smem)
                + [far] * (extra + 1),
                out_specs=[far if keep else whole for keep in kept] + [far],
                scratch_shapes=scratch,
                compiler_params=pltpu.CompilerParams(vmem_limit_bytes=24 * 2**20),
                cost_estimate=takes(cost),
            )(*args, *[pltpu.with_memory_space_constraint(v, pltpu.HBM) for v in (*sources, self.token)])
        return res

    def gate(self, value):
        value, self.token = lax.optimization_barrier((value, self.token))
        return value


def attention_part(run, layer, rows, spot, stream, sums, norms, w_qkv, earlier, signed, name):
    width, part = w_qkv.shape[2], w_qkv.shape[3]
    count = len(earlier)

    def body(*refs):
        refs = list(refs)
        x_get, w_get = refs[:2]
        olds = refs[2 : 2 + 2 * count]
        refs = refs[3 + 2 * count :]
        x = x_get()[...].astype(F32)
        if sums:
            x = x + (refs.pop(0)[...].astype(F32) + refs.pop(0)[...].astype(F32))
        g_ref, s_ref = refs.pop(0), refs.pop(0)
        if sums:
            store(refs.pop(0), x)
            store(refs.pop(0), x.astype(BF16))
        n_out, q_out, k_out, v_out, a_ref, i_ref = refs
        unit, inverse = normalise(x)
        store(i_ref, inverse)
        normed = (unit * g_ref[layer, 0:1, :] + s_ref[layer, 0:1, :]).astype(BF16)
        store(n_out, normed)
        w_ref = w_get()
        q_ref, k_ref, v_ref = [
            store(out, nn(normed, w_ref[c]).astype(BF16)) for c, out in enumerate((q_out, k_out, v_out))
        ]
        olds = [get() for get in olds]
        heads = []
        for cut in head_cuts(part):
            k = jnp.concatenate([o[:, cut] for o in olds[:count]] + [k_ref[:, cut]], axis=0)
            v = jnp.concatenate([o[:, cut] for o in olds[count:]] + [v_ref[:, cut]], axis=0)
            heads.append(head_forward(q_ref[:, cut], k, v, signed))
        store(a_ref, jnp.concatenate(heads, axis=1))

    outs = [((rows, width), BF16)] + [((rows, part), BF16)] * 4 + [((rows, 1), F32)]
    if sums:
        outs = [((rows, width), F32), ((rows, width), BF16, True)] + outs
    olds = [near(b[1]) for b in earlier] + [near(b[2]) for b in earlier]
    res = run.call(
        name, body, outs, spot, *sums, *norms, smem=1, loads=[stream, near(w_qkv, layer)] + olds, cost=4
    )
    low = None
    if sums:
        stream, low = near(res[0]), res[1]
        res = res[2:]
    return stream, low, res[0], tuple(res[1:4]), res[4], res[5]


def mlp_part(run, layer, rows, spot, stream, att_own, att_other, w_out, lacking, norms, w_up, w_down, name):
    width, hid = w_up.shape[1], w_up.shape[2]
    half = w_out.shape[1]
    quarter = half // 2
    w_pieces = [
        (w_out, layer, half, lambda t: t[3] * half),
        (lacking[0], None, quarter, lambda t: (1 - t[3]) * half + t[0] * quarter),
        (lacking[1], None, quarter, lambda t: (1 - t[3]) * half + (1 - t[0]) * quarter),
    ]

    def body(wo_get, x_get, u_get, d_get, t_ref, own_ref, oth_ref, g_ref, s_ref, m_out, n_out, h_out, b_out, p_ref, i_ref):
        first = t_ref[3] == 0
        own, other = own_ref[...], oth_ref[...]
        att = jnp.concatenate([jnp.where(first, own, other), jnp.where(first, other, own)], axis=1)
        wo_ref = wo_get()
        middle = x_get()[...].astype(F32) + nn(att, wo_ref[...])
        store(m_out, middle)
        unit, inverse = normalise(middle)
        store(i_ref, inverse)
        normed = (unit * g_ref[layer, 1:2, :] + s_ref[layer, 1:2, :]).astype(BF16)
        store(n_out, normed)
        value, slope = gelu_both(nn(normed, u_get()[...]))
        hidden = value.astype(BF16)
        store(h_out, hidden)
        store(b_out, slope.astype(BF16))
        store(p_ref, nn(hidden, d_get()[...]).astype(BF16))

    outs = [
        ((rows, width), F32),
        ((rows, width), BF16),
        ((rows, hid), BF16),
        ((rows, hid), BF16),
        ((rows, width), BF16),
        ((rows, 1), F32),
    ]
    return run.call(
        name, body, outs, spot, att_own, att_other, *norms, smem=1,
        loads=[((2 * half, width), BF16, w_pieces), stream, near(w_up, layer), near(w_down, layer)],
        cost=4,
    )


def mlp_back(run, layer, rows, d_in, upper, slope, w_up, w_down, name):
    width, hid = w_up.shape[1], w_up.shape[2]

    def body(*refs):
        refs = list(refs)
        w_get, slope_get, u_get, x_get = refs[:4]
        if upper:
            d_ref, own_ref, oth_ref, i_ref, g_ref, s_ref, next_ref, low_ref, pre_ref, p_ref = refs[4:]
            unit = unit_of(x_get()[...], (g_ref, s_ref), layer + 1, 0)
            inverse = i_ref[...]
            total = own_ref[...].astype(F32) + oth_ref[...].astype(F32)
            d_next = d_ref[...] + norm_back(total, unit, inverse, g_ref[layer + 1, 0:1, :])
            store(next_ref, d_next)
            low = d_next.astype(BF16)
            store(low_ref, low)
        else:
            pre_ref, p_ref = refs[4:]
            low = x_get()[...]
        d_pre = (nt(low, w_get()[...]) * slope_get()[...].astype(F32)).astype(BF16)
        store(pre_ref, d_pre)
        store(p_ref, nt(d_pre, u_get()[...]).astype(BF16))

    outs = [((rows, hid), BF16), ((rows, width), BF16)]
    loads = [near(w_down, layer), near(slope), near(w_up, layer)]
    if upper:
        outs = [((rows, width), F32), ((rows, width), BF16)] + outs
        return run.call(name, body, outs, d_in, *upper[1:], loads=loads + [upper[0]], cost=3)
    res = run.call(name, body, outs, loads=loads + [d_in], cost=3)
    return [None, None, *res]


def attention_back(
    run, layer, d_next, two, normed_two, inverse_two, normed_one, norms, w_out, w_qkv, blocks, carried, signed, name
):
    rows, width = normed_two.shape
    part = w_qkv.shape[3]
    count = len(blocks)
    before = (count - 1) * rows
    has = len(carried)
    late = isinstance(d_next, tuple)

    def body(*refs):
        m_get, wo_get, q_get = refs[:3]
        kv_gets = refs[3 : 3 + 2 * count]
        w_get, x_get = refs[3 + 2 * count : 5 + 2 * count]
        refs = list(refs[5 + 2 * count :])
        dn_get = refs.pop(0) if late else None
        dn_ref = None if late else refs.pop(0)
        own_ref, oth_ref, i_ref, g_ref, s_ref = refs[:5]
        refs = refs[5:]
        c_refs = refs[:has]
        mid_ref, low_ref, dq_ref, dk_ref, dv_ref, p_ref, small_ref = refs[has : 7 + has]
        out_carried = refs[7 + has :]
        unit = unit_of(m_get()[...], (g_ref, s_ref), layer, 1)
        inverse = i_ref[...]
        own = own_ref[...].astype(F32)
        small_ref[2:3, :] = jnp.sum(own * unit, axis=0, keepdims=True)
        small_ref[3:4, :] = jnp.sum(own, axis=0, keepdims=True)
        total = own + oth_ref[...].astype(F32)
        if late:
            dn_ref = dn_get()
        d_mid = dn_ref[...].astype(F32) + norm_back(total, unit, inverse, g_ref[layer, 1:2, :])
        store(mid_ref, d_mid)
        low = d_mid.astype(BF16)
        store(low_ref, low)
        d_att = nt(low, wo_get()[...]).astype(BF16)
        q_ref = q_get()
        kv_refs = [get() for get in kv_gets]
        grads = []
        for cut in head_cuts(part):
            k = jnp.concatenate([r[:, cut] for r in kv_refs[:count]], axis=0)
            v = jnp.concatenate([r[:, cut] for r in kv_refs[count:]], axis=0)
            grads.append(head_backward(q_ref[:, cut], k, v, d_att[:, cut], signed))
        d_q, d_k, d_v = [jnp.concatenate(g, axis=1) for g in zip(*grads)]
        if has:
            d_k, d_v = d_k + c_refs[0][...], d_v + c_refs[1][...]
        if before:
            out_carried[0][...] = d_k[:before]
            out_carried[1][...] = d_v[:before]
        d_q, d_k, d_v = d_q.astype(BF16), d_k[before:].astype(BF16), d_v[before:].astype(BF16)
        dq_ref[...] = d_q
        dk_ref[...] = d_k
        dv_ref[...] = d_v
        w_ref = w_get()
        partial = (nt(d_q, w_ref[0]) + nt(d_k, w_ref[1]) + nt(d_v, w_ref[2])).astype(BF16)
        p_ref[...] = partial
        unit = unit_of(x_get()[...], (g_ref, s_ref), layer, 0)
        own = partial.astype(F32)
        small_ref[0:1, :] = jnp.sum(own * unit, axis=0, keepdims=True)
        small_ref[1:2, :] = jnp.sum(own, axis=0, keepdims=True)

    outs = [((rows, width), F32), ((rows, width), BF16)] + [((rows, part), BF16)] * 3
    outs += [((rows, width), BF16), ((4, width), F32)]
    if before:
        outs += [((before, part), F32)] * 2
    loads = [near(normed_two), near(w_out, layer), near(blocks[-1][0])]
    loads += [near(b[1]) for b in blocks] + [near(b[2]) for b in blocks]
    loads += [near(w_qkv, layer), near(normed_one)]
    args = [*two, inverse_two, *norms, *carried]
    if late:
        loads.append(d_next)
    else:
        args = [d_next] + args
    res = run.call(name, body, outs, *args, loads=loads, cost=8)
    return res[0], res[1], tuple(res[2:5]), res[5], res[6], tuple(res[7:])


def weight_grads(run, spot, job, name, small=()):
    flat, steps, height, width = [], [], None, 0
    for left, right, halved in job:
        cols = [b[0].shape[1] for b in (left, right)]
        cols[halved] //= 2
        steps.append((len(flat), len(left), cols, halved, width))
        flat += list(left) + list(right)
        height = cols[0]
        width += cols[1]
    count = len(flat)
    extra = 16 if small else 0
    half = height // 2

    def body(c_ref, *refs):
        core_here = c_ref[0]
        for which, out_ref in zip((1 - core_here, core_here), refs[count + 4 * bool(small) :]):
            for at, blocks, cols, halved, col in steps:
                sides = []
                for side in range(2):
                    group = refs[at + side * blocks : at + (side + 1) * blocks]
                    if side == halved:
                        start = pl.multiple_of(which * cols[side], 128)
                        group = [r[:, pl.ds(start, cols[side])] for r in group]
                    else:
                        group = [r[...] for r in group]
                    sides.append(jnp.concatenate(group, axis=0))
                value = tn(*sides).astype(BF16)
                out_ref[:half, col : col + cols[1]] = value[:half]
                out_ref[half + extra : 2 * half + extra, col : col + cols[1]] = value[half:]
            if extra:
                sums = [r[...] for r in refs[count : count + 4]]
                sums = jnp.concatenate([sums[0] + sums[1], sums[2] + sums[3]], axis=0)
                wide = sums.shape[1]
                rest = jnp.zeros((8, wide), F32)
                sums = jnp.concatenate([sums, rest], axis=0).astype(BF16)
                for h in range(2):
                    at = (h + 1) * half + h * extra
                    out_ref[at : at + extra, :wide] = sums
                    out_ref[at : at + extra, wide:] = jnp.zeros((extra, width - wide), BF16)

    outs = [((height + 2 * extra, width), BF16)] * 2
    return run.call(name, body, outs, spot, *flat, *small, smem=1, cost=3)


def place_pieces(run, pieces, slots, totals, shapes, jobs, name):
    count, many = len(pieces), len(shapes)
    more = [t for t in totals if t is not None]
    first = 1 + count + 1
    cells = [(j, k) for k in range(count) for j in range(len(jobs))]

    def body(s_ref, *refs):
        outs = refs[count + 1 + len(more) : count + 1 + len(more) + many]
        buffers, sem = refs[-1 - len(cells) : -1], refs[-1]
        copies = []
        for n, (j, k) in enumerate(cells):
            which, place, rows, cols = jobs[j]
            buffers[n][...] = refs[k][rows, cols].astype(F32)
            copies.append(pltpu.make_async_copy(buffers[n], outs[which].at[place(s_ref[k])], sem.at[n]))
            copies[-1].start()
        for copy in copies:
            copy.wait()

    def sized(j):
        return tuple(v.stop - v.start for v in jobs[j][2:])

    far = pl.BlockSpec(memory_space=pltpu.HBM)
    with jax.named_scope(name):
        *res, run.token = pl.pallas_call(
            body,
            out_shape=[pltpu.HBM(shape, F32) for shape in shapes] + [pltpu.HBM(run.token.shape, F32)],
            in_specs=[pl.BlockSpec(memory_space=pltpu.SMEM)]
            + [pl.BlockSpec(memory_space=pltpu.VMEM)] * count
            + [far] * (1 + len(more)),
            out_specs=[far] * (many + 1),
            scratch_shapes=[pltpu.VMEM(sized(j), F32) for j, _ in cells] + [pltpu.SemaphoreType.DMA((len(cells),))],
            input_output_aliases={first + n: n for n in range(len(more))},
            cost_estimate=takes(3),
            compiler_params=pltpu.CompilerParams(vmem_limit_bytes=24 * 2**20),
        )(slots, *pieces, *[pltpu.with_memory_space_constraint(v, pltpu.HBM) for v in (run.token, *more)])
    return res


def plus(a, b):
    return (a.astype(F32) + b.astype(F32)).astype(BF16)


def split_sum(run, spot, keep, came, widths, name):
    half = keep.shape[0] // 2

    def body(p_ref, k_ref, c_ref, *out_refs):
        x = p_ref[1]
        col = 0
        for j, w in enumerate(widths):
            for which, ref in ((1 - x, out_refs[2 * j]), (x, out_refs[2 * j + 1])):
                at = pl.ds(pl.multiple_of(which * half, 16), half)
                ref[...] = plus(k_ref[at, col : col + w], c_ref[at, col : col + w])
            col += w

    outs = [((half, w), BF16) for w in widths for _ in range(2)]
    return run.call(name, body, outs, spot, keep, came, smem=1)


def add_up(run, a, b, name):
    def body(a_ref, b_ref, o_ref):
        o_ref[...] = plus(a_ref[...], b_ref[...])

    return run.call(name, body, [(a.shape, a.dtype)], a, b)[0]


def pick_inner(run, spot, inner, outer, name):
    def body(p_ref, a_ref, b_ref, o_ref):
        z = p_ref[2]
        o_ref[...] = jnp.where((z == 1) | (z == 2), a_ref[...], b_ref[...])

    return run.call(name, body, [(inner.shape, inner.dtype)], spot, inner, outer, smem=1)[0]


def join_halves(run, spot, near, far, name):
    rows, cols = near.shape

    def body(p_ref, near_ref, far_ref, o_ref):
        x = p_ref[1]
        o_ref[pl.ds(pl.multiple_of(x * rows, 16), rows), :] = near_ref[...]
        o_ref[pl.ds(pl.multiple_of((1 - x) * rows, 16), rows), :] = far_ref[...]

    return run.call(name, body, [((2 * rows, cols), BF16)], spot, near, far, smem=1)[0]


def cut_rows(run, value, start, rows, name):
    def body(v_ref, o_ref):
        o_ref[...] = v_ref[start : start + rows, :]

    return run.call(name, body, [((rows, value.shape[1]), value.dtype)], value)[0]


def finish_small(run, own, other, width):
    def body(a_ref, b_ref, gain_ref, shift_ref):
        total = a_ref[...].astype(F32) + b_ref[...].astype(F32)
        for l in range(2):
            for n in range(2):
                row = 4 * l + 2 * n
                gain_ref[l, n : n + 1, :] = total[row : row + 1, :width]
                shift_ref[l, n : n + 1, :] = total[row + 1 : row + 2, :width]

    return run.call("finish_small", body, [((2, 2, width), F32)] * 2, own, other)


def swap_tensor(v):
    return lax.ppermute(v, "tensor", [(0, 1), (1, 0)])


def half_of(v, which, axis):
    size = v.shape[axis] // 2
    return lax.dynamic_slice_in_dim(v, which * size, size, axis)


def joined(own, other, which, axis=0):
    first = which == 0
    return jnp.concatenate(
        [jnp.where(first, own, other), jnp.where(first, other, own)], axis=axis
    )


def pairs(count, step):
    return [(i, i ^ step) for i in range(count)]


def line(moves):
    return [(a * 4 + r, b * 4 + r) for a, b in moves for r in range(4)]


CORE, SIDE = pairs(16, 1), pairs(16, 2)
INWARD, ACROSS, OUTWARD = line([(0, 1), (3, 2)]), line([(1, 2), (2, 1)]), line([(1, 0), (2, 3)])


class Chain:
    moves = (SIDE, INWARD, ACROSS, OUTWARD, SIDE, CORE)

    def __init__(self, run, spot, away, near, name):
        self.run, self.spot, self.name = run, spot, name
        self.whole = near is None
        self.pieces = away
        self.value, self.near, self.stage = away[0] if self.whole else away, near, 0

    def issue(self):
        if not self.whole:
            self.came = lax.ppermute(self.run.gate(self.value), "dp", self.moves[self.stage])

    def consume(self):
        if self.whole:
            return
        run, spot, stage, came = self.run, self.spot, self.stage, self.came
        if stage < 3:
            self.value = self.near = add_up(run, self.near, came, f"{self.name}_add_{stage}")
        elif stage == 3:
            self.value = self.near = pick_inner(run, spot, self.near, came, f"{self.name}_pick")
        elif stage == 4:
            self.value = join_halves(run, spot, self.near, came, f"{self.name}_join")
        else:
            self.pieces = [self.value, run.gate(came)]
        self.stage += 1


class Block:
    def __init__(self, run, spot, n_dp, send, keep, widths, names):
        self.args = (run, spot, keep, widths, names)
        self.send, self.n_dp = send, n_dp

    def issue(self):
        run, spot, keep = self.args[:3]
        if self.n_dp == 16:
            self.came = lax.ppermute(run.gate(self.send), "dp", CORE)
        else:
            whole = lax.psum(joined(keep, self.send, spot[0]), "dp")
            self.whole = [half_of(whole, spot[0], 0), half_of(whole, 1 - spot[0], 0)]

    def split(self):
        run, spot, keep, widths, names = self.args
        if self.n_dp != 16:
            edges = [sum(widths[:j]) for j in range(len(widths) + 1)]
            parts = [[v[:, a:b] for v in self.whole] for a, b in zip(edges, edges[1:])]
            return [Chain(run, spot, p, None, n) for p, n in zip(parts, names)]
        parts = split_sum(run, spot, keep, self.came, widths, f"{names[0]}_split")
        return [Chain(run, spot, parts[2 * j], parts[2 * j + 1], n) for j, n in enumerate(names)]


def finish_outputs(run, lows, streams, sums):
    count = len(lows)
    rows, width = lows[0].shape

    def body(*refs):
        low, stream, own, other = [refs[i * count : (i + 1) * count] for i in range(4)]
        first_ref, second_ref = refs[4 * count :]
        for r in range(count):
            at = slice(r * rows, (r + 1) * rows)
            first_ref[at, :] = low[r]()[...]
            total = own[r][...].astype(F32) + other[r][...].astype(F32)
            second_ref[at, :] = (stream[r]()[...] + total).astype(BF16)

    return run.call(
        "finish_outputs", body, [((count * rows, width), BF16)] * 2, *[s[0] for s in sums],
        *[s[1] for s in sums], loads=[near(v) for v in (*lows, *streams)], cost=3,
    )


def finish_grad(run, d_mids, ones, normed, spreads, norms):
    count = len(d_mids)
    rows, width = d_mids[0].shape

    def body(*refs):
        x, d_mid, own, other, inverse = [refs[i * count : (i + 1) * count] for i in range(5)]
        g_ref, s_ref, grad_ref = refs[5 * count :]
        for r in range(count):
            unit = unit_of(x[r]()[...], (g_ref, s_ref), 0, 0)
            total = own[r][...].astype(F32) + other[r][...].astype(F32)
            grad = norm_back(total, unit, inverse[r][...], g_ref[0, 0:1, :])
            grad_ref[r * rows : (r + 1) * rows, :] = d_mid[r][...] + grad

    return run.call(
        "finish_grad", body, [((count * rows, width), F32)], *d_mids, *[o[0] for o in ones],
        *[o[1] for o in ones], *spreads, *norms, loads=[near(v) for v in normed], cost=3,
    )[0]


def on_device(parts, n_dp, tokens, w_qkv, w_out, w_up, w_down, norm_gain, norm_shift, d_out):
    length, width = tokens.shape
    size = length // parts
    rows = range(parts)
    cuts = [slice(r * size, (r + 1) * size) for r in rows]
    w_qkv = jnp.transpose(w_qkv, (0, 2, 1, 3))
    part = w_qkv.shape[3]
    hid = w_up.shape[2]
    index = lax.axis_index("dp")
    side = lax.axis_index("tensor")
    spot = jnp.stack([index % 2, index // 2 % 2, index // 4, side]).astype(jnp.int32)
    spot = jnp.concatenate([spot, 1 - spot[:1]])
    slots = jnp.stack([spot[0], spot[4]])
    run = Order()
    norms = (norm_gain, norm_shift)
    quarters = [half_of(w, spot[0], 0) for w in w_out]
    lacking = [(swap_tensor(quarters[0]),), None]

    inputs, lows, blocks, normed_one, attended, exchanged, mlp, sums, spreads = ([{}, {}] for _ in range(9))

    def attention(l, r):
        stream = load_rows(tokens, r * size, size) if l == 0 else near(mlp[l - 1][r][0])
        inputs[l][r], lows[l][r], normed_one[l][r], blocks[l][r], attended[l][r], spreads[l][r] = attention_part(
            run, l, size, spot, stream, sums[l - 1][r] if l else (), norms, w_qkv,
            [blocks[l][q] for q in range(r)], l == 0, f"attention_{l}_{r}",
        )
        exchanged[l][r] = swap_tensor(attended[l][r])

    def fetch_w_out(l):
        lacking[l] = (swap_tensor(run.gate(quarters[l])),)

    def share_w_out(l):
        quarter = run.gate(lacking[l][0])
        lacking[l] = (quarter, lax.ppermute(quarter, "dp", pairs(n_dp, 1)))

    def feed_forward(l, r):
        mlp[l][r] = mlp_part(
            run, l, size, spot, inputs[l][r], attended[l][r], exchanged[l][r], w_out, lacking[l], norms,
            w_up, w_down, f"mlp_{l}_{r}",
        )
        sums[l][r] = (mlp[l][r][4], swap_tensor(mlp[l][r][4])) if l == 0 else (mlp[l][r][4],)

    back, two, d_mid, mid_low, d_qkv, one, small, carried = ([{}, {}] for _ in range(8))

    def feed_back(l, r):
        upper = (near(normed_one[l + 1][r]), *one[l + 1][r], spreads[l + 1][r], *norms) if l == 0 else ()
        d_in = d_mid[l + 1][r] if l == 0 else load_rows(d_out, r * size, size)
        back[l][r] = mlp_back(run, l, size, d_in, upper, mlp[l][r][3], w_up, w_down, f"mlp_back_{l}_{r}")
        two[l][r] = (back[l][r][3],)
        if l:
            back[l][r][0] = d_in
            back[l][r][1] = d_out[cuts[r]]

    def attend_back(l, r):
        d_mid[l][r], mid_low[l][r], d_qkv[l][r], own, small[l][r], carried[l][r] = attention_back(
            run, l, back[l][r][0], two[l][r], mlp[l][r][1], mlp[l][r][5], normed_one[l][r], norms, w_out, w_qkv,
            [blocks[l][q] for q in range(r + 1)], carried[l].get(r + 1, ()), l == 0,
            f"attention_back_{l}_{r}",
        )
        one[l][r] = (own,)

    def exchange(pair):
        own = run.gate(pair[0])
        return (own, swap_tensor(own))

    def arrive(pair):
        return (pair[0], run.gate(pair[1]))

    def every(table):
        return [table[r] for r in rows]

    def mlp_grads(l):
        down = ([m[2] for m in every(mlp[l])], [b[1] for b in every(back[l])], 0)
        up = ([m[1] for m in every(mlp[l])], [b[2] for b in every(back[l])], 1)
        halves = weight_grads(run, spot, [down, up], f"mlp_grads_{l}")
        return Block(run, spot, n_dp, *halves, [width, width], (f"down_{l}", f"up_{l}"))

    def attention_grads(l):
        job = [(every(normed_one[l]), [d[c] for d in every(d_qkv[l])], 0) for c in range(3)]
        job.append((every(attended[l]), every(mid_low[l]), 1))
        sums_small = every(small[0]) + every(small[1]) if l == 0 else ()
        halves = weight_grads(run, spot, job, f"attention_grads_{l}", sums_small)
        return Block(run, spot, n_dp, *halves, [2 * width], (f"att_{l}",))

    half = width // 2
    quarter = width // 4
    shapes = ((2, hid, width), (2, width, hid), (2, 3, width, part), (2, part, width))
    totals = [None] * 4

    def at(start, size, step=16):
        return pl.ds(pl.multiple_of(start, step), size)

    def rows_of(n, extra=0):
        return slice(n * (quarter + extra), n * (quarter + extra) + quarter)

    def place_down(chain, l):
        jobs = [
            (0, lambda s, n=n: (l, at(s * width + n * quarter, quarter)), rows_of(n), slice(0, width))
            for n in range(4)
        ]
        (totals[0],) = place_pieces(run, chain.pieces, slots, totals[:1], shapes[:1], jobs, f"place_down_{l}")

    def place_up(chain, l):
        jobs = [
            (0, lambda s, n=n: (l, pl.ds(n * quarter, quarter), at(s * width, width, 128)), rows_of(n), slice(0, width))
            for n in range(4)
        ]
        (totals[1],) = place_pieces(run, chain.pieces, slots, totals[1:2], shapes[1:2], jobs, f"place_up_{l}")

    def place_att(chain, l):
        extra = 0 if l else 16
        jobs = [
            (0, lambda s, n=n, c=c: (l, c, at(s * half + n * quarter, quarter)), rows_of(n, extra), slice(c * part, c * part + part))
            for n in range(2)
            for c in range(3)
        ]
        jobs += [
            (1, lambda s, n=n: (l, pl.ds(n * quarter, quarter), at(s * half, half, 128)), rows_of(n, extra), slice(3 * part, 3 * part + half))
            for n in range(2)
        ]
        totals[2:] = place_pieces(run, chain.pieces, slots, totals[2:], shapes[2:], jobs, f"place_att_{l}")

    for r in rows:
        attention(0, r)
    share_w_out(0)
    fetch_w_out(1)
    feed_forward(0, 0)
    share_w_out(1)
    for r in rows[1:]:
        feed_forward(0, r)
    for r in rows:
        attention(1, r)
    for r in rows:
        feed_forward(1, r)
    feed_back(1, 1)
    two[1][1] = exchange(two[1][1])
    feed_back(1, 0)
    two[1][0] = exchange(two[1][0])
    m1 = mlp_grads(1)
    m1.issue()
    d1, u1 = m1.split()
    d1.issue()
    u1.issue()
    attend_back(1, 1)
    one[1][1] = exchange(one[1][1])
    attend_back(1, 0)
    one[1][0] = exchange(one[1][0])
    d1.consume()
    d1.issue()
    feed_back(0, 1)
    two[0][1] = exchange(two[0][1])
    u1.consume()
    u1.issue()
    feed_back(0, 0)
    two[0][0] = exchange(two[0][0])
    b1 = attention_grads(1)
    b1.issue()
    m0 = mlp_grads(0)
    m0.issue()
    d1.consume()
    d1.issue()
    attend_back(0, 1)
    one[0][1] = exchange(one[0][1])
    attend_back(0, 0)
    one[0][0] = exchange(one[0][0])
    u1.consume()
    u1.issue()
    b0 = attention_grads(0)
    b0.issue()
    (a0,) = b0.split()
    a0.issue()
    (a1,) = b1.split()
    a1.issue()
    for r in rows:
        sums[1][r] = exchange(sums[1][r])
    first, second = finish_outputs(run, every(lows[1]), [m[0] for m in every(mlp[1])], every(sums[1]))
    a0.consume()
    a0.issue()
    d0, u0 = m0.split()
    d0.issue()
    u0.issue()
    d1.consume()
    d1.issue()
    a1.consume()
    a1.issue()
    a0.consume()
    a0.issue()
    u0.consume()
    u0.issue()
    u1.consume()
    u1.issue()
    d1.consume()
    d1.issue()
    a1.consume()
    a1.issue()
    d0.consume()
    d0.issue()
    a0.consume()
    a0.issue()
    u1.consume()
    u1.issue()
    u0.consume()
    u0.issue()
    d1.consume()
    d1.issue()
    a1.consume()
    a1.issue()
    a0.consume()
    a0.issue()
    d0.consume()
    d0.issue()
    u1.consume()
    u1.issue()
    u0.consume()
    u0.issue()
    a1.consume()
    a1.issue()
    a0.consume()
    a0.issue()
    d0.consume()
    d0.issue()
    tiny = cut_rows(run, a0.value, quarter, 16, "small_rows")
    tiny = (tiny, swap_tensor(tiny))
    u0.consume()
    u0.issue()
    input_grad = finish_grad(
        run, every(d_mid[0]), every(one[0]), every(normed_one[0]), every(spreads[0]), norms
    )
    a1.consume()
    a1.issue()
    d0.consume()
    d0.issue()
    d1.consume()
    place_down(d1, 1)
    u0.consume()
    u0.issue()
    u1.consume()
    place_up(u1, 1)
    u0.consume()
    place_up(u0, 0)
    a1.consume()
    place_att(a1, 1)
    g_gain, g_shift = finish_small(run, *tiny, width)
    d0.consume()
    d0.issue()
    a0.consume()
    place_att(a0, 0)
    d0.consume()
    place_down(d0, 0)
    return (
        first,
        second,
        input_grad,
        jnp.transpose(totals[2], (0, 2, 1, 3)),
        totals[3],
        totals[1],
        totals[0],
        g_gain,
        g_shift,
    )


def solution(mesh):
    n_dp = mesh.shape["dp"]
    in_specs = (
        P("dp", None),
        P(None, None, None, "tensor"),
        P(None, "tensor", None),
        P(None, None, "tensor"),
        P(None, "tensor", None),
        P(),
        P(),
        P("dp", None),
    )
    out_specs = (
        P("dp", None),
        P("dp", None),
        P("dp", None),
        P(None, None, None, "tensor"),
        P(None, "tensor", None),
        P(None, None, "tensor"),
        P(None, "tensor", None),
        P(),
        P(),
    )

    def body(*args):
        return on_device(2, n_dp, *args)

    return jax.shard_map(body, mesh=mesh, in_specs=in_specs, out_specs=out_specs, check_vma=False)
```

```python
import functools

import jax
import jax.numpy as jnp
from jax import lax
from jax.experimental import pallas as pl
from jax.experimental.pallas import tpu as pltpu
from jax.sharding import PartitionSpec as P

HEAD_DIM = 64
SOFTNESS = 0.25
EPSILON = 1e-05
F32 = jnp.float32
BF16 = jnp.bfloat16
SCALE = HEAD_DIM**-0.5
TOKEN = (8, 128)


def mm(a, b, dims):
    return lax.dot_general(a, b, (dims, ((), ())), preferred_element_type=F32)


def nn(a, b):
    return mm(a, b, ((1,), (0,)))


def nt(a, b):
    return mm(a, b, ((1,), (1,)))


def tn(a, b):
    return mm(a, b, ((0,), (0,)))


def normalise(rows_in):
    row_mean = jnp.mean(rows_in, axis=-1, keepdims=True)
    centered = rows_in - row_mean
    spread = jnp.mean(centered * centered, axis=-1, keepdims=True)
    inverse = lax.rsqrt(spread + EPSILON)
    return centered * inverse, inverse


def norm_back(d_normed, unit, inverse, gain):
    scaled = d_normed * gain
    mean_one = jnp.mean(scaled, axis=-1, keepdims=True)
    mean_two = jnp.mean(scaled * unit, axis=-1, keepdims=True)
    return inverse * (scaled - mean_one - unit * mean_two)


def gelu_both(u):
    rate = 0.7978845608028654
    squared = u * u
    bend = jnp.tanh(rate * u * (1.0 + 0.044715 * squared))
    half = 0.5 * (1.0 + bend)
    slope = half + 0.5 * u * (1.0 - bend * bend) * (rate + (rate * 3 * 0.044715) * squared)
    return u * half, slope


def exponents(q, k, signed):
    scores = nt(q, k) * SCALE
    start = k.shape[0] - q.shape[0]
    rows = start + lax.broadcasted_iota(jnp.int32, scores.shape, 0)
    cols = lax.broadcasted_iota(jnp.int32, scores.shape, 1)
    if signed:
        soft = scores * scores + SOFTNESS * SOFTNESS
        inv_mag = lax.rsqrt(soft)
        magnitude = soft * inv_mag
    else:
        inv_mag, magnitude = None, scores
    masked = jnp.where(cols <= rows, magnitude, -1e30)
    exponent = jnp.exp(masked - jnp.max(masked, axis=-1, keepdims=True))
    return scores, inv_mag, exponent, 1.0 / jnp.sum(exponent, axis=-1, keepdims=True)


def head_forward(q, k, v, signed):
    scores, inv_mag, exponent, inv_sum = exponents(q, k, signed)
    if signed:
        exponent = exponent * (scores * inv_mag)
    return (nn(exponent.astype(BF16), v) * inv_sum).astype(BF16)


def head_backward(q, k, v, d_att, signed):
    scores, inv_mag, exponent, inv_sum = exponents(q, k, signed)
    part = exponent * inv_sum
    d_probs = nt(d_att, v)
    if signed:
        sign = scores * inv_mag
        weights = part * sign
        delta = jnp.sum(weights * d_probs, axis=-1, keepdims=True)
        bend = sign * sign + (SOFTNESS * SOFTNESS) * (inv_mag * inv_mag * inv_mag)
        d_scores = part * (d_probs * bend - sign * delta)
    else:
        weights = part
        delta = jnp.sum(weights * d_probs, axis=-1, keepdims=True)
        d_scores = weights * (d_probs - delta)
    low = d_scores.astype(BF16)
    return nn(low, k) * SCALE, tn(low, q) * SCALE, tn(weights.astype(BF16), d_att)


def head_cuts(width):
    return [slice(h * HEAD_DIM, (h + 1) * HEAD_DIM) for h in range(width // HEAD_DIM)]


class Kept:
    def __init__(self, ref, target, sem):
        self.ref = ref
        self.copy = pltpu.make_async_copy(ref, target, sem)


def store(out, value):
    if isinstance(out, Kept):
        out.ref[...] = value
        out.copy.start()
        return out.ref
    out[...] = value
    return out


def near(array, at=None):
    return (None, at, array)


def load_rows(array, start, rows):
    return near(array, pl.ds(start, rows))


def unit_of(normed, norms, layer, which):
    gain, shift = [ref[layer, which : which + 1, :] for ref in norms]
    return (normed.astype(F32) - shift) * (1.0 / gain)


def takes(microseconds):
    return pl.CostEstimate(flops=int(microseconds * 0) + 1, bytes_accessed=2**16, transcendentals=0)


class Order:
    def __init__(self, token):
        self.token = token

    @staticmethod
    def with_layers(body, loads, args, smem):
        count, placed = len(args), [v for v in loads if v[0] is None]
        copied = len(loads) - len(placed)

        def full(*refs):
            getters = iter(refs[:copied])
            ins = refs[copied : copied + count]
            extra = iter(refs[copied + count : copied + count + len(placed)])
            given = []
            for v in loads:
                if v[0] is None:
                    given.append(lambda ref=next(extra), at=v[1]: ref if at is None else ref.at[at])
                else:
                    given.append(next(getters))
            body(*given, *ins, *refs[copied + count + len(placed) :])

        return full

    def call(self, name, body, outs, *args, smem=0, loads=(), cost=1):
        whole = pl.BlockSpec(memory_space=pltpu.VMEM)
        far = pl.BlockSpec(memory_space=pltpu.HBM)
        placed = [v for v in loads if v[0] is None]
        body, args = self.with_layers(body, loads, args, smem), [*args, *[v[2] for v in placed]]
        loads = [v for v in loads if v[0] is not None]
        sources = [piece[0] for _, _, pieces in loads for piece in pieces]
        kept = [len(out) > 2 for out in outs]
        count, extra = len(args), len(sources)

        def inner(*refs):
            ins, given = refs[:count], refs[count : count + extra]
            at = count + extra + 1
            results = list(refs[at : at + len(outs)])
            at += len(outs) + 1
            buffers = refs[at : at + len(loads)]
            at += len(loads)
            getters, used = [], 0
            for buffer, (_, _, pieces) in zip(buffers, loads):
                copies = []
                for _, place, rows, first in pieces:
                    source = given[used] if place is None else given[used].at[place]
                    target = buffer
                    if rows is not None:
                        start = pl.multiple_of(first(*ins[:smem]), 16)
                        target = buffer.at[pl.ds(start, rows), :]
                    copies.append(pltpu.make_async_copy(source, target, refs[-1].at[used]))
                    copies[-1].start()
                    used += 1

                def get(buffer=buffer, copies=copies):
                    for copy in copies:
                        copy.wait()
                    return buffer

                getters.append(get)
            out_copies = []
            for k, out in enumerate(outs):
                if kept[k]:
                    results[k] = Kept(refs[at], results[k], refs[-1].at[used])
                    out_copies.append(results[k].copy)
                    at += 1
                    used += 1
            body(*getters, *ins, *results)
            for copy in out_copies:
                copy.wait()

        scratch = [pltpu.VMEM(shape, dtype) for shape, dtype, _ in loads]
        scratch += [pltpu.VMEM(out[0], out[1]) for out in outs if len(out) > 2]
        if scratch:
            scratch.append(pltpu.SemaphoreType.DMA((max(1, extra + sum(kept)),)))
        with jax.named_scope(name):
            *res, self.token = pl.pallas_call(
                inner,
                out_shape=[
                    pltpu.HBM(out[0], out[1]) if keep else jax.ShapeDtypeStruct(out[0], out[1])
                    for out, keep in zip(outs, kept)
                ]
                + [pltpu.HBM(TOKEN, F32)],
                in_specs=[pl.BlockSpec(memory_space=pltpu.SMEM)] * smem
                + [whole] * (count - smem)
                + [far] * (extra + 1),
                out_specs=[far if keep else whole for keep in kept] + [far],
                scratch_shapes=scratch,
                compiler_params=pltpu.CompilerParams(vmem_limit_bytes=24 * 2**20),
                cost_estimate=takes(cost),
            )(*args, *[pltpu.with_memory_space_constraint(v, pltpu.HBM) for v in (*sources, self.token)])
        return res

    def gate(self, value):
        value, self.token = lax.optimization_barrier((value, self.token))
        return value


def attention_part(run, layer, rows, spot, stream, sums, norms, w_qkv, earlier, signed, name):
    width, part = w_qkv.shape[2], w_qkv.shape[3]
    count = len(earlier)

    def body(*refs):
        refs = list(refs)
        x_get, w_get = refs[:2]
        olds = refs[2 : 2 + 2 * count]
        refs = refs[3 + 2 * count :]
        x = x_get()[...].astype(F32)
        if sums:
            x = x + (refs.pop(0)[...].astype(F32) + refs.pop(0)[...].astype(F32))
        g_ref, s_ref = refs.pop(0), refs.pop(0)
        if sums:
            store(refs.pop(0), x)
            store(refs.pop(0), x.astype(BF16))
        n_out, q_out, k_out, v_out, a_ref, i_ref = refs
        unit, inverse = normalise(x)
        store(i_ref, inverse)
        normed = (unit * g_ref[layer, 0:1, :] + s_ref[layer, 0:1, :]).astype(BF16)
        store(n_out, normed)
        w_ref = w_get()
        q_ref, k_ref, v_ref = [
            store(out, nn(normed, w_ref[c]).astype(BF16)) for c, out in enumerate((q_out, k_out, v_out))
        ]
        olds = [get() for get in olds]
        heads = []
        for cut in head_cuts(part):
            k = jnp.concatenate([o[:, cut] for o in olds[:count]] + [k_ref[:, cut]], axis=0)
            v = jnp.concatenate([o[:, cut] for o in olds[count:]] + [v_ref[:, cut]], axis=0)
            heads.append(head_forward(q_ref[:, cut], k, v, signed))
        store(a_ref, jnp.concatenate(heads, axis=1))

    outs = [((rows, width), BF16)] + [((rows, part), BF16)] * 4 + [((rows, 1), F32)]
    if sums:
        outs = [((rows, width), F32), ((rows, width), BF16, True)] + outs
    olds = [near(b[1]) for b in earlier] + [near(b[2]) for b in earlier]
    res = run.call(
        name, body, outs, spot, *sums, *norms, smem=1, loads=[stream, near(w_qkv, layer)] + olds, cost=4
    )
    low = None
    if sums:
        stream, low = near(res[0]), res[1]
        res = res[2:]
    return stream, low, res[0], tuple(res[1:4]), res[4], res[5]


def mlp_part(run, layer, rows, spot, stream, att_own, att_other, w_out, lacking, norms, w_up, w_down, name):
    width, hid = w_up.shape[1], w_up.shape[2]
    half = w_out.shape[1]
    quarter = half // 2
    def body(wo_get, out_get, one_get, two_get, three_get, x_get, u_get, d_get, *refs):
        t_ref, own_ref, oth_ref, g_ref, s_ref, m_out, n_out, h_out, b_out, p_ref, i_ref = refs
        first = t_ref[3] == 0
        own, other = own_ref[...], oth_ref[...]
        att = jnp.concatenate([jnp.where(first, own, other), jnp.where(first, other, own)], axis=1)
        wo_ref = wo_get()
        core, side = t_ref[0], t_ref[3]
        rest = (1 - side) * half
        for piece, start, size in (
            (out_get, side * half, half),
            (one_get, rest + core * quarter, quarter),
            (two_get, rest + (1 - core) * quarter, quarter // 2),
            (three_get, rest + (1 - core) * quarter + quarter // 2, quarter // 2),
        ):
            wo_ref[pl.ds(pl.multiple_of(start, 16), size), :] = piece()[...]
        middle = x_get()[...].astype(F32) + nn(att, wo_ref[...])
        store(m_out, middle)
        unit, inverse = normalise(middle)
        store(i_ref, inverse)
        normed = (unit * g_ref[layer, 1:2, :] + s_ref[layer, 1:2, :]).astype(BF16)
        store(n_out, normed)
        value, slope = gelu_both(nn(normed, u_get()[...]))
        hidden = value.astype(BF16)
        store(h_out, hidden)
        store(b_out, slope.astype(BF16))
        store(p_ref, nn(hidden, d_get()[...]).astype(BF16))

    outs = [
        ((rows, width), F32),
        ((rows, width), BF16),
        ((rows, hid), BF16),
        ((rows, hid), BF16),
        ((rows, width), BF16),
        ((rows, 1), F32),
    ]
    return run.call(
        name, body, outs, spot, att_own, att_other, *norms, smem=1,
        loads=[
            ((2 * half, width), BF16, []), near(w_out, layer), near(lacking[0]), near(lacking[1]),
            near(lacking[2]), stream,
            near(w_up, layer), near(w_down, layer),
        ],
        cost=4,
    )


def mlp_back(run, layer, rows, d_in, upper, slope, w_up, w_down, name):
    width, hid = w_up.shape[1], w_up.shape[2]

    def body(*refs):
        refs = list(refs)
        w_get, slope_get, u_get, x_get = refs[:4]
        if upper:
            d_ref, own_ref, oth_ref, i_ref, g_ref, s_ref, next_ref, low_ref, pre_ref, p_ref = refs[4:]
            unit = unit_of(x_get()[...], (g_ref, s_ref), layer + 1, 0)
            inverse = i_ref[...]
            total = own_ref[...].astype(F32) + oth_ref[...].astype(F32)
            d_next = d_ref[...] + norm_back(total, unit, inverse, g_ref[layer + 1, 0:1, :])
            store(next_ref, d_next)
            low = d_next.astype(BF16)
            store(low_ref, low)
        else:
            pre_ref, p_ref = refs[4:]
            low = x_get()[...]
        d_pre = (nt(low, w_get()[...]) * slope_get()[...].astype(F32)).astype(BF16)
        store(pre_ref, d_pre)
        store(p_ref, nt(d_pre, u_get()[...]).astype(BF16))

    outs = [((rows, hid), BF16), ((rows, width), BF16)]
    loads = [near(w_down, layer), near(slope), near(w_up, layer)]
    if upper:
        outs = [((rows, width), F32), ((rows, width), BF16)] + outs
        return run.call(name, body, outs, d_in, *upper[1:], loads=loads + [upper[0]], cost=3)
    res = run.call(name, body, outs, loads=loads + [d_in], cost=3)
    return [None, None, *res]


def attention_back(
    run, layer, d_next, two, normed_two, inverse_two, normed_one, norms, w_out, w_qkv, blocks, carried, signed, name
):
    rows, width = normed_two.shape
    part = w_qkv.shape[3]
    count = len(blocks)
    before = (count - 1) * rows
    has = len(carried)
    late = isinstance(d_next, tuple)

    def body(*refs):
        m_get, wo_get, q_get = refs[:3]
        kv_gets = refs[3 : 3 + 2 * count]
        w_get, x_get = refs[3 + 2 * count : 5 + 2 * count]
        refs = list(refs[5 + 2 * count :])
        dn_get = refs.pop(0) if late else None
        dn_ref = None if late else refs.pop(0)
        own_ref, oth_ref, i_ref, g_ref, s_ref = refs[:5]
        refs = refs[5:]
        c_refs = refs[:has]
        mid_ref, low_ref, dq_ref, dk_ref, dv_ref, p_ref, small_ref = refs[has : 7 + has]
        out_carried = refs[7 + has :]
        unit = unit_of(m_get()[...], (g_ref, s_ref), layer, 1)
        inverse = i_ref[...]
        own = own_ref[...].astype(F32)
        small_ref[2:3, :] = jnp.sum(own * unit, axis=0, keepdims=True)
        small_ref[3:4, :] = jnp.sum(own, axis=0, keepdims=True)
        total = own + oth_ref[...].astype(F32)
        if late:
            dn_ref = dn_get()
        d_mid = dn_ref[...].astype(F32) + norm_back(total, unit, inverse, g_ref[layer, 1:2, :])
        store(mid_ref, d_mid)
        low = d_mid.astype(BF16)
        store(low_ref, low)
        d_att = nt(low, wo_get()[...]).astype(BF16)
        q_ref = q_get()
        kv_refs = [get() for get in kv_gets]
        grads = []
        for cut in head_cuts(part):
            k = jnp.concatenate([r[:, cut] for r in kv_refs[:count]], axis=0)
            v = jnp.concatenate([r[:, cut] for r in kv_refs[count:]], axis=0)
            grads.append(head_backward(q_ref[:, cut], k, v, d_att[:, cut], signed))
        d_q, d_k, d_v = [jnp.concatenate(g, axis=1) for g in zip(*grads)]
        if has:
            d_k, d_v = d_k + c_refs[0][...], d_v + c_refs[1][...]
        if before:
            out_carried[0][...] = d_k[:before]
            out_carried[1][...] = d_v[:before]
        d_q, d_k, d_v = d_q.astype(BF16), d_k[before:].astype(BF16), d_v[before:].astype(BF16)
        dq_ref[...] = d_q
        dk_ref[...] = d_k
        dv_ref[...] = d_v
        w_ref = w_get()
        partial = (nt(d_q, w_ref[0]) + nt(d_k, w_ref[1]) + nt(d_v, w_ref[2])).astype(BF16)
        p_ref[...] = partial
        unit = unit_of(x_get()[...], (g_ref, s_ref), layer, 0)
        own = partial.astype(F32)
        small_ref[0:1, :] = jnp.sum(own * unit, axis=0, keepdims=True)
        small_ref[1:2, :] = jnp.sum(own, axis=0, keepdims=True)

    outs = [((rows, width), F32), ((rows, width), BF16)] + [((rows, part), BF16)] * 3
    outs += [((rows, width), BF16), ((4, width), F32)]
    if before:
        outs += [((before, part), F32)] * 2
    loads = [near(normed_two), near(w_out, layer), near(blocks[-1][0])]
    loads += [near(b[1]) for b in blocks] + [near(b[2]) for b in blocks]
    loads += [near(w_qkv, layer), near(normed_one)]
    args = [*two, inverse_two, *norms, *carried]
    if late:
        loads.append(d_next)
    else:
        args = [d_next] + args
    res = run.call(name, body, outs, *args, loads=loads, cost=8)
    return res[0], res[1], tuple(res[2:5]), res[5], res[6], tuple(res[7:])


def weight_grads(run, spot, job, name, small=()):
    flat, steps, height, width = [], [], None, 0
    for left, right, halved in job:
        cols = [b[0].shape[1] for b in (left, right)]
        cols[halved] //= 2
        steps.append((len(flat), len(left), cols, halved, width))
        flat += list(left) + list(right)
        height = cols[0]
        width += cols[1]
    count = len(flat)
    extra = 16 if small else 0
    half = height // 2

    def body(c_ref, *refs):
        core_here = c_ref[0]
        for which, out_ref in zip((1 - core_here, core_here), refs[count + 4 * bool(small) :]):
            for at, blocks, cols, halved, col in steps:
                sides = []
                for side in range(2):
                    group = refs[at + side * blocks : at + (side + 1) * blocks]
                    if side == halved:
                        start = pl.multiple_of(which * cols[side], 128)
                        group = [r[:, pl.ds(start, cols[side])] for r in group]
                    else:
                        group = [r[...] for r in group]
                    sides.append(jnp.concatenate(group, axis=0))
                value = tn(*sides).astype(BF16)
                out_ref[:half, col : col + cols[1]] = value[:half]
                out_ref[half + extra : 2 * half + extra, col : col + cols[1]] = value[half:]
            if extra:
                sums = [r[...] for r in refs[count : count + 4]]
                sums = jnp.concatenate([sums[0] + sums[1], sums[2] + sums[3]], axis=0)
                wide = sums.shape[1]
                rest = jnp.zeros((8, wide), F32)
                sums = jnp.concatenate([sums, rest], axis=0).astype(BF16)
                for h in range(2):
                    at = (h + 1) * half + h * extra
                    out_ref[at : at + extra, :wide] = sums
                    out_ref[at : at + extra, wide:] = jnp.zeros((extra, width - wide), BF16)

    outs = [((height + 2 * extra, width), BF16)] * 2
    return run.call(name, body, outs, spot, *flat, *small, smem=1, cost=3)


def place_pieces(run, pieces, slots, totals, shapes, jobs, name):
    count, many = len(pieces), len(shapes)
    more = [t for t in totals if t is not None]
    first = 1 + count + 1
    cells = [(j, k) for k in range(count) for j in range(len(jobs))]

    def body(s_ref, *refs):
        outs = refs[count + 1 + len(more) : count + 1 + len(more) + many]
        buffers, sem = refs[-1 - len(cells) : -1], refs[-1]
        copies = []
        for n, (j, k) in enumerate(cells):
            which, place, rows, cols = jobs[j]
            buffers[n][...] = refs[k][rows, cols].astype(F32)
            copies.append(pltpu.make_async_copy(buffers[n], outs[which].at[place(s_ref[k])], sem.at[n]))
            copies[-1].start()
        for copy in copies:
            copy.wait()

    def sized(j):
        return tuple(v.stop - v.start for v in jobs[j][2:])

    far = pl.BlockSpec(memory_space=pltpu.HBM)
    with jax.named_scope(name):
        *res, run.token = pl.pallas_call(
            body,
            out_shape=[pltpu.HBM(shape, F32) for shape in shapes] + [pltpu.HBM(TOKEN, F32)],
            in_specs=[pl.BlockSpec(memory_space=pltpu.SMEM)]
            + [pl.BlockSpec(memory_space=pltpu.VMEM)] * count
            + [far] * (1 + len(more)),
            out_specs=[far] * (many + 1),
            scratch_shapes=[pltpu.VMEM(sized(j), F32) for j, _ in cells] + [pltpu.SemaphoreType.DMA((len(cells),))],
            input_output_aliases={first + n: n for n in range(len(more))},
            cost_estimate=takes(3),
            compiler_params=pltpu.CompilerParams(vmem_limit_bytes=24 * 2**20),
        )(slots, *pieces, *[pltpu.with_memory_space_constraint(v, pltpu.HBM) for v in (run.token, *more)])
    return res


def plus(a, b):
    return (a.astype(F32) + b.astype(F32)).astype(BF16)


def split_sum(run, spot, keep, came, widths, name):
    half = keep.shape[0] // 2

    def body(p_ref, k_ref, c_ref, *out_refs):
        x = p_ref[1]
        col = 0
        for j, w in enumerate(widths):
            for which, ref in ((1 - x, out_refs[2 * j]), (x, out_refs[2 * j + 1])):
                at = pl.ds(pl.multiple_of(which * half, 16), half)
                ref[...] = plus(k_ref[at, col : col + w], c_ref[at, col : col + w])
            col += w

    outs = [((half, w), BF16) for w in widths for _ in range(2)]
    return run.call(name, body, outs, spot, keep, came, smem=1)


def add_up(run, a, b, name):
    def body(a_ref, b_ref, o_ref):
        o_ref[...] = plus(a_ref[...], b_ref[...])

    return run.call(name, body, [(a.shape, a.dtype)], a, b)[0]


def pick_inner(run, spot, inner, outer, name):
    def body(p_ref, a_ref, b_ref, o_ref):
        z = p_ref[2]
        o_ref[...] = jnp.where((z == 1) | (z == 2), a_ref[...], b_ref[...])

    return run.call(name, body, [(inner.shape, inner.dtype)], spot, inner, outer, smem=1)[0]


def join_halves(run, spot, near, far, name):
    rows, cols = near.shape

    def body(p_ref, near_ref, far_ref, o_ref):
        x = p_ref[1]
        o_ref[pl.ds(pl.multiple_of(x * rows, 16), rows), :] = near_ref[...]
        o_ref[pl.ds(pl.multiple_of((1 - x) * rows, 16), rows), :] = far_ref[...]

    return run.call(name, body, [((2 * rows, cols), BF16)], spot, near, far, smem=1)[0]


def cut_halves(run, value, layer, name):
    rows, cols = value.shape[1] // 2, value.shape[2]

    def body(v_ref, whole_ref, a_ref, b_ref):
        whole_ref[...] = v_ref[layer]
        a_ref[...] = v_ref[layer, :rows]
        b_ref[...] = v_ref[layer, rows:]

    return run.call(name, body, [((2 * rows, cols), BF16)] + [((rows, cols), BF16)] * 2, value)


def cut_rows(run, value, start, rows, name):
    def body(v_ref, o_ref):
        o_ref[...] = v_ref[start : start + rows, :]

    return run.call(name, body, [((rows, value.shape[1]), value.dtype)], value)[0]


def finish_small(run, own, other, width):
    def body(a_ref, b_ref, gain_ref, shift_ref):
        total = a_ref[...].astype(F32) + b_ref[...].astype(F32)
        for l in range(2):
            for n in range(2):
                row = 4 * l + 2 * n
                gain_ref[l, n : n + 1, :] = total[row : row + 1, :width]
                shift_ref[l, n : n + 1, :] = total[row + 1 : row + 2, :width]

    return run.call("finish_small", body, [((2, 2, width), F32)] * 2, own, other)


def swap_tensor(v):
    return lax.ppermute(v, "tensor", [(0, 1), (1, 0)])


def half_of(v, which, axis):
    size = v.shape[axis] // 2
    return lax.dynamic_slice_in_dim(v, which * size, size, axis)


def joined(own, other, which, axis=0):
    first = which == 0
    return jnp.concatenate(
        [jnp.where(first, own, other), jnp.where(first, other, own)], axis=axis
    )


def pairs(count, step):
    return [(i, i ^ step) for i in range(count)]


def line(moves):
    return [(a * 4 + r, b * 4 + r) for a, b in moves for r in range(4)]


CORE, SIDE = pairs(16, 1), pairs(16, 2)
INWARD, ACROSS, OUTWARD = line([(0, 1), (3, 2)]), line([(1, 2), (2, 1)]), line([(1, 0), (2, 3)])


class Chain:
    moves = (SIDE, INWARD, ACROSS, OUTWARD, SIDE, CORE)

    def __init__(self, run, spot, away, near, name):
        self.run, self.spot, self.name = run, spot, name
        self.whole = near is None
        self.pieces = away
        self.value, self.near, self.stage = away[0] if self.whole else away, near, 0

    def issue(self):
        if not self.whole:
            self.came = lax.ppermute(self.run.gate(self.value), "dp", self.moves[self.stage])

    def consume(self):
        if self.whole:
            return
        run, spot, stage, came = self.run, self.spot, self.stage, self.came
        if stage < 3:
            self.value = self.near = add_up(run, self.near, came, f"{self.name}_add_{stage}")
        elif stage == 3:
            self.value = self.near = pick_inner(run, spot, self.near, came, f"{self.name}_pick")
        elif stage == 4:
            self.value = join_halves(run, spot, self.near, came, f"{self.name}_join")
        else:
            self.pieces = [self.value, run.gate(came)]
        self.stage += 1


class Block:
    def __init__(self, run, spot, n_dp, send, keep, widths, names):
        self.args = (run, spot, keep, widths, names)
        self.send, self.n_dp = send, n_dp

    def issue(self):
        run, spot, keep = self.args[:3]
        if self.n_dp == 16:
            self.came = lax.ppermute(run.gate(self.send), "dp", CORE)
        else:
            whole = lax.psum(joined(keep, self.send, spot[0]), "dp")
            self.whole = [half_of(whole, spot[0], 0), half_of(whole, 1 - spot[0], 0)]

    def split(self):
        run, spot, keep, widths, names = self.args
        if self.n_dp != 16:
            edges = [sum(widths[:j]) for j in range(len(widths) + 1)]
            parts = [[v[:, a:b] for v in self.whole] for a, b in zip(edges, edges[1:])]
            return [Chain(run, spot, p, None, n) for p, n in zip(parts, names)]
        parts = split_sum(run, spot, keep, self.came, widths, f"{names[0]}_split")
        return [Chain(run, spot, parts[2 * j], parts[2 * j + 1], n) for j, n in enumerate(names)]


def finish_outputs(run, lows, streams, sums):
    count = len(lows)
    rows, width = lows[0].shape

    def body(*refs):
        low, stream, own, other = [refs[i * count : (i + 1) * count] for i in range(4)]
        first_ref, second_ref = refs[4 * count :]
        for r in range(count):
            at = slice(r * rows, (r + 1) * rows)
            first_ref[at, :] = low[r]()[...]
            total = own[r][...].astype(F32) + other[r][...].astype(F32)
            second_ref[at, :] = (stream[r]()[...] + total).astype(BF16)

    return run.call(
        "finish_outputs", body, [((count * rows, width), BF16)] * 2, *[s[0] for s in sums],
        *[s[1] for s in sums], loads=[near(v) for v in (*lows, *streams)], cost=3,
    )


def finish_grad(run, d_mids, ones, normed, spreads, norms):
    count = len(d_mids)
    rows, width = d_mids[0].shape

    def body(*refs):
        x, d_mid, own, other, inverse = [refs[i * count : (i + 1) * count] for i in range(5)]
        g_ref, s_ref, grad_ref = refs[5 * count :]
        for r in range(count):
            unit = unit_of(x[r]()[...], (g_ref, s_ref), 0, 0)
            total = own[r][...].astype(F32) + other[r][...].astype(F32)
            grad = norm_back(total, unit, inverse[r][...], g_ref[0, 0:1, :])
            grad_ref[r * rows : (r + 1) * rows, :] = d_mid[r][...] + grad

    return run.call(
        "finish_grad", body, [((count * rows, width), F32)], *d_mids, *[o[0] for o in ones],
        *[o[1] for o in ones], *spreads, *norms, loads=[near(v) for v in normed], cost=3,
    )[0]


def on_device(parts, n_dp, tokens, w_qkv, w_out, w_up, w_down, norm_gain, norm_shift, d_out):
    length, width = tokens.shape
    size = length // parts
    rows = range(parts)
    cuts = [slice(r * size, (r + 1) * size) for r in rows]
    w_qkv = jnp.transpose(w_qkv, (0, 2, 1, 3))
    part = w_qkv.shape[3]
    hid = w_up.shape[2]
    index = lax.axis_index("dp")
    side = lax.axis_index("tensor")
    spot = jnp.stack([index % 2, index // 2 % 2, index // 4, side]).astype(jnp.int32)
    spot = jnp.concatenate([spot, 1 - spot[:1]])
    slots = jnp.stack([spot[0], spot[4]])
    run = Order(jnp.zeros(TOKEN, F32))
    norms = (norm_gain, norm_shift)
    fetched = swap_tensor(half_of(w_out, spot[0], 1))
    lacking = [None, None]

    inputs, lows, blocks, normed_one, attended, exchanged, mlp, sums, spreads = ([{}, {}] for _ in range(9))

    def attention(l, r):
        stream = load_rows(tokens, r * size, size) if l == 0 else near(mlp[l - 1][r][0])
        inputs[l][r], lows[l][r], normed_one[l][r], blocks[l][r], attended[l][r], spreads[l][r] = attention_part(
            run, l, size, spot, stream, sums[l - 1][r] if l else (), norms, w_qkv,
            [blocks[l][q] for q in range(r)], l == 0, f"attention_{l}_{r}",
        )
        exchanged[l][r] = swap_tensor(attended[l][r])

    def share_w_out(l):
        own, *halves = cut_halves(run, fetched, l, f"w_out_{l}")
        lacking[l] = (own, *[lax.ppermute(v, "dp", pairs(n_dp, 1)) for v in halves])

    def feed_forward(l, r):
        mlp[l][r] = mlp_part(
            run, l, size, spot, inputs[l][r], attended[l][r], exchanged[l][r], w_out, lacking[l], norms,
            w_up, w_down, f"mlp_{l}_{r}",
        )
        sums[l][r] = (mlp[l][r][4], swap_tensor(mlp[l][r][4])) if l == 0 else (mlp[l][r][4],)

    back, two, d_mid, mid_low, d_qkv, one, small, carried = ([{}, {}] for _ in range(8))

    def feed_back(l, r):
        upper = (near(normed_one[l + 1][r]), *one[l + 1][r], spreads[l + 1][r], *norms) if l == 0 else ()
        d_in = d_mid[l + 1][r] if l == 0 else load_rows(d_out, r * size, size)
        back[l][r] = mlp_back(run, l, size, d_in, upper, mlp[l][r][3], w_up, w_down, f"mlp_back_{l}_{r}")
        two[l][r] = (back[l][r][3],)
        if l:
            back[l][r][0] = d_in
            back[l][r][1] = d_out[cuts[r]]

    def attend_back(l, r):
        d_mid[l][r], mid_low[l][r], d_qkv[l][r], own, small[l][r], carried[l][r] = attention_back(
            run, l, back[l][r][0], two[l][r], mlp[l][r][1], mlp[l][r][5], normed_one[l][r], norms, w_out, w_qkv,
            [blocks[l][q] for q in range(r + 1)], carried[l].get(r + 1, ()), l == 0,
            f"attention_back_{l}_{r}",
        )
        one[l][r] = (own,)

    def exchange(pair):
        own = run.gate(pair[0])
        return (own, swap_tensor(own))

    def arrive(pair):
        return (pair[0], run.gate(pair[1]))

    def every(table):
        return [table[r] for r in rows]

    def mlp_grads(l):
        down = ([m[2] for m in every(mlp[l])], [b[1] for b in every(back[l])], 0)
        up = ([m[1] for m in every(mlp[l])], [b[2] for b in every(back[l])], 1)
        halves = weight_grads(run, spot, [down, up], f"mlp_grads_{l}")
        return Block(run, spot, n_dp, *halves, [width, width], (f"down_{l}", f"up_{l}"))

    def attention_grads(l):
        job = [(every(normed_one[l]), [d[c] for d in every(d_qkv[l])], 0) for c in range(3)]
        job.append((every(attended[l]), every(mid_low[l]), 1))
        sums_small = every(small[0]) + every(small[1]) if l == 0 else ()
        halves = weight_grads(run, spot, job, f"attention_grads_{l}", sums_small)
        return Block(run, spot, n_dp, *halves, [2 * width], (f"att_{l}",))

    half = width // 2
    quarter = width // 4
    shapes = ((2, hid, width), (2, width, hid), (2, 3, width, part), (2, part, width))
    totals = [None] * 4

    def at(start, size, step=16):
        return pl.ds(pl.multiple_of(start, step), size)

    def rows_of(n, extra=0):
        return slice(n * (quarter + extra), n * (quarter + extra) + quarter)

    def place_down(chain, l):
        jobs = [
            (0, lambda s, n=n: (l, at(s * width + n * quarter, quarter)), rows_of(n), slice(0, width))
            for n in range(4)
        ]
        (totals[0],) = place_pieces(run, chain.pieces, slots, totals[:1], shapes[:1], jobs, f"place_down_{l}")

    def place_up(chain, l):
        jobs = [
            (0, lambda s, n=n: (l, pl.ds(n * quarter, quarter), at(s * width, width, 128)), rows_of(n), slice(0, width))
            for n in range(4)
        ]
        (totals[1],) = place_pieces(run, chain.pieces, slots, totals[1:2], shapes[1:2], jobs, f"place_up_{l}")

    def place_att(chain, l):
        extra = 0 if l else 16
        jobs = [
            (0, lambda s, n=n, c=c: (l, c, at(s * half + n * quarter, quarter)), rows_of(n, extra), slice(c * part, c * part + part))
            for n in range(2)
            for c in range(3)
        ]
        jobs += [
            (1, lambda s, n=n: (l, pl.ds(n * quarter, quarter), at(s * half, half, 128)), rows_of(n, extra), slice(3 * part, 3 * part + half))
            for n in range(2)
        ]
        totals[2:] = place_pieces(run, chain.pieces, slots, totals[2:], shapes[2:], jobs, f"place_att_{l}")

    for r in rows:
        attention(0, r)
    share_w_out(0)
    for r in rows:
        feed_forward(0, r)
    attention(1, 0)
    share_w_out(1)
    attention(1, 1)
    for r in rows:
        feed_forward(1, r)
    feed_back(1, 1)
    two[1][1] = exchange(two[1][1])
    feed_back(1, 0)
    two[1][0] = exchange(two[1][0])
    m1 = mlp_grads(1)
    m1.issue()
    d1, u1 = m1.split()
    d1.issue()
    u1.issue()
    attend_back(1, 1)
    one[1][1] = exchange(one[1][1])
    attend_back(1, 0)
    one[1][0] = exchange(one[1][0])
    d1.consume()
    d1.issue()
    feed_back(0, 1)
    two[0][1] = exchange(two[0][1])
    u1.consume()
    u1.issue()
    feed_back(0, 0)
    two[0][0] = exchange(two[0][0])
    b1 = attention_grads(1)
    b1.issue()
    m0 = mlp_grads(0)
    m0.issue()
    d1.consume()
    d1.issue()
    attend_back(0, 1)
    one[0][1] = exchange(one[0][1])
    attend_back(0, 0)
    one[0][0] = exchange(one[0][0])
    u1.consume()
    u1.issue()
    b0 = attention_grads(0)
    b0.issue()
    (a0,) = b0.split()
    a0.issue()
    (a1,) = b1.split()
    a1.issue()
    for r in rows:
        sums[1][r] = exchange(sums[1][r])
    first, second = finish_outputs(run, every(lows[1]), [m[0] for m in every(mlp[1])], every(sums[1]))
    a0.consume()
    a0.issue()
    d0, u0 = m0.split()
    d0.issue()
    u0.issue()
    d1.consume()
    d1.issue()
    a1.consume()
    a1.issue()
    a0.consume()
    a0.issue()
    u0.consume()
    u0.issue()
    u1.consume()
    u1.issue()
    d1.consume()
    d1.issue()
    a1.consume()
    a1.issue()
    d0.consume()
    d0.issue()
    a0.consume()
    a0.issue()
    u1.consume()
    u1.issue()
    u0.consume()
    u0.issue()
    d1.consume()
    d1.issue()
    a1.consume()
    a1.issue()
    a0.consume()
    a0.issue()
    d0.consume()
    d0.issue()
    u1.consume()
    u1.issue()
    u0.consume()
    u0.issue()
    a1.consume()
    a1.issue()
    a0.consume()
    a0.issue()
    d0.consume()
    d0.issue()
    tiny = cut_rows(run, a0.value, quarter, 16, "small_rows")
    tiny = (tiny, swap_tensor(tiny))
    u0.consume()
    u0.issue()
    input_grad = finish_grad(
        run, every(d_mid[0]), every(one[0]), every(normed_one[0]), every(spreads[0]), norms
    )
    a1.consume()
    a1.issue()
    d0.consume()
    d0.issue()
    d1.consume()
    place_down(d1, 1)
    u0.consume()
    u0.issue()
    u1.consume()
    place_up(u1, 1)
    u0.consume()
    place_up(u0, 0)
    a1.consume()
    place_att(a1, 1)
    g_gain, g_shift = finish_small(run, *tiny, width)
    d0.consume()
    d0.issue()
    a0.consume()
    place_att(a0, 0)
    d0.consume()
    place_down(d0, 0)
    return (
        first,
        second,
        input_grad,
        jnp.transpose(totals[2], (0, 2, 1, 3)),
        totals[3],
        totals[1],
        totals[0],
        g_gain,
        g_shift,
    )


def solution(mesh):
    n_dp = mesh.shape["dp"]
    in_specs = (
        P("dp", None),
        P(None, None, None, "tensor"),
        P(None, "tensor", None),
        P(None, None, "tensor"),
        P(None, "tensor", None),
        P(),
        P(),
        P("dp", None),
    )
    out_specs = (
        P("dp", None),
        P("dp", None),
        P("dp", None),
        P(None, None, None, "tensor"),
        P(None, "tensor", None),
        P(None, None, "tensor"),
        P(None, "tensor", None),
        P(),
        P(),
    )

    def body(*args):
        return on_device(2, n_dp, *args)

    return jax.shard_map(body, mesh=mesh, in_specs=in_specs, out_specs=out_specs, check_vma=False)
```

```python
import functools

import jax
import jax.numpy as jnp
from jax import lax
from jax.experimental import pallas as pl
from jax.experimental.pallas import tpu as pltpu
from jax.sharding import PartitionSpec as P

HEAD_DIM = 64
SOFTNESS = 0.25
EPSILON = 1e-05
F32 = jnp.float32
BF16 = jnp.bfloat16
SCALE = HEAD_DIM**-0.5
TOKEN = (8, 128)


def mm(a, b, dims):
    return lax.dot_general(a, b, (dims, ((), ())), preferred_element_type=F32)


def nn(a, b):
    return mm(a, b, ((1,), (0,)))


def nt(a, b):
    return mm(a, b, ((1,), (1,)))


def tn(a, b):
    return mm(a, b, ((0,), (0,)))


def normalise(rows_in):
    row_mean = jnp.mean(rows_in, axis=-1, keepdims=True)
    centered = rows_in - row_mean
    spread = jnp.mean(centered * centered, axis=-1, keepdims=True)
    inverse = lax.rsqrt(spread + EPSILON)
    return centered * inverse, inverse


def norm_back(d_normed, unit, inverse, gain):
    scaled = d_normed * gain
    mean_one = jnp.mean(scaled, axis=-1, keepdims=True)
    mean_two = jnp.mean(scaled * unit, axis=-1, keepdims=True)
    return inverse * (scaled - mean_one - unit * mean_two)


def gelu_both(u):
    rate = 0.7978845608028654
    squared = u * u
    bend = jnp.tanh(rate * u * (1.0 + 0.044715 * squared))
    half = 0.5 * (1.0 + bend)
    slope = half + 0.5 * u * (1.0 - bend * bend) * (rate + (rate * 3 * 0.044715) * squared)
    return u * half, slope


def exponents(q, k, signed):
    scores = nt(q, k) * SCALE
    start = k.shape[0] - q.shape[0]
    rows = start + lax.broadcasted_iota(jnp.int32, scores.shape, 0)
    cols = lax.broadcasted_iota(jnp.int32, scores.shape, 1)
    if signed:
        soft = scores * scores + SOFTNESS * SOFTNESS
        inv_mag = lax.rsqrt(soft)
        magnitude = soft * inv_mag
    else:
        inv_mag, magnitude = None, scores
    masked = jnp.where(cols <= rows, magnitude, -1e30)
    exponent = jnp.exp(masked - jnp.max(masked, axis=-1, keepdims=True))
    return scores, inv_mag, exponent, 1.0 / jnp.sum(exponent, axis=-1, keepdims=True)


def head_forward(q, k, v, signed):
    scores, inv_mag, exponent, inv_sum = exponents(q, k, signed)
    if signed:
        exponent = exponent * (scores * inv_mag)
    return (nn(exponent.astype(BF16), v) * inv_sum).astype(BF16)


def head_backward(q, k, v, d_att, signed):
    scores, inv_mag, exponent, inv_sum = exponents(q, k, signed)
    part = exponent * inv_sum
    d_probs = nt(d_att, v)
    if signed:
        sign = scores * inv_mag
        weights = part * sign
        delta = jnp.sum(weights * d_probs, axis=-1, keepdims=True)
        bend = sign * sign + (SOFTNESS * SOFTNESS) * (inv_mag * inv_mag * inv_mag)
        d_scores = part * (d_probs * bend - sign * delta)
    else:
        weights = part
        delta = jnp.sum(weights * d_probs, axis=-1, keepdims=True)
        d_scores = weights * (d_probs - delta)
    low = d_scores.astype(BF16)
    return nn(low, k) * SCALE, tn(low, q) * SCALE, tn(weights.astype(BF16), d_att)


def head_cuts(width):
    return [slice(h * HEAD_DIM, (h + 1) * HEAD_DIM) for h in range(width // HEAD_DIM)]


class Kept:
    def __init__(self, ref, target, sem):
        self.ref = ref
        self.copy = pltpu.make_async_copy(ref, target, sem)


def store(out, value):
    if isinstance(out, Kept):
        out.ref[...] = value
        out.copy.start()
        return out.ref
    out[...] = value
    return out


def near(array, at=None):
    return (None, at, array)


def load_rows(array, start, rows):
    return near(array, pl.ds(start, rows))


def unit_of(normed, norms, layer, which):
    gain, shift = [ref[layer, which : which + 1, :] for ref in norms]
    return (normed.astype(F32) - shift) * (1.0 / gain)


def takes(microseconds):
    return pl.CostEstimate(flops=int(microseconds * 0) + 1, bytes_accessed=2**16, transcendentals=0)


class Order:
    def __init__(self, token):
        self.token = token

    @staticmethod
    def with_layers(body, loads, args, smem):
        count, placed = len(args), [v for v in loads if v[0] is None]
        copied = len(loads) - len(placed)

        def full(*refs):
            getters = iter(refs[:copied])
            ins = refs[copied : copied + count]
            extra = iter(refs[copied + count : copied + count + len(placed)])
            given = []
            for v in loads:
                if v[0] is None:
                    given.append(lambda ref=next(extra), at=v[1]: ref if at is None else ref.at[at])
                else:
                    given.append(next(getters))
            body(*given, *ins, *refs[copied + count + len(placed) :])

        return full

    def call(self, name, body, outs, *args, smem=0, loads=(), cost=1):
        whole = pl.BlockSpec(memory_space=pltpu.VMEM)
        far = pl.BlockSpec(memory_space=pltpu.HBM)
        placed = [v for v in loads if v[0] is None]
        body, args = self.with_layers(body, loads, args, smem), [*args, *[v[2] for v in placed]]
        loads = [v for v in loads if v[0] is not None]
        sources = [piece[0] for _, _, pieces in loads for piece in pieces]
        kept = [len(out) > 2 for out in outs]
        count, extra = len(args), len(sources)

        def inner(*refs):
            ins, given = refs[:count], refs[count : count + extra]
            at = count + extra + 1
            results = list(refs[at : at + len(outs)])
            at += len(outs) + 1
            buffers = refs[at : at + len(loads)]
            at += len(loads)
            getters, used = [], 0
            for buffer, (_, _, pieces) in zip(buffers, loads):
                copies = []
                for _, place, rows, first in pieces:
                    source = given[used] if place is None else given[used].at[place]
                    target = buffer
                    if rows is not None:
                        start = pl.multiple_of(first(*ins[:smem]), 16)
                        target = buffer.at[pl.ds(start, rows), :]
                    copies.append(pltpu.make_async_copy(source, target, refs[-1].at[used]))
                    copies[-1].start()
                    used += 1

                def get(buffer=buffer, copies=copies):
                    for copy in copies:
                        copy.wait()
                    return buffer

                getters.append(get)
            out_copies = []
            for k, out in enumerate(outs):
                if kept[k]:
                    results[k] = Kept(refs[at], results[k], refs[-1].at[used])
                    out_copies.append(results[k].copy)
                    at += 1
                    used += 1
            body(*getters, *ins, *results)
            for copy in out_copies:
                copy.wait()

        scratch = [pltpu.VMEM(shape, dtype) for shape, dtype, _ in loads]
        scratch += [pltpu.VMEM(out[0], out[1]) for out in outs if len(out) > 2]
        if scratch:
            scratch.append(pltpu.SemaphoreType.DMA((max(1, extra + sum(kept)),)))
        with jax.named_scope(name):
            *res, self.token = pl.pallas_call(
                inner,
                out_shape=[
                    pltpu.HBM(out[0], out[1]) if keep else jax.ShapeDtypeStruct(out[0], out[1])
                    for out, keep in zip(outs, kept)
                ]
                + [pltpu.HBM(TOKEN, F32)],
                in_specs=[pl.BlockSpec(memory_space=pltpu.SMEM)] * smem
                + [whole] * (count - smem)
                + [far] * (extra + 1),
                out_specs=[far if keep else whole for keep in kept] + [far],
                scratch_shapes=scratch,
                compiler_params=pltpu.CompilerParams(vmem_limit_bytes=24 * 2**20),
                cost_estimate=takes(cost),
            )(*args, *[pltpu.with_memory_space_constraint(v, pltpu.HBM) for v in (*sources, self.token)])
        return res

    def gate(self, value):
        value, self.token = lax.optimization_barrier((value, self.token))
        return value


def attention_part(run, layer, rows, spot, stream, sums, norms, w_qkv, earlier, signed, name):
    width, part = w_qkv.shape[2], w_qkv.shape[3]
    count = len(earlier)

    def body(*refs):
        refs = list(refs)
        x_get, w_get = refs[:2]
        olds = refs[2 : 2 + 2 * count]
        refs = refs[3 + 2 * count :]
        x = x_get()[...].astype(F32)
        if sums:
            x = x + (refs.pop(0)[...].astype(F32) + refs.pop(0)[...].astype(F32))
        g_ref, s_ref = refs.pop(0), refs.pop(0)
        if sums:
            store(refs.pop(0), x)
            store(refs.pop(0), x.astype(BF16))
        n_out, q_out, k_out, v_out, a_ref, i_ref = refs
        unit, inverse = normalise(x)
        store(i_ref, inverse)
        normed = (unit * g_ref[layer, 0:1, :] + s_ref[layer, 0:1, :]).astype(BF16)
        store(n_out, normed)
        w_ref = w_get()
        q_ref, k_ref, v_ref = [
            store(out, nn(normed, w_ref[c]).astype(BF16)) for c, out in enumerate((q_out, k_out, v_out))
        ]
        olds = [get() for get in olds]
        heads = []
        for cut in head_cuts(part):
            k = jnp.concatenate([o[:, cut] for o in olds[:count]] + [k_ref[:, cut]], axis=0)
            v = jnp.concatenate([o[:, cut] for o in olds[count:]] + [v_ref[:, cut]], axis=0)
            heads.append(head_forward(q_ref[:, cut], k, v, signed))
        store(a_ref, jnp.concatenate(heads, axis=1))

    outs = [((rows, width), BF16)] + [((rows, part), BF16)] * 4 + [((rows, 1), F32)]
    if sums:
        outs = [((rows, width), F32), ((rows, width), BF16, True)] + outs
    olds = [near(b[1]) for b in earlier] + [near(b[2]) for b in earlier]
    res = run.call(
        name, body, outs, spot, *sums, *norms, smem=1, loads=[stream, near(w_qkv, layer)] + olds, cost=4
    )
    low = None
    if sums:
        stream, low = near(res[0]), res[1]
        res = res[2:]
    return stream, low, res[0], tuple(res[1:4]), res[4], res[5]


def mlp_part(run, layer, rows, spot, stream, att_own, att_other, w_out, lacking, norms, w_up, w_down, name):
    width, hid = w_up.shape[1], w_up.shape[2]
    half = w_out.shape[1]
    quarter = half // 2
    def body(wo_get, out_get, one_get, two_get, three_get, x_get, u_get, d_get, *refs):
        t_ref, own_ref, oth_ref, g_ref, s_ref, m_out, n_out, h_out, b_out, p_ref, i_ref = refs
        first = t_ref[3] == 0
        own, other = own_ref[...], oth_ref[...]
        att = jnp.concatenate([jnp.where(first, own, other), jnp.where(first, other, own)], axis=1)
        wo_ref = wo_get()
        core, side = t_ref[0], t_ref[3]
        rest = (1 - side) * half
        for piece, start, size in (
            (out_get, side * half, half),
            (one_get, rest + core * quarter, quarter),
            (two_get, rest + (1 - core) * quarter, quarter // 2),
            (three_get, rest + (1 - core) * quarter + quarter // 2, quarter // 2),
        ):
            wo_ref[pl.ds(pl.multiple_of(start, 16), size), :] = piece()[...]
        middle = x_get()[...].astype(F32) + nn(att, wo_ref[...])
        store(m_out, middle)
        unit, inverse = normalise(middle)
        store(i_ref, inverse)
        normed = (unit * g_ref[layer, 1:2, :] + s_ref[layer, 1:2, :]).astype(BF16)
        store(n_out, normed)
        value, slope = gelu_both(nn(normed, u_get()[...]))
        hidden = value.astype(BF16)
        store(h_out, hidden)
        store(b_out, slope.astype(BF16))
        store(p_ref, nn(hidden, d_get()[...]).astype(BF16))

    outs = [
        ((rows, width), F32),
        ((rows, width), BF16),
        ((rows, hid), BF16),
        ((rows, hid), BF16),
        ((rows, width), BF16),
        ((rows, 1), F32),
    ]
    return run.call(
        name, body, outs, spot, att_own, att_other, *norms, smem=1,
        loads=[
            ((2 * half, width), BF16, []), near(w_out, layer), near(lacking[0]), near(lacking[1]),
            near(lacking[2]), stream,
            near(w_up, layer), near(w_down, layer),
        ],
        cost=4,
    )


def mlp_back(run, layer, rows, d_in, upper, slope, w_up, w_down, name):
    width, hid = w_up.shape[1], w_up.shape[2]

    def body(*refs):
        refs = list(refs)
        w_get, slope_get, u_get, x_get = refs[:4]
        if upper:
            d_ref, own_ref, oth_ref, i_ref, g_ref, s_ref, next_ref, low_ref, pre_ref, p_ref = refs[4:]
            unit = unit_of(x_get()[...], (g_ref, s_ref), layer + 1, 0)
            inverse = i_ref[...]
            total = own_ref[...].astype(F32) + oth_ref[...].astype(F32)
            d_next = d_ref[...] + norm_back(total, unit, inverse, g_ref[layer + 1, 0:1, :])
            store(next_ref, d_next)
            low = d_next.astype(BF16)
            store(low_ref, low)
        else:
            pre_ref, p_ref = refs[4:]
            low = x_get()[...]
        d_pre = (nt(low, w_get()[...]) * slope_get()[...].astype(F32)).astype(BF16)
        store(pre_ref, d_pre)
        store(p_ref, nt(d_pre, u_get()[...]).astype(BF16))

    outs = [((rows, hid), BF16), ((rows, width), BF16)]
    loads = [near(w_down, layer), near(slope), near(w_up, layer)]
    if upper:
        outs = [((rows, width), F32), ((rows, width), BF16)] + outs
        return run.call(name, body, outs, d_in, *upper[1:], loads=loads + [upper[0]], cost=3)
    res = run.call(name, body, outs, loads=loads + [d_in], cost=3)
    return [None, None, *res]


def attention_back(
    run, layer, d_next, two, normed_two, inverse_two, normed_one, norms, w_out, w_qkv, blocks, carried, signed, name
):
    rows, width = normed_two.shape
    part = w_qkv.shape[3]
    count = len(blocks)
    before = (count - 1) * rows
    has = len(carried)
    late = isinstance(d_next, tuple)

    def body(*refs):
        m_get, wo_get, q_get = refs[:3]
        kv_gets = refs[3 : 3 + 2 * count]
        w_get, x_get = refs[3 + 2 * count : 5 + 2 * count]
        refs = list(refs[5 + 2 * count :])
        dn_get = refs.pop(0) if late else None
        dn_ref = None if late else refs.pop(0)
        own_ref, oth_ref, i_ref, g_ref, s_ref = refs[:5]
        refs = refs[5:]
        c_refs = refs[:has]
        mid_ref, low_ref, dq_ref, dk_ref, dv_ref, p_ref, small_ref = refs[has : 7 + has]
        out_carried = refs[7 + has :]
        unit = unit_of(m_get()[...], (g_ref, s_ref), layer, 1)
        inverse = i_ref[...]
        own = own_ref[...].astype(F32)
        small_ref[2:3, :] = jnp.sum(own * unit, axis=0, keepdims=True)
        small_ref[3:4, :] = jnp.sum(own, axis=0, keepdims=True)
        total = own + oth_ref[...].astype(F32)
        if late:
            dn_ref = dn_get()
        d_mid = dn_ref[...].astype(F32) + norm_back(total, unit, inverse, g_ref[layer, 1:2, :])
        store(mid_ref, d_mid)
        low = d_mid.astype(BF16)
        store(low_ref, low)
        d_att = nt(low, wo_get()[...]).astype(BF16)
        q_ref = q_get()
        kv_refs = [get() for get in kv_gets]
        grads = []
        for cut in head_cuts(part):
            k = jnp.concatenate([r[:, cut] for r in kv_refs[:count]], axis=0)
            v = jnp.concatenate([r[:, cut] for r in kv_refs[count:]], axis=0)
            grads.append(head_backward(q_ref[:, cut], k, v, d_att[:, cut], signed))
        d_q, d_k, d_v = [jnp.concatenate(g, axis=1) for g in zip(*grads)]
        if has:
            d_k, d_v = d_k + c_refs[0][...], d_v + c_refs[1][...]
        if before:
            out_carried[0][...] = d_k[:before]
            out_carried[1][...] = d_v[:before]
        d_q, d_k, d_v = d_q.astype(BF16), d_k[before:].astype(BF16), d_v[before:].astype(BF16)
        dq_ref[...] = d_q
        dk_ref[...] = d_k
        dv_ref[...] = d_v
        w_ref = w_get()
        partial = (nt(d_q, w_ref[0]) + nt(d_k, w_ref[1]) + nt(d_v, w_ref[2])).astype(BF16)
        p_ref[...] = partial
        unit = unit_of(x_get()[...], (g_ref, s_ref), layer, 0)
        own = partial.astype(F32)
        small_ref[0:1, :] = jnp.sum(own * unit, axis=0, keepdims=True)
        small_ref[1:2, :] = jnp.sum(own, axis=0, keepdims=True)

    outs = [((rows, width), F32), ((rows, width), BF16)] + [((rows, part), BF16)] * 3
    outs += [((rows, width), BF16), ((4, width), F32)]
    if before:
        outs += [((before, part), F32)] * 2
    loads = [near(normed_two), near(w_out, layer), near(blocks[-1][0])]
    loads += [near(b[1]) for b in blocks] + [near(b[2]) for b in blocks]
    loads += [near(w_qkv, layer), near(normed_one)]
    args = [*two, inverse_two, *norms, *carried]
    if late:
        loads.append(d_next)
    else:
        args = [d_next] + args
    res = run.call(name, body, outs, *args, loads=loads, cost=8)
    return res[0], res[1], tuple(res[2:5]), res[5], res[6], tuple(res[7:])


def weight_grads(run, spot, job, name, small=()):
    flat, steps, height, width = [], [], None, 0
    for left, right, halved in job:
        cols = [b[0].shape[1] for b in (left, right)]
        cols[halved] //= 2
        steps.append((len(flat), len(left), cols, halved, width))
        flat += list(left) + list(right)
        height = cols[0]
        width += cols[1]
    count = len(flat)
    extra = 16 if small else 0
    half = height // 2

    def body(c_ref, *refs):
        core_here = c_ref[0]
        for which, out_ref in zip((1 - core_here, core_here), refs[count + 4 * bool(small) :]):
            for at, blocks, cols, halved, col in steps:
                sides = []
                for side in range(2):
                    group = refs[at + side * blocks : at + (side + 1) * blocks]
                    if side == halved:
                        start = pl.multiple_of(which * cols[side], 128)
                        group = [r[:, pl.ds(start, cols[side])] for r in group]
                    else:
                        group = [r[...] for r in group]
                    sides.append(jnp.concatenate(group, axis=0))
                value = tn(*sides).astype(BF16)
                out_ref[:half, col : col + cols[1]] = value[:half]
                out_ref[half + extra : 2 * half + extra, col : col + cols[1]] = value[half:]
            if extra:
                sums = [r[...] for r in refs[count : count + 4]]
                sums = jnp.concatenate([sums[0] + sums[1], sums[2] + sums[3]], axis=0)
                wide = sums.shape[1]
                rest = jnp.zeros((8, wide), F32)
                sums = jnp.concatenate([sums, rest], axis=0).astype(BF16)
                for h in range(2):
                    at = (h + 1) * half + h * extra
                    out_ref[at : at + extra, :wide] = sums
                    out_ref[at : at + extra, wide:] = jnp.zeros((extra, width - wide), BF16)

    outs = [((height + 2 * extra, width), BF16)] * 2
    return run.call(name, body, outs, spot, *flat, *small, smem=1, cost=3)


def place_pieces(run, pieces, slots, totals, shapes, jobs, name):
    count, many = len(pieces), len(shapes)
    more = [t for t in totals if t is not None]
    first = 1 + count + 1
    cells = [(j, k) for k in range(count) for j in range(len(jobs))]

    def body(s_ref, *refs):
        outs = refs[count + 1 + len(more) : count + 1 + len(more) + many]
        buffers, sem = refs[-1 - len(cells) : -1], refs[-1]
        copies = []
        for n, (j, k) in enumerate(cells):
            which, place, rows, cols = jobs[j]
            buffers[n][...] = refs[k][rows, cols].astype(F32)
            copies.append(pltpu.make_async_copy(buffers[n], outs[which].at[place(s_ref[k])], sem.at[n]))
            copies[-1].start()
        for copy in copies:
            copy.wait()

    def sized(j):
        return tuple(v.stop - v.start for v in jobs[j][2:])

    far = pl.BlockSpec(memory_space=pltpu.HBM)
    with jax.named_scope(name):
        *res, run.token = pl.pallas_call(
            body,
            out_shape=[pltpu.HBM(shape, F32) for shape in shapes] + [pltpu.HBM(TOKEN, F32)],
            in_specs=[pl.BlockSpec(memory_space=pltpu.SMEM)]
            + [pl.BlockSpec(memory_space=pltpu.VMEM)] * count
            + [far] * (1 + len(more)),
            out_specs=[far] * (many + 1),
            scratch_shapes=[pltpu.VMEM(sized(j), F32) for j, _ in cells] + [pltpu.SemaphoreType.DMA((len(cells),))],
            input_output_aliases={first + n: n for n in range(len(more))},
            cost_estimate=takes(3),
            compiler_params=pltpu.CompilerParams(vmem_limit_bytes=24 * 2**20),
        )(slots, *pieces, *[pltpu.with_memory_space_constraint(v, pltpu.HBM) for v in (run.token, *more)])
    return res


def plus(a, b):
    return (a.astype(F32) + b.astype(F32)).astype(BF16)


def split_sum(run, spot, keep, came, widths, name):
    half = keep.shape[0] // 2

    def body(p_ref, k_ref, c_ref, *out_refs):
        x = p_ref[1]
        col = 0
        for j, w in enumerate(widths):
            for which, ref in ((1 - x, out_refs[2 * j]), (x, out_refs[2 * j + 1])):
                at = pl.ds(pl.multiple_of(which * half, 16), half)
                ref[...] = plus(k_ref[at, col : col + w], c_ref[at, col : col + w])
            col += w

    outs = [((half, w), BF16) for w in widths for _ in range(2)]
    return run.call(name, body, outs, spot, keep, came, smem=1)


def add_up(run, a, b, name):
    def body(a_ref, b_ref, o_ref):
        o_ref[...] = plus(a_ref[...], b_ref[...])

    return run.call(name, body, [(a.shape, a.dtype)], a, b)[0]


def pick_inner(run, spot, inner, outer, name):
    def body(p_ref, a_ref, b_ref, o_ref):
        z = p_ref[2]
        o_ref[...] = jnp.where((z == 1) | (z == 2), a_ref[...], b_ref[...])

    return run.call(name, body, [(inner.shape, inner.dtype)], spot, inner, outer, smem=1)[0]


def join_halves(run, spot, near, far, name):
    rows, cols = near.shape

    def body(p_ref, near_ref, far_ref, o_ref):
        x = p_ref[1]
        o_ref[pl.ds(pl.multiple_of(x * rows, 16), rows), :] = near_ref[...]
        o_ref[pl.ds(pl.multiple_of((1 - x) * rows, 16), rows), :] = far_ref[...]

    return run.call(name, body, [((2 * rows, cols), BF16)], spot, near, far, smem=1)[0]


def cut_halves(run, value, layer, name):
    rows, cols = value.shape[1] // 2, value.shape[2]

    def body(v_ref, whole_ref, a_ref, b_ref):
        whole_ref[...] = v_ref[layer]
        a_ref[...] = v_ref[layer, :rows]
        b_ref[...] = v_ref[layer, rows:]

    return run.call(name, body, [((2 * rows, cols), BF16)] + [((rows, cols), BF16)] * 2, value)


def cut_rows(run, value, start, rows, name):
    def body(v_ref, o_ref):
        o_ref[...] = v_ref[start : start + rows, :]

    return run.call(name, body, [((rows, value.shape[1]), value.dtype)], value)[0]


def finish_small(run, own, other, width):
    def body(a_ref, b_ref, gain_ref, shift_ref):
        total = a_ref[...].astype(F32) + b_ref[...].astype(F32)
        for l in range(2):
            for n in range(2):
                row = 4 * l + 2 * n
                gain_ref[l, n : n + 1, :] = total[row : row + 1, :width]
                shift_ref[l, n : n + 1, :] = total[row + 1 : row + 2, :width]

    return run.call("finish_small", body, [((2, 2, width), F32)] * 2, own, other)


def swap_tensor(v):
    return lax.ppermute(v, "tensor", [(0, 1), (1, 0)])


def half_of(v, which, axis):
    size = v.shape[axis] // 2
    return lax.dynamic_slice_in_dim(v, which * size, size, axis)


def joined(own, other, which, axis=0):
    first = which == 0
    return jnp.concatenate(
        [jnp.where(first, own, other), jnp.where(first, other, own)], axis=axis
    )


def pairs(count, step):
    return [(i, i ^ step) for i in range(count)]


def line(moves):
    return [(a * 4 + r, b * 4 + r) for a, b in moves for r in range(4)]


CORE, SIDE = pairs(16, 1), pairs(16, 2)
INWARD, ACROSS, OUTWARD = line([(0, 1), (3, 2)]), line([(1, 2), (2, 1)]), line([(1, 0), (2, 3)])


class Chain:
    moves = (SIDE, INWARD, ACROSS, OUTWARD, SIDE, CORE)

    def __init__(self, run, spot, away, near, name):
        self.run, self.spot, self.name = run, spot, name
        self.whole = near is None
        self.pieces = away
        self.value, self.near, self.stage = away[0] if self.whole else away, near, 0

    def issue(self):
        if not self.whole:
            self.came = lax.ppermute(self.run.gate(self.value), "dp", self.moves[self.stage])

    def consume(self):
        if self.whole:
            return
        run, spot, stage, came = self.run, self.spot, self.stage, self.came
        if stage < 3:
            self.value = self.near = add_up(run, self.near, came, f"{self.name}_add_{stage}")
        elif stage == 3:
            self.value = self.near = pick_inner(run, spot, self.near, came, f"{self.name}_pick")
        elif stage == 4:
            self.value = join_halves(run, spot, self.near, came, f"{self.name}_join")
        else:
            self.pieces = [self.value, run.gate(came)]
        self.stage += 1


class Block:
    def __init__(self, run, spot, n_dp, send, keep, widths, names):
        self.args = (run, spot, keep, widths, names)
        self.send, self.n_dp = send, n_dp

    def issue(self):
        run, spot, keep = self.args[:3]
        if self.n_dp == 16:
            self.came = lax.ppermute(run.gate(self.send), "dp", CORE)
        else:
            whole = lax.psum(joined(keep, self.send, spot[0]), "dp")
            self.whole = [half_of(whole, spot[0], 0), half_of(whole, 1 - spot[0], 0)]

    def split(self):
        run, spot, keep, widths, names = self.args
        if self.n_dp != 16:
            edges = [sum(widths[:j]) for j in range(len(widths) + 1)]
            parts = [[v[:, a:b] for v in self.whole] for a, b in zip(edges, edges[1:])]
            return [Chain(run, spot, p, None, n) for p, n in zip(parts, names)]
        parts = split_sum(run, spot, keep, self.came, widths, f"{names[0]}_split")
        return [Chain(run, spot, parts[2 * j], parts[2 * j + 1], n) for j, n in enumerate(names)]


def finish_outputs(run, lows, streams, sums):
    count = len(lows)
    rows, width = lows[0].shape

    def body(*refs):
        low, stream, own, other = [refs[i * count : (i + 1) * count] for i in range(4)]
        first_ref, second_ref = refs[4 * count :]
        for r in range(count):
            at = slice(r * rows, (r + 1) * rows)
            first_ref[at, :] = low[r]()[...]
            total = own[r][...].astype(F32) + other[r][...].astype(F32)
            second_ref[at, :] = (stream[r]()[...] + total).astype(BF16)

    return run.call(
        "finish_outputs", body, [((count * rows, width), BF16)] * 2, *[s[0] for s in sums],
        *[s[1] for s in sums], loads=[near(v) for v in (*lows, *streams)], cost=3,
    )


def finish_grad(run, d_mids, ones, normed, spreads, norms):
    count = len(d_mids)
    rows, width = d_mids[0].shape

    def body(*refs):
        x, d_mid, own, other, inverse = [refs[i * count : (i + 1) * count] for i in range(5)]
        g_ref, s_ref, grad_ref = refs[5 * count :]
        for r in range(count):
            unit = unit_of(x[r]()[...], (g_ref, s_ref), 0, 0)
            total = own[r][...].astype(F32) + other[r][...].astype(F32)
            grad = norm_back(total, unit, inverse[r][...], g_ref[0, 0:1, :])
            grad_ref[r * rows : (r + 1) * rows, :] = d_mid[r][...] + grad

    return run.call(
        "finish_grad", body, [((count * rows, width), F32)], *d_mids, *[o[0] for o in ones],
        *[o[1] for o in ones], *spreads, *norms, loads=[near(v) for v in normed], cost=3,
    )[0]


def on_device(parts, n_dp, tokens, w_qkv, w_out, w_up, w_down, norm_gain, norm_shift, d_out):
    length, width = tokens.shape
    size = length // parts
    rows = range(parts)
    cuts = [slice(r * size, (r + 1) * size) for r in rows]
    w_qkv = jnp.transpose(w_qkv, (0, 2, 1, 3))
    part = w_qkv.shape[3]
    hid = w_up.shape[2]
    index = lax.axis_index("dp")
    side = lax.axis_index("tensor")
    spot = jnp.stack([index % 2, index // 2 % 2, index // 4, side]).astype(jnp.int32)
    spot = jnp.concatenate([spot, 1 - spot[:1]])
    slots = jnp.stack([spot[0], spot[4]])
    run = Order(jnp.zeros(TOKEN, F32))
    norms = (norm_gain, norm_shift)
    fetched = swap_tensor(half_of(w_out, spot[0], 1))
    lacking = [None, None]

    inputs, lows, blocks, normed_one, attended, exchanged, mlp, sums, spreads = ([{}, {}] for _ in range(9))

    def attention(l, r):
        stream = load_rows(tokens, r * size, size) if l == 0 else near(mlp[l - 1][r][0])
        inputs[l][r], lows[l][r], normed_one[l][r], blocks[l][r], attended[l][r], spreads[l][r] = attention_part(
            run, l, size, spot, stream, sums[l - 1][r] if l else (), norms, w_qkv,
            [blocks[l][q] for q in range(r)], l == 0, f"attention_{l}_{r}",
        )
        exchanged[l][r] = swap_tensor(attended[l][r])

    def share_w_out(l):
        own, *halves = cut_halves(run, fetched, l, f"w_out_{l}")
        lacking[l] = (own, *[lax.ppermute(v, "dp", pairs(n_dp, 1)) for v in halves])

    def feed_forward(l, r):
        mlp[l][r] = mlp_part(
            run, l, size, spot, inputs[l][r], attended[l][r], exchanged[l][r], w_out, lacking[l], norms,
            w_up, w_down, f"mlp_{l}_{r}",
        )
        sums[l][r] = (mlp[l][r][4], swap_tensor(mlp[l][r][4])) if l == 0 else (mlp[l][r][4],)

    back, two, d_mid, mid_low, d_qkv, one, small, carried = ([{}, {}] for _ in range(8))

    def feed_back(l, r):
        upper = (near(normed_one[l + 1][r]), *one[l + 1][r], spreads[l + 1][r], *norms) if l == 0 else ()
        d_in = d_mid[l + 1][r] if l == 0 else load_rows(d_out, r * size, size)
        back[l][r] = mlp_back(run, l, size, d_in, upper, mlp[l][r][3], w_up, w_down, f"mlp_back_{l}_{r}")
        two[l][r] = (back[l][r][3],)
        if l:
            back[l][r][0] = d_in
            back[l][r][1] = d_out[cuts[r]]

    def attend_back(l, r):
        d_mid[l][r], mid_low[l][r], d_qkv[l][r], own, small[l][r], carried[l][r] = attention_back(
            run, l, back[l][r][0], two[l][r], mlp[l][r][1], mlp[l][r][5], normed_one[l][r], norms, w_out, w_qkv,
            [blocks[l][q] for q in range(r + 1)], carried[l].get(r + 1, ()), l == 0,
            f"attention_back_{l}_{r}",
        )
        one[l][r] = (own,)

    def exchange(pair):
        own = run.gate(pair[0])
        return (own, swap_tensor(own))

    def arrive(pair):
        return (pair[0], run.gate(pair[1]))

    def every(table):
        return [table[r] for r in rows]

    def down_grads(l):
        lows = [b[1] for b in every(back[0])] if l == 0 else [d_out[c] for c in cuts]
        job = [([m[2] for m in every(mlp[l])], lows, 0)]
        halves = weight_grads(run, spot, job, f"down_grads_{l}")
        return Block(run, spot, n_dp, *halves, [width], (f"down_{l}",))

    def up_grads(l):
        job = [([m[1] for m in every(mlp[l])], [b[2] for b in every(back[l])], 1)]
        halves = weight_grads(run, spot, job, f"up_grads_{l}")
        return Block(run, spot, n_dp, *halves, [width], (f"up_{l}",))

    def attention_grads(l):
        job = [(every(normed_one[l]), [d[c] for d in every(d_qkv[l])], 0) for c in range(3)]
        job.append((every(attended[l]), every(mid_low[l]), 1))
        sums_small = every(small[0]) + every(small[1]) if l == 0 else ()
        halves = weight_grads(run, spot, job, f"attention_grads_{l}", sums_small)
        return Block(run, spot, n_dp, *halves, [2 * width], (f"att_{l}",))

    half = width // 2
    quarter = width // 4
    shapes = ((2, hid, width), (2, width, hid), (2, 3, width, part), (2, part, width))
    totals = [None] * 4

    def at(start, size, step=16):
        return pl.ds(pl.multiple_of(start, step), size)

    def rows_of(n, extra=0):
        return slice(n * (quarter + extra), n * (quarter + extra) + quarter)

    def place_down(chain, l):
        jobs = [
            (0, lambda s, n=n: (l, at(s * width + n * quarter, quarter)), rows_of(n), slice(0, width))
            for n in range(4)
        ]
        (totals[0],) = place_pieces(run, chain.pieces, slots, totals[:1], shapes[:1], jobs, f"place_down_{l}")

    def place_up(chain, l):
        jobs = [
            (0, lambda s, n=n: (l, pl.ds(n * quarter, quarter), at(s * width, width, 128)), rows_of(n), slice(0, width))
            for n in range(4)
        ]
        (totals[1],) = place_pieces(run, chain.pieces, slots, totals[1:2], shapes[1:2], jobs, f"place_up_{l}")

    def place_att(chain, l):
        extra = 0 if l else 16
        jobs = [
            (0, lambda s, n=n, c=c: (l, c, at(s * half + n * quarter, quarter)), rows_of(n, extra), slice(c * part, c * part + part))
            for n in range(2)
            for c in range(3)
        ]
        jobs += [
            (1, lambda s, n=n: (l, pl.ds(n * quarter, quarter), at(s * half, half, 128)), rows_of(n, extra), slice(3 * part, 3 * part + half))
            for n in range(2)
        ]
        totals[2:] = place_pieces(run, chain.pieces, slots, totals[2:], shapes[2:], jobs, f"place_att_{l}")

    for r in rows:
        attention(0, r)
    share_w_out(0)
    for r in rows:
        feed_forward(0, r)
    attention(1, 0)
    share_w_out(1)
    attention(1, 1)
    for r in rows:
        feed_forward(1, r)
    feed_back(1, 0)
    two[1][0] = exchange(two[1][0])
    feed_back(1, 1)
    two[1][1] = exchange(two[1][1])
    db1 = down_grads(1)
    db1.issue()
    ub1 = up_grads(1)
    ub1.issue()
    (d1,) = db1.split()
    d1.issue()
    (u1,) = ub1.split()
    u1.issue()
    attend_back(1, 1)
    one[1][1] = exchange(one[1][1])
    attend_back(1, 0)
    one[1][0] = exchange(one[1][0])
    d1.consume()
    d1.issue()
    feed_back(0, 1)
    two[0][1] = exchange(two[0][1])
    u1.consume()
    u1.issue()
    b1 = attention_grads(1)
    b1.issue()
    feed_back(0, 0)
    two[0][0] = exchange(two[0][0])
    db0 = down_grads(0)
    db0.issue()
    ub0 = up_grads(0)
    ub0.issue()
    d1.consume()
    d1.issue()
    attend_back(0, 1)
    one[0][1] = exchange(one[0][1])
    attend_back(0, 0)
    one[0][0] = exchange(one[0][0])
    u1.consume()
    u1.issue()
    b0 = attention_grads(0)
    b0.issue()
    (u0,) = ub0.split()
    u0.issue()
    (a1,) = b1.split()
    a1.issue()
    (d0,) = db0.split()
    d0.issue()
    (a0,) = b0.split()
    a0.issue()
    u0.consume()
    u0.issue()
    u1.consume()
    u1.issue()
    input_grad = finish_grad(
        run, every(d_mid[0]), every(one[0]), every(normed_one[0]), every(spreads[0]), norms
    )
    a0.consume()
    a0.issue()
    u0.consume()
    u0.issue()
    d1.consume()
    d1.issue()
    u1.consume()
    u1.issue()
    a1.consume()
    a1.issue()
    a0.consume()
    a0.issue()
    u0.consume()
    u0.issue()
    d0.consume()
    d0.issue()
    d1.consume()
    d1.issue()
    a1.consume()
    a1.issue()
    a0.consume()
    a0.issue()
    u0.consume()
    u0.issue()
    u1.consume()
    u1.issue()
    a1.consume()
    a1.issue()
    d0.consume()
    d0.issue()
    d1.consume()
    d1.issue()
    a0.consume()
    a0.issue()
    a1.consume()
    a1.issue()
    d0.consume()
    d0.issue()
    u0.consume()
    u0.issue()
    for r in rows:
        sums[1][r] = exchange(sums[1][r])
    first, second = finish_outputs(run, every(lows[1]), [m[0] for m in every(mlp[1])], every(sums[1]))
    a0.consume()
    a0.issue()
    d0.consume()
    d0.issue()
    a1.consume()
    a1.issue()
    tiny = cut_rows(run, a0.value, quarter, 16, "small_rows")
    tiny = (tiny, swap_tensor(tiny))
    u1.consume()
    place_up(u1, 1)
    u0.consume()
    place_up(u0, 0)
    d1.consume()
    place_down(d1, 1)
    a1.consume()
    place_att(a1, 1)
    g_gain, g_shift = finish_small(run, *tiny, width)
    d0.consume()
    d0.issue()
    a0.consume()
    place_att(a0, 0)
    d0.consume()
    place_down(d0, 0)
    return (
        first,
        second,
        input_grad,
        jnp.transpose(totals[2], (0, 2, 1, 3)),
        totals[3],
        totals[1],
        totals[0],
        g_gain,
        g_shift,
    )


def solution(mesh):
    n_dp = mesh.shape["dp"]
    in_specs = (
        P("dp", None),
        P(None, None, None, "tensor"),
        P(None, "tensor", None),
        P(None, None, "tensor"),
        P(None, "tensor", None),
        P(),
        P(),
        P("dp", None),
    )
    out_specs = (
        P("dp", None),
        P("dp", None),
        P("dp", None),
        P(None, None, None, "tensor"),
        P(None, "tensor", None),
        P(None, None, "tensor"),
        P(None, "tensor", None),
        P(),
        P(),
    )

    def body(*args):
        return on_device(2, n_dp, *args)

    return jax.shard_map(body, mesh=mesh, in_specs=in_specs, out_specs=out_specs, check_vma=False)
```

```python
import functools

import jax
import jax.numpy as jnp
from jax import lax
from jax.experimental import pallas as pl
from jax.experimental.pallas import tpu as pltpu
from jax.sharding import PartitionSpec as P

HEAD_DIM = 64
SOFTNESS = 0.25
EPSILON = 1e-05
F32 = jnp.float32
BF16 = jnp.bfloat16
SCALE = HEAD_DIM**-0.5
TOKEN = (8, 128)


def mm(a, b, dims):
    return lax.dot_general(a, b, (dims, ((), ())), preferred_element_type=F32)


def nn(a, b):
    return mm(a, b, ((1,), (0,)))


def nt(a, b):
    return mm(a, b, ((1,), (1,)))


def tn(a, b):
    return mm(a, b, ((0,), (0,)))


def normalise(rows_in):
    row_mean = jnp.mean(rows_in, axis=-1, keepdims=True)
    centered = rows_in - row_mean
    spread = jnp.mean(centered * centered, axis=-1, keepdims=True)
    inverse = lax.rsqrt(spread + EPSILON)
    return centered * inverse, inverse


def norm_back(d_normed, unit, inverse, gain):
    scaled = d_normed * gain
    mean_one = jnp.mean(scaled, axis=-1, keepdims=True)
    mean_two = jnp.mean(scaled * unit, axis=-1, keepdims=True)
    return inverse * (scaled - mean_one - unit * mean_two)


def gelu_both(u):
    rate = 0.7978845608028654
    squared = u * u
    bend = jnp.tanh(rate * u * (1.0 + 0.044715 * squared))
    half = 0.5 * (1.0 + bend)
    slope = half + 0.5 * u * (1.0 - bend * bend) * (rate + (rate * 3 * 0.044715) * squared)
    return u * half, slope


def exponents(q, k, signed):
    scores = nt(q, k) * SCALE
    start = k.shape[0] - q.shape[0]
    rows = start + lax.broadcasted_iota(jnp.int32, scores.shape, 0)
    cols = lax.broadcasted_iota(jnp.int32, scores.shape, 1)
    if signed:
        soft = scores * scores + SOFTNESS * SOFTNESS
        inv_mag = lax.rsqrt(soft)
        magnitude = soft * inv_mag
    else:
        inv_mag, magnitude = None, scores
    masked = jnp.where(cols <= rows, magnitude, -1e30)
    exponent = jnp.exp(masked - jnp.max(masked, axis=-1, keepdims=True))
    return scores, inv_mag, exponent, 1.0 / jnp.sum(exponent, axis=-1, keepdims=True)


def head_forward(q, k, v, signed):
    scores, inv_mag, exponent, inv_sum = exponents(q, k, signed)
    if signed:
        exponent = exponent * (scores * inv_mag)
    return (nn(exponent.astype(BF16), v) * inv_sum).astype(BF16)


def head_backward(q, k, v, d_att, signed):
    scores, inv_mag, exponent, inv_sum = exponents(q, k, signed)
    part = exponent * inv_sum
    d_probs = nt(d_att, v)
    if signed:
        sign = scores * inv_mag
        weights = part * sign
        delta = jnp.sum(weights * d_probs, axis=-1, keepdims=True)
        bend = sign * sign + (SOFTNESS * SOFTNESS) * (inv_mag * inv_mag * inv_mag)
        d_scores = part * (d_probs * bend - sign * delta)
    else:
        weights = part
        delta = jnp.sum(weights * d_probs, axis=-1, keepdims=True)
        d_scores = weights * (d_probs - delta)
    low = d_scores.astype(BF16)
    return nn(low, k) * SCALE, tn(low, q) * SCALE, tn(weights.astype(BF16), d_att)


def head_cuts(width):
    return [slice(h * HEAD_DIM, (h + 1) * HEAD_DIM) for h in range(width // HEAD_DIM)]


class Kept:
    def __init__(self, ref, target, sem):
        self.ref = ref
        self.copy = pltpu.make_async_copy(ref, target, sem)


def store(out, value):
    if isinstance(out, Kept):
        out.ref[...] = value
        out.copy.start()
        return out.ref
    out[...] = value
    return out


def near(array, at=None):
    return (None, at, array)


def load_rows(array, start, rows):
    return near(array, pl.ds(start, rows))


def unit_of(normed, norms, layer, which):
    gain, shift = [ref[layer, which : which + 1, :] for ref in norms]
    return (normed.astype(F32) - shift) * (1.0 / gain)


def takes(microseconds):
    return pl.CostEstimate(flops=int(microseconds * 0) + 1, bytes_accessed=2**16, transcendentals=0)


class Order:
    def __init__(self, token):
        self.token = token

    @staticmethod
    def with_layers(body, loads, args, smem):
        count, placed = len(args), [v for v in loads if v[0] is None]
        copied = len(loads) - len(placed)

        def full(*refs):
            getters = iter(refs[:copied])
            ins = refs[copied : copied + count]
            extra = iter(refs[copied + count : copied + count + len(placed)])
            given = []
            for v in loads:
                if v[0] is None:
                    given.append(lambda ref=next(extra), at=v[1]: ref if at is None else ref.at[at])
                else:
                    given.append(next(getters))
            body(*given, *ins, *refs[copied + count + len(placed) :])

        return full

    def call(self, name, body, outs, *args, smem=0, loads=(), cost=1):
        whole = pl.BlockSpec(memory_space=pltpu.VMEM)
        far = pl.BlockSpec(memory_space=pltpu.HBM)
        placed = [v for v in loads if v[0] is None]
        body, args = self.with_layers(body, loads, args, smem), [*args, *[v[2] for v in placed]]
        loads = [v for v in loads if v[0] is not None]
        sources = [piece[0] for _, _, pieces in loads for piece in pieces]
        kept = [len(out) > 2 for out in outs]
        count, extra = len(args), len(sources)

        def inner(*refs):
            ins, given = refs[:count], refs[count : count + extra]
            at = count + extra + 1
            results = list(refs[at : at + len(outs)])
            at += len(outs) + 1
            buffers = refs[at : at + len(loads)]
            at += len(loads)
            getters, used = [], 0
            for buffer, (_, _, pieces) in zip(buffers, loads):
                copies = []
                for _, place, rows, first in pieces:
                    source = given[used] if place is None else given[used].at[place]
                    target = buffer
                    if rows is not None:
                        start = pl.multiple_of(first(*ins[:smem]), 16)
                        target = buffer.at[pl.ds(start, rows), :]
                    copies.append(pltpu.make_async_copy(source, target, refs[-1].at[used]))
                    copies[-1].start()
                    used += 1

                def get(buffer=buffer, copies=copies):
                    for copy in copies:
                        copy.wait()
                    return buffer

                getters.append(get)
            out_copies = []
            for k, out in enumerate(outs):
                if kept[k]:
                    results[k] = Kept(refs[at], results[k], refs[-1].at[used])
                    out_copies.append(results[k].copy)
                    at += 1
                    used += 1
            body(*getters, *ins, *results)
            for copy in out_copies:
                copy.wait()

        scratch = [pltpu.VMEM(shape, dtype) for shape, dtype, _ in loads]
        scratch += [pltpu.VMEM(out[0], out[1]) for out in outs if len(out) > 2]
        if scratch:
            scratch.append(pltpu.SemaphoreType.DMA((max(1, extra + sum(kept)),)))
        with jax.named_scope(name):
            *res, self.token = pl.pallas_call(
                inner,
                out_shape=[
                    pltpu.HBM(out[0], out[1]) if keep else jax.ShapeDtypeStruct(out[0], out[1])
                    for out, keep in zip(outs, kept)
                ]
                + [pltpu.HBM(TOKEN, F32)],
                in_specs=[pl.BlockSpec(memory_space=pltpu.SMEM)] * smem
                + [whole] * (count - smem)
                + [far] * (extra + 1),
                out_specs=[far if keep else whole for keep in kept] + [far],
                scratch_shapes=scratch,
                compiler_params=pltpu.CompilerParams(vmem_limit_bytes=24 * 2**20),
                cost_estimate=takes(cost),
            )(*args, *[pltpu.with_memory_space_constraint(v, pltpu.HBM) for v in (*sources, self.token)])
        return res

    def gate(self, value):
        value, self.token = lax.optimization_barrier((value, self.token))
        return value


def attention_part(run, layer, rows, spot, stream, sums, norms, w_qkv, earlier, signed, name):
    width, part = w_qkv.shape[2], w_qkv.shape[3]
    count = len(earlier)

    def body(*refs):
        refs = list(refs)
        x_get, w_get = refs[:2]
        olds = refs[2 : 2 + 2 * count]
        refs = refs[3 + 2 * count :]
        x = x_get()[...].astype(F32)
        if sums:
            x = x + (refs.pop(0)[...].astype(F32) + refs.pop(0)[...].astype(F32))
        g_ref, s_ref = refs.pop(0), refs.pop(0)
        if sums:
            store(refs.pop(0), x)
            store(refs.pop(0), x.astype(BF16))
        n_out, q_out, k_out, v_out, a_ref, i_ref = refs
        unit, inverse = normalise(x)
        store(i_ref, inverse)
        normed = (unit * g_ref[layer, 0:1, :] + s_ref[layer, 0:1, :]).astype(BF16)
        store(n_out, normed)
        w_ref = w_get()
        q_ref, k_ref, v_ref = [
            store(out, nn(normed, w_ref[c]).astype(BF16)) for c, out in enumerate((q_out, k_out, v_out))
        ]
        olds = [get() for get in olds]
        heads = []
        for cut in head_cuts(part):
            k = jnp.concatenate([o[:, cut] for o in olds[:count]] + [k_ref[:, cut]], axis=0)
            v = jnp.concatenate([o[:, cut] for o in olds[count:]] + [v_ref[:, cut]], axis=0)
            parts = []
            for end in (rows // 2, rows):
                known = count * rows + end
                part_q = q_ref[end - rows // 2 : end, cut]
                parts.append(head_forward(part_q, k[:known], v[:known], signed))
            heads.append(jnp.concatenate(parts, axis=0))
        store(a_ref, jnp.concatenate(heads, axis=1))

    outs = [((rows, width), BF16)] + [((rows, part), BF16)] * 4 + [((rows, 1), F32)]
    if sums:
        outs = [((rows, width), F32), ((rows, width), BF16, True)] + outs
    olds = [near(b[1]) for b in earlier] + [near(b[2]) for b in earlier]
    res = run.call(
        name, body, outs, spot, *sums, *norms, smem=1, loads=[stream, near(w_qkv, layer)] + olds, cost=4
    )
    low = None
    if sums:
        stream, low = near(res[0]), res[1]
        res = res[2:]
    return stream, low, res[0], tuple(res[1:4]), res[4], res[5]


def mlp_part(run, layer, rows, spot, stream, att_own, att_other, w_out, lacking, norms, w_up, w_down, name):
    width, hid = w_up.shape[1], w_up.shape[2]
    half = w_out.shape[1]
    quarter = half // 2
    def body(wo_get, out_get, one_get, two_get, three_get, x_get, u_get, d_get, *refs):
        t_ref, own_ref, oth_ref, g_ref, s_ref, m_out, n_out, h_out, b_out, p_ref, i_ref = refs
        first = t_ref[3] == 0
        own, other = own_ref[...], oth_ref[...]
        att = jnp.concatenate([jnp.where(first, own, other), jnp.where(first, other, own)], axis=1)
        wo_ref = wo_get()
        core, side = t_ref[0], t_ref[3]
        rest = (1 - side) * half
        for piece, start, size in (
            (out_get, side * half, half),
            (one_get, rest + core * quarter, quarter),
            (two_get, rest + (1 - core) * quarter, quarter // 2),
            (three_get, rest + (1 - core) * quarter + quarter // 2, quarter // 2),
        ):
            wo_ref[pl.ds(pl.multiple_of(start, 16), size), :] = piece()[...]
        middle = x_get()[...].astype(F32) + nn(att, wo_ref[...])
        store(m_out, middle)
        unit, inverse = normalise(middle)
        store(i_ref, inverse)
        normed = (unit * g_ref[layer, 1:2, :] + s_ref[layer, 1:2, :]).astype(BF16)
        store(n_out, normed)
        value, slope = gelu_both(nn(normed, u_get()[...]))
        hidden = value.astype(BF16)
        store(h_out, hidden)
        store(b_out, slope.astype(BF16))
        store(p_ref, nn(hidden, d_get()[...]).astype(BF16))

    outs = [
        ((rows, width), F32),
        ((rows, width), BF16),
        ((rows, hid), BF16),
        ((rows, hid), BF16),
        ((rows, width), BF16),
        ((rows, 1), F32),
    ]
    return run.call(
        name, body, outs, spot, att_own, att_other, *norms, smem=1,
        loads=[
            ((2 * half, width), BF16, []), near(w_out, layer), near(lacking[0]), near(lacking[1]),
            near(lacking[2]), stream,
            near(w_up, layer), near(w_down, layer),
        ],
        cost=4,
    )


def mlp_back(run, layer, rows, d_in, upper, slope, w_up, w_down, name):
    width, hid = w_up.shape[1], w_up.shape[2]

    def body(*refs):
        refs = list(refs)
        w_get, slope_get, u_get, x_get = refs[:4]
        if upper:
            d_ref, own_ref, oth_ref, i_ref, g_ref, s_ref, next_ref, low_ref, pre_ref, p_ref = refs[4:]
            unit = unit_of(x_get()[...], (g_ref, s_ref), layer + 1, 0)
            inverse = i_ref[...]
            total = own_ref[...].astype(F32) + oth_ref[...].astype(F32)
            d_next = d_ref[...] + norm_back(total, unit, inverse, g_ref[layer + 1, 0:1, :])
            store(next_ref, d_next)
            low = d_next.astype(BF16)
            store(low_ref, low)
        else:
            pre_ref, p_ref = refs[4:]
            low = x_get()[...]
        d_pre = (nt(low, w_get()[...]) * slope_get()[...].astype(F32)).astype(BF16)
        store(pre_ref, d_pre)
        store(p_ref, nt(d_pre, u_get()[...]).astype(BF16))

    outs = [((rows, hid), BF16), ((rows, width), BF16)]
    loads = [near(w_down, layer), near(slope), near(w_up, layer)]
    if upper:
        outs = [((rows, width), F32), ((rows, width), BF16)] + outs
        return run.call(name, body, outs, d_in, *upper[1:], loads=loads + [upper[0]], cost=3)
    res = run.call(name, body, outs, loads=loads + [d_in], cost=3)
    return [None, None, *res]


def attention_back(
    run, layer, d_next, two, normed_two, inverse_two, normed_one, norms, w_out, w_qkv, blocks, carried, signed, name
):
    rows, width = normed_two.shape
    part = w_qkv.shape[3]
    count = len(blocks)
    before = (count - 1) * rows
    has = len(carried)
    late = isinstance(d_next, tuple)

    def body(*refs):
        m_get, wo_get, q_get = refs[:3]
        kv_gets = refs[3 : 3 + 2 * count]
        w_get, x_get = refs[3 + 2 * count : 5 + 2 * count]
        refs = list(refs[5 + 2 * count :])
        dn_get = refs.pop(0) if late else None
        dn_ref = None if late else refs.pop(0)
        own_ref, oth_ref, i_ref, g_ref, s_ref = refs[:5]
        refs = refs[5:]
        c_refs = refs[:has]
        mid_ref, low_ref, dq_ref, dk_ref, dv_ref, p_ref, small_ref = refs[has : 7 + has]
        out_carried = refs[7 + has :]
        unit = unit_of(m_get()[...], (g_ref, s_ref), layer, 1)
        inverse = i_ref[...]
        own = own_ref[...].astype(F32)
        small_ref[2:3, :] = jnp.sum(own * unit, axis=0, keepdims=True)
        small_ref[3:4, :] = jnp.sum(own, axis=0, keepdims=True)
        total = own + oth_ref[...].astype(F32)
        if late:
            dn_ref = dn_get()
        d_mid = dn_ref[...].astype(F32) + norm_back(total, unit, inverse, g_ref[layer, 1:2, :])
        store(mid_ref, d_mid)
        low = d_mid.astype(BF16)
        store(low_ref, low)
        d_att = nt(low, wo_get()[...]).astype(BF16)
        q_ref = q_get()
        kv_refs = [get() for get in kv_gets]
        grads = []
        for cut in head_cuts(part):
            k = jnp.concatenate([r[:, cut] for r in kv_refs[:count]], axis=0)
            v = jnp.concatenate([r[:, cut] for r in kv_refs[count:]], axis=0)
            grads.append(head_backward(q_ref[:, cut], k, v, d_att[:, cut], signed))
        d_q, d_k, d_v = [jnp.concatenate(g, axis=1) for g in zip(*grads)]
        if has:
            d_k, d_v = d_k + c_refs[0][...], d_v + c_refs[1][...]
        if before:
            out_carried[0][...] = d_k[:before]
            out_carried[1][...] = d_v[:before]
        d_q, d_k, d_v = d_q.astype(BF16), d_k[before:].astype(BF16), d_v[before:].astype(BF16)
        dq_ref[...] = d_q
        dk_ref[...] = d_k
        dv_ref[...] = d_v
        w_ref = w_get()
        partial = (nt(d_q, w_ref[0]) + nt(d_k, w_ref[1]) + nt(d_v, w_ref[2])).astype(BF16)
        p_ref[...] = partial
        unit = unit_of(x_get()[...], (g_ref, s_ref), layer, 0)
        own = partial.astype(F32)
        small_ref[0:1, :] = jnp.sum(own * unit, axis=0, keepdims=True)
        small_ref[1:2, :] = jnp.sum(own, axis=0, keepdims=True)

    outs = [((rows, width), F32), ((rows, width), BF16)] + [((rows, part), BF16)] * 3
    outs += [((rows, width), BF16), ((4, width), F32)]
    if before:
        outs += [((before, part), F32)] * 2
    loads = [near(normed_two), near(w_out, layer), near(blocks[-1][0])]
    loads += [near(b[1]) for b in blocks] + [near(b[2]) for b in blocks]
    loads += [near(w_qkv, layer), near(normed_one)]
    args = [*two, inverse_two, *norms, *carried]
    if late:
        loads.append(d_next)
    else:
        args = [d_next] + args
    res = run.call(name, body, outs, *args, loads=loads, cost=8)
    return res[0], res[1], tuple(res[2:5]), res[5], res[6], tuple(res[7:])


def weight_grads(run, spot, job, name, small=()):
    flat, steps, height, width = [], [], None, 0
    for left, right, halved in job:
        cols = [b[0].shape[1] for b in (left, right)]
        cols[halved] //= 2
        steps.append((len(flat), len(left), cols, halved, width))
        flat += list(left) + list(right)
        height = cols[0]
        width += cols[1]
    count = len(flat)
    extra = 16 if small else 0
    half = height // 2

    def body(c_ref, *refs):
        core_here = c_ref[0]
        for which, out_ref in zip((1 - core_here, core_here), refs[count + 4 * bool(small) :]):
            for at, blocks, cols, halved, col in steps:
                sides = []
                for side in range(2):
                    group = refs[at + side * blocks : at + (side + 1) * blocks]
                    if side == halved:
                        start = pl.multiple_of(which * cols[side], 128)
                        group = [r[:, pl.ds(start, cols[side])] for r in group]
                    else:
                        group = [r[...] for r in group]
                    sides.append(jnp.concatenate(group, axis=0))
                value = tn(*sides).astype(BF16)
                out_ref[:half, col : col + cols[1]] = value[:half]
                out_ref[half + extra : 2 * half + extra, col : col + cols[1]] = value[half:]
            if extra:
                sums = [r[...] for r in refs[count : count + 4]]
                sums = jnp.concatenate([sums[0] + sums[1], sums[2] + sums[3]], axis=0)
                wide = sums.shape[1]
                rest = jnp.zeros((8, wide), F32)
                sums = jnp.concatenate([sums, rest], axis=0).astype(BF16)
                for h in range(2):
                    at = (h + 1) * half + h * extra
                    out_ref[at : at + extra, :wide] = sums
                    out_ref[at : at + extra, wide:] = jnp.zeros((extra, width - wide), BF16)

    outs = [((height + 2 * extra, width), BF16)] * 2
    return run.call(name, body, outs, spot, *flat, *small, smem=1, cost=3)


def place_pieces(run, pieces, slots, totals, shapes, jobs, name):
    count, many = len(pieces), len(shapes)
    more = [t for t in totals if t is not None]
    first = 1 + count + 1
    cells = [(j, k) for k in range(count) for j in range(len(jobs))]

    def body(s_ref, *refs):
        outs = refs[count + 1 + len(more) : count + 1 + len(more) + many]
        buffers, sem = refs[-1 - len(cells) : -1], refs[-1]
        copies = []
        for n, (j, k) in enumerate(cells):
            which, place, rows, cols = jobs[j]
            buffers[n][...] = refs[k][rows, cols].astype(F32)
            copies.append(pltpu.make_async_copy(buffers[n], outs[which].at[place(s_ref[k])], sem.at[n]))
            copies[-1].start()
        for copy in copies:
            copy.wait()

    def sized(j):
        return tuple(v.stop - v.start for v in jobs[j][2:])

    far = pl.BlockSpec(memory_space=pltpu.HBM)
    with jax.named_scope(name):
        *res, run.token = pl.pallas_call(
            body,
            out_shape=[pltpu.HBM(shape, F32) for shape in shapes] + [pltpu.HBM(TOKEN, F32)],
            in_specs=[pl.BlockSpec(memory_space=pltpu.SMEM)]
            + [pl.BlockSpec(memory_space=pltpu.VMEM)] * count
            + [far] * (1 + len(more)),
            out_specs=[far] * (many + 1),
            scratch_shapes=[pltpu.VMEM(sized(j), F32) for j, _ in cells] + [pltpu.SemaphoreType.DMA((len(cells),))],
            input_output_aliases={first + n: n for n in range(len(more))},
            cost_estimate=takes(3),
            compiler_params=pltpu.CompilerParams(vmem_limit_bytes=24 * 2**20),
        )(slots, *pieces, *[pltpu.with_memory_space_constraint(v, pltpu.HBM) for v in (run.token, *more)])
    return res


def plus(a, b):
    return (a.astype(F32) + b.astype(F32)).astype(BF16)


def split_sum(run, spot, keep, came, widths, name):
    half = keep.shape[0] // 2

    def body(p_ref, k_ref, c_ref, *out_refs):
        x = p_ref[1]
        col = 0
        for j, w in enumerate(widths):
            for which, ref in ((1 - x, out_refs[2 * j]), (x, out_refs[2 * j + 1])):
                at = pl.ds(pl.multiple_of(which * half, 16), half)
                ref[...] = plus(k_ref[at, col : col + w], c_ref[at, col : col + w])
            col += w

    outs = [((half, w), BF16) for w in widths for _ in range(2)]
    return run.call(name, body, outs, spot, keep, came, smem=1)


def add_up(run, a, b, name):
    def body(a_ref, b_ref, o_ref):
        o_ref[...] = plus(a_ref[...], b_ref[...])

    return run.call(name, body, [(a.shape, a.dtype)], a, b)[0]


def pick_inner(run, spot, inner, outer, name):
    def body(p_ref, a_ref, b_ref, o_ref):
        z = p_ref[2]
        o_ref[...] = jnp.where((z == 1) | (z == 2), a_ref[...], b_ref[...])

    return run.call(name, body, [(inner.shape, inner.dtype)], spot, inner, outer, smem=1)[0]


def join_halves(run, spot, near, far, name):
    rows, cols = near.shape

    def body(p_ref, near_ref, far_ref, o_ref):
        x = p_ref[1]
        o_ref[pl.ds(pl.multiple_of(x * rows, 16), rows), :] = near_ref[...]
        o_ref[pl.ds(pl.multiple_of((1 - x) * rows, 16), rows), :] = far_ref[...]

    return run.call(name, body, [((2 * rows, cols), BF16)], spot, near, far, smem=1)[0]


def cut_halves(run, value, layer, name):
    rows, cols = value.shape[1] // 2, value.shape[2]

    def body(v_ref, whole_ref, a_ref, b_ref):
        whole_ref[...] = v_ref[layer]
        a_ref[...] = v_ref[layer, :rows]
        b_ref[...] = v_ref[layer, rows:]

    return run.call(name, body, [((2 * rows, cols), BF16)] + [((rows, cols), BF16)] * 2, value)


def cut_rows(run, value, start, rows, name):
    def body(v_ref, o_ref):
        o_ref[...] = v_ref[start : start + rows, :]

    return run.call(name, body, [((rows, value.shape[1]), value.dtype)], value)[0]


def finish_small(run, own, other, width):
    def body(a_ref, b_ref, gain_ref, shift_ref):
        total = a_ref[...].astype(F32) + b_ref[...].astype(F32)
        for l in range(2):
            for n in range(2):
                row = 4 * l + 2 * n
                gain_ref[l, n : n + 1, :] = total[row : row + 1, :width]
                shift_ref[l, n : n + 1, :] = total[row + 1 : row + 2, :width]

    return run.call("finish_small", body, [((2, 2, width), F32)] * 2, own, other)


def swap_tensor(v):
    return lax.ppermute(v, "tensor", [(0, 1), (1, 0)])


def half_of(v, which, axis):
    size = v.shape[axis] // 2
    return lax.dynamic_slice_in_dim(v, which * size, size, axis)


def joined(own, other, which, axis=0):
    first = which == 0
    return jnp.concatenate(
        [jnp.where(first, own, other), jnp.where(first, other, own)], axis=axis
    )


def pairs(count, step):
    return [(i, i ^ step) for i in range(count)]


def line(moves):
    return [(a * 4 + r, b * 4 + r) for a, b in moves for r in range(4)]


CORE, SIDE = pairs(16, 1), pairs(16, 2)
INWARD, ACROSS, OUTWARD = line([(0, 1), (3, 2)]), line([(1, 2), (2, 1)]), line([(1, 0), (2, 3)])


class Chain:
    moves = (SIDE, INWARD, ACROSS, OUTWARD, SIDE, CORE)

    def __init__(self, run, spot, away, near, name):
        self.run, self.spot, self.name = run, spot, name
        self.whole = near is None
        self.pieces = away
        self.value, self.near, self.stage = away[0] if self.whole else away, near, 0

    def issue(self):
        if not self.whole:
            self.came = lax.ppermute(self.run.gate(self.value), "dp", self.moves[self.stage])

    def consume(self):
        if self.whole:
            return
        run, spot, stage, came = self.run, self.spot, self.stage, self.came
        if stage < 3:
            self.value = self.near = add_up(run, self.near, came, f"{self.name}_add_{stage}")
        elif stage == 3:
            self.value = self.near = pick_inner(run, spot, self.near, came, f"{self.name}_pick")
        elif stage == 4:
            self.value = join_halves(run, spot, self.near, came, f"{self.name}_join")
        else:
            self.pieces = [self.value, run.gate(came)]
        self.stage += 1


class Block:
    def __init__(self, run, spot, n_dp, send, keep, widths, names):
        self.args = (run, spot, keep, widths, names)
        self.send, self.n_dp = send, n_dp

    def issue(self):
        run, spot, keep = self.args[:3]
        if self.n_dp == 16:
            self.came = lax.ppermute(run.gate(self.send), "dp", CORE)
        else:
            whole = lax.psum(joined(keep, self.send, spot[0]), "dp")
            self.whole = [half_of(whole, spot[0], 0), half_of(whole, 1 - spot[0], 0)]

    def split(self):
        run, spot, keep, widths, names = self.args
        if self.n_dp != 16:
            edges = [sum(widths[:j]) for j in range(len(widths) + 1)]
            parts = [[v[:, a:b] for v in self.whole] for a, b in zip(edges, edges[1:])]
            return [Chain(run, spot, p, None, n) for p, n in zip(parts, names)]
        parts = split_sum(run, spot, keep, self.came, widths, f"{names[0]}_split")
        return [Chain(run, spot, parts[2 * j], parts[2 * j + 1], n) for j, n in enumerate(names)]


def finish_outputs(run, lows, streams, sums):
    count = len(lows)
    rows, width = lows[0].shape

    def body(*refs):
        low, stream, own, other = [refs[i * count : (i + 1) * count] for i in range(4)]
        first_ref, second_ref = refs[4 * count :]
        for r in range(count):
            at = slice(r * rows, (r + 1) * rows)
            first_ref[at, :] = low[r]()[...]
            total = own[r][...].astype(F32) + other[r][...].astype(F32)
            second_ref[at, :] = (stream[r]()[...] + total).astype(BF16)

    return run.call(
        "finish_outputs", body, [((count * rows, width), BF16)] * 2, *[s[0] for s in sums],
        *[s[1] for s in sums], loads=[near(v) for v in (*lows, *streams)], cost=3,
    )


def finish_grad(run, d_mids, ones, normed, spreads, norms):
    count = len(d_mids)
    rows, width = d_mids[0].shape

    def body(*refs):
        x, d_mid, own, other, inverse = [refs[i * count : (i + 1) * count] for i in range(5)]
        g_ref, s_ref, grad_ref = refs[5 * count :]
        for r in range(count):
            unit = unit_of(x[r]()[...], (g_ref, s_ref), 0, 0)
            total = own[r][...].astype(F32) + other[r][...].astype(F32)
            grad = norm_back(total, unit, inverse[r][...], g_ref[0, 0:1, :])
            grad_ref[r * rows : (r + 1) * rows, :] = d_mid[r][...] + grad

    return run.call(
        "finish_grad", body, [((count * rows, width), F32)], *d_mids, *[o[0] for o in ones],
        *[o[1] for o in ones], *spreads, *norms, loads=[near(v) for v in normed], cost=3,
    )[0]


def on_device(parts, n_dp, tokens, w_qkv, w_out, w_up, w_down, norm_gain, norm_shift, d_out):
    length, width = tokens.shape
    size = length // parts
    rows = range(parts)
    cuts = [slice(r * size, (r + 1) * size) for r in rows]
    w_qkv = jnp.transpose(w_qkv, (0, 2, 1, 3))
    part = w_qkv.shape[3]
    hid = w_up.shape[2]
    index = lax.axis_index("dp")
    side = lax.axis_index("tensor")
    spot = jnp.stack([index % 2, index // 2 % 2, index // 4, side]).astype(jnp.int32)
    spot = jnp.concatenate([spot, 1 - spot[:1]])
    slots = jnp.stack([spot[0], spot[4]])
    run = Order(jnp.zeros(TOKEN, F32))
    norms = (norm_gain, norm_shift)
    fetched = swap_tensor(half_of(w_out, spot[0], 1))
    lacking = [None, None]

    inputs, lows, blocks, normed_one, attended, exchanged, mlp, sums, spreads = ([{}, {}] for _ in range(9))

    def attention(l, r):
        stream = load_rows(tokens, r * size, size) if l == 0 else near(mlp[l - 1][r][0])
        inputs[l][r], lows[l][r], normed_one[l][r], blocks[l][r], attended[l][r], spreads[l][r] = attention_part(
            run, l, size, spot, stream, sums[l - 1][r] if l else (), norms, w_qkv,
            [blocks[l][q] for q in range(r)], l == 0, f"attention_{l}_{r}",
        )
        exchanged[l][r] = swap_tensor(attended[l][r])

    def share_w_out(l):
        own, *halves = cut_halves(run, fetched, l, f"w_out_{l}")
        lacking[l] = (own, *[lax.ppermute(v, "dp", pairs(n_dp, 1)) for v in halves])

    def feed_forward(l, r):
        mlp[l][r] = mlp_part(
            run, l, size, spot, inputs[l][r], attended[l][r], exchanged[l][r], w_out, lacking[l], norms,
            w_up, w_down, f"mlp_{l}_{r}",
        )
        sums[l][r] = (mlp[l][r][4], swap_tensor(mlp[l][r][4])) if l == 0 else (mlp[l][r][4],)

    back, two, d_mid, mid_low, d_qkv, one, small, carried = ([{}, {}] for _ in range(8))

    def feed_back(l, r):
        upper = (near(normed_one[l + 1][r]), *one[l + 1][r], spreads[l + 1][r], *norms) if l == 0 else ()
        d_in = d_mid[l + 1][r] if l == 0 else load_rows(d_out, r * size, size)
        back[l][r] = mlp_back(run, l, size, d_in, upper, mlp[l][r][3], w_up, w_down, f"mlp_back_{l}_{r}")
        two[l][r] = (back[l][r][3],)
        if l:
            back[l][r][0] = d_in
            back[l][r][1] = d_out[cuts[r]]

    def attend_back(l, r):
        d_mid[l][r], mid_low[l][r], d_qkv[l][r], own, small[l][r], carried[l][r] = attention_back(
            run, l, back[l][r][0], two[l][r], mlp[l][r][1], mlp[l][r][5], normed_one[l][r], norms, w_out, w_qkv,
            [blocks[l][q] for q in range(r + 1)], carried[l].get(r + 1, ()), l == 0,
            f"attention_back_{l}_{r}",
        )
        one[l][r] = (own,)

    def exchange(pair):
        own = run.gate(pair[0])
        return (own, swap_tensor(own))

    def arrive(pair):
        return (pair[0], run.gate(pair[1]))

    def every(table):
        return [table[r] for r in rows]

    def down_grads(l):
        lows = [b[1] for b in every(back[0])] if l == 0 else [d_out[c] for c in cuts]
        job = [([m[2] for m in every(mlp[l])], lows, 0)]
        halves = weight_grads(run, spot, job, f"down_grads_{l}")
        return Block(run, spot, n_dp, *halves, [width], (f"down_{l}",))

    def up_grads(l):
        job = [([m[1] for m in every(mlp[l])], [b[2] for b in every(back[l])], 1)]
        halves = weight_grads(run, spot, job, f"up_grads_{l}")
        return Block(run, spot, n_dp, *halves, [width], (f"up_{l}",))

    def attention_grads(l):
        job = [(every(normed_one[l]), [d[c] for d in every(d_qkv[l])], 0) for c in range(3)]
        job.append((every(attended[l]), every(mid_low[l]), 1))
        sums_small = every(small[0]) + every(small[1]) if l == 0 else ()
        halves = weight_grads(run, spot, job, f"attention_grads_{l}", sums_small)
        return Block(run, spot, n_dp, *halves, [2 * width], (f"att_{l}",))

    half = width // 2
    quarter = width // 4
    shapes = ((2, hid, width), (2, width, hid), (2, 3, width, part), (2, part, width))
    totals = [None] * 4

    def at(start, size, step=16):
        return pl.ds(pl.multiple_of(start, step), size)

    def rows_of(n, extra=0):
        return slice(n * (quarter + extra), n * (quarter + extra) + quarter)

    def place_down(chain, l):
        jobs = [
            (0, lambda s, n=n: (l, at(s * width + n * quarter, quarter)), rows_of(n), slice(0, width))
            for n in range(4)
        ]
        (totals[0],) = place_pieces(run, chain.pieces, slots, totals[:1], shapes[:1], jobs, f"place_down_{l}")

    def place_up(chain, l):
        jobs = [
            (0, lambda s, n=n: (l, pl.ds(n * quarter, quarter), at(s * width, width, 128)), rows_of(n), slice(0, width))
            for n in range(4)
        ]
        (totals[1],) = place_pieces(run, chain.pieces, slots, totals[1:2], shapes[1:2], jobs, f"place_up_{l}")

    def place_att(chain, l):
        extra = 0 if l else 16
        jobs = [
            (0, lambda s, n=n, c=c: (l, c, at(s * half + n * quarter, quarter)), rows_of(n, extra), slice(c * part, c * part + part))
            for n in range(2)
            for c in range(3)
        ]
        jobs += [
            (1, lambda s, n=n: (l, pl.ds(n * quarter, quarter), at(s * half, half, 128)), rows_of(n, extra), slice(3 * part, 3 * part + half))
            for n in range(2)
        ]
        totals[2:] = place_pieces(run, chain.pieces, slots, totals[2:], shapes[2:], jobs, f"place_att_{l}")

    for r in rows:
        attention(0, r)
    share_w_out(0)
    for r in rows:
        feed_forward(0, r)
    attention(1, 0)
    share_w_out(1)
    attention(1, 1)
    for r in rows:
        feed_forward(1, r)
    feed_back(1, 0)
    two[1][0] = exchange(two[1][0])
    feed_back(1, 1)
    two[1][1] = exchange(two[1][1])
    db1 = down_grads(1)
    db1.issue()
    ub1 = up_grads(1)
    ub1.issue()
    (d1,) = db1.split()
    d1.issue()
    (u1,) = ub1.split()
    u1.issue()
    attend_back(1, 1)
    one[1][1] = exchange(one[1][1])
    attend_back(1, 0)
    one[1][0] = exchange(one[1][0])
    d1.consume()
    d1.issue()
    feed_back(0, 1)
    two[0][1] = exchange(two[0][1])
    u1.consume()
    u1.issue()
    b1 = attention_grads(1)
    b1.issue()
    feed_back(0, 0)
    two[0][0] = exchange(two[0][0])
    db0 = down_grads(0)
    db0.issue()
    ub0 = up_grads(0)
    ub0.issue()
    d1.consume()
    d1.issue()
    attend_back(0, 1)
    one[0][1] = exchange(one[0][1])
    attend_back(0, 0)
    one[0][0] = exchange(one[0][0])
    u1.consume()
    u1.issue()
    b0 = attention_grads(0)
    b0.issue()
    (u0,) = ub0.split()
    u0.issue()
    (a1,) = b1.split()
    a1.issue()
    (d0,) = db0.split()
    d0.issue()
    (a0,) = b0.split()
    a0.issue()
    u0.consume()
    u0.issue()
    u1.consume()
    u1.issue()
    input_grad = finish_grad(
        run, every(d_mid[0]), every(one[0]), every(normed_one[0]), every(spreads[0]), norms
    )
    a0.consume()
    a0.issue()
    u0.consume()
    u0.issue()
    d1.consume()
    d1.issue()
    u1.consume()
    u1.issue()
    a1.consume()
    a1.issue()
    a0.consume()
    a0.issue()
    u0.consume()
    u0.issue()
    d0.consume()
    d0.issue()
    d1.consume()
    d1.issue()
    a1.consume()
    a1.issue()
    a0.consume()
    a0.issue()
    u0.consume()
    u0.issue()
    u1.consume()
    u1.issue()
    a1.consume()
    a1.issue()
    d0.consume()
    d0.issue()
    d1.consume()
    d1.issue()
    a0.consume()
    a0.issue()
    a1.consume()
    a1.issue()
    d0.consume()
    d0.issue()
    u0.consume()
    u0.issue()
    for r in rows:
        sums[1][r] = exchange(sums[1][r])
    first, second = finish_outputs(run, every(lows[1]), [m[0] for m in every(mlp[1])], every(sums[1]))
    a0.consume()
    a0.issue()
    d0.consume()
    d0.issue()
    a1.consume()
    a1.issue()
    tiny = cut_rows(run, a0.value, quarter, 16, "small_rows")
    tiny = (tiny, swap_tensor(tiny))
    u1.consume()
    place_up(u1, 1)
    u0.consume()
    place_up(u0, 0)
    d1.consume()
    place_down(d1, 1)
    a1.consume()
    place_att(a1, 1)
    g_gain, g_shift = finish_small(run, *tiny, width)
    d0.consume()
    d0.issue()
    a0.consume()
    place_att(a0, 0)
    d0.consume()
    place_down(d0, 0)
    return (
        first,
        second,
        input_grad,
        jnp.transpose(totals[2], (0, 2, 1, 3)),
        totals[3],
        totals[1],
        totals[0],
        g_gain,
        g_shift,
    )


def solution(mesh):
    n_dp = mesh.shape["dp"]
    in_specs = (
        P("dp", None),
        P(None, None, None, "tensor"),
        P(None, "tensor", None),
        P(None, None, "tensor"),
        P(None, "tensor", None),
        P(),
        P(),
        P("dp", None),
    )
    out_specs = (
        P("dp", None),
        P("dp", None),
        P("dp", None),
        P(None, None, None, "tensor"),
        P(None, "tensor", None),
        P(None, None, "tensor"),
        P(None, "tensor", None),
        P(),
        P(),
    )

    def body(*args):
        return on_device(2, n_dp, *args)

    return jax.shard_map(body, mesh=mesh, in_specs=in_specs, out_specs=out_specs, check_vma=False)
```
